32 devices in a mesh: dp: 8 (over z, y), task: 4 (over x, core).
Axes of the slice: x: 2, y: 2, z: 4, core: 2. Of those that a mesh axis runs over, the one named last changes fastest.
Arguments:
- images: bfloat16 [32768, 2, 2, 512], P(('dp', 'task')), may hold values from -6 to 6
- image_counts: int32 [32], P(('dp', 'task')), may hold values from 341 to 1024, as said below
- labels: int32 [32768, 40], P(('dp', 'task')), may hold values from 0 to 1
- fw_picks: int32 [20], replicated, may hold values from 0 to 39
- task_average: float32 [40], replicated, may hold values from 0 to 1, as said below
- conv_weights: float32 [2, 4608, 512], P(None, ('dp', 'task')), may hold values from -0.09375 to 0.09375
- conv_momentum: float32 [2, 4608, 512], P(None, ('dp', 'task')), may hold values from -0.00015258789 to 0.00015258789
- conv_average: float32 [2, 4608, 512], P(None, ('dp', 'task')), may hold values from -0.09375 to 0.09375
- norm_parameter_list: float32 [4, 512], replicated, may hold values from -1.2 to 1.3
- norm_momentum: float32 [4, 512], replicated, may hold values from -0.00015258789 to 0.00015258789
- norm_average: float32 [4, 512], replicated, may hold values from -4 to 4
- head_params: float32 [513, 40], P(None, 'task'), may hold values from -6 to 6
- head_momentum: float32 [513, 40], P(None, 'task'), may hold values from -0.0008544922 to 0.0008544922
- head_average: float32 [513, 40], P(None, 'task'), may hold values from -4 to 4
Outputs:
- block_output: bfloat16 [32768, 2, 2, 512], P(('dp', 'task'))
- image_grad: float32 [32768, 2, 2, 512], P(('dp', 'task'))
- conv_grads: float32 [2, 4608, 512], P(None, ('dp', 'task'))
- conv_momentum_new: float32 [2, 4608, 512], P(None, ('dp', 'task'))
- conv_weights_new: float32 [2, 4608, 512], P(None, ('dp', 'task'))
- conv_average_new: float32 [2, 4608, 512], P(None, ('dp', 'task'))
- conv_weights_low: bfloat16 [2, 4608, 512], P(None, ('dp', 'task'))
- norm_grads: float32 [4, 512], replicated
- norm_momentum_new: float32 [4, 512], replicated
- norm_params_new: float32 [4, 512], replicated
- norm_average_new: float32 [4, 512], replicated
- head_grads: float32 [513, 40], P(None, 'task')
- head_momentum_new: float32 [513, 40], P(None, 'task')
- head_params_new: float32 [513, 40], P(None, 'task')
- head_average_new: float32 [513, 40], P(None, 'task')
- task_average_new: float32 [40], replicated
The draws below stay inside these ranges and needn't reach their ends.
Inputs may be any that keep to these rules, and one draw needn't show every extreme that they name: Slot i of the d-th block of 1024 slots holds a real image when i < image_counts[d]; padded slots enter no statistic or loss. The last block is full. `task_average`: positive entries summing to one.
All inputs are finite; a program needn't handle non-finite values.
Results may differ from the reference program's by a relative error of at most 0.0035.
The reference program's roundings to bfloat16 on the way count: a program that leaves them out, or rounds other values in their place, can miss the bound.
Values may be sent and summed in bfloat16 or wider, within the bound.
No kernel may reach another device: no remote copies, remote signals or barrier semaphores. Data moves between devices by JAX's collectives and lax.ppermute only.
A program may use at most 192 MiB of HBM per device.

```python
import jax
import jax.numpy as jnp
from jax import lax

C = 512
TASKS = 40
MAP = 2
FW_STEPS = 20
IMG_DEV = 1024
IMAGES = 32768
DEVICES = 32


def draw_image_counts(key, part):
    device_ids = jnp.arange(DEVICES, dtype=jnp.int32)
    low_count = IMG_DEV // 3
    base_count = low_count + (IMG_DEV - low_count) * device_ids // (DEVICES - 1)
    jitter = jax.random.randint(key, (DEVICES,), 0, max(IMG_DEV // 4, 2), dtype=jnp.int32)
    return jnp.minimum(base_count + jitter, IMG_DEV).astype(jnp.int32)


def draw_labels(key, part):
    first_key, second_key = jax.random.split(jax.random.fold_in(key, 11))
    thresholds = jax.random.randint(first_key, (DEVICES, TASKS), 5, 96, dtype=jnp.int32)
    rolls = jax.random.randint(second_key, (IMAGES, TASKS), 0, 100, dtype=jnp.int32)
    block_limit = jnp.repeat(thresholds, IMG_DEV, axis=0)
    return (rolls < block_limit).astype(jnp.int32)


def draw_task_average(key, part):
    raw_values = jnp.exp(jax.random.uniform(key, (TASKS,), jnp.float32, -1.0, 1.0))
    return raw_values / jnp.sum(raw_values)


def draw_norm_parameter_list(key, part):
    gain_key, shift_key = jax.random.split(jax.random.fold_in(key, 23))
    gains = 1.0 + jax.random.uniform(gain_key, (4, C), jnp.float32, -0.3, 0.3)
    shifts = 0.3 * jnp.clip(jax.random.normal(shift_key, (4, C), jnp.float32), -4.0, 4.0)
    gain_rows = (jnp.arange(4) % 2 == 0)[:, None]
    return jnp.where(gain_rows, gains, shifts)


def draw_head_params(key, part):
    scale_key, weight_key, bias_key = jax.random.split(jax.random.fold_in(key, 37), 3)
    column_scale = jnp.exp(jax.random.uniform(scale_key, (TASKS,), jnp.float32, -0.69, 0.69))
    weight_matrix_rows = jnp.clip(jax.random.normal(weight_key, (C, TASKS), jnp.float32), -4.0, 4.0)
    bias_row = 1.5 * jnp.clip(jax.random.normal(bias_key, (1, TASKS), jnp.float32), -4.0, 4.0)
    weight_matrix_rows = weight_matrix_rows * column_scale[None, :] / C ** 0.5
    return jnp.concatenate([weight_matrix_rows, bias_row], axis=0)


def plant(array, stream_key, smallest, high):
    shape = array.shape
    index_at = [jax.random.randint(jax.random.fold_in(stream_key, axis), (), 0, shape[axis]) for axis in range(len(shape))]
    array = array.at[tuple(index_at)].set(smallest)
    longest = shape.index(max(shape))
    index_at[longest] = (index_at[longest] + 1) % shape[longest]
    return array.at[tuple(index_at)].set(high)


def level_of(own_key, shape, shards, least, top_value):
    level = 1.0
    for axis_at, parts in shards:
        draws = jax.random.uniform(jax.random.fold_in(jax.random.fold_in(own_key, 6), axis_at), (parts,), jnp.float32, least / len(shards), top_value / len(shards))
        level = level * jnp.repeat(jnp.exp(draws), shape[axis_at] // parts).reshape((-1,) + (1,) * (len(shape) - 1 - axis_at))
    return level


def centred(rng, dims, deviation, limit, shards=(), kind=jnp.bfloat16):
    drawn = deviation * jax.random.normal(rng, dims, jnp.float32)
    if shards:
        drawn = drawn * level_of(rng, dims, shards, -0.22, 0.18)
    return jnp.clip(drawn, -limit, limit).astype(kind)


def setup_inputs(seed: int = 0) -> dict:
    seeds = jax.random.split(jax.random.key(seed), 15)
    images = centred(seeds[0], (IMAGES, MAP, MAP, C), 1.0, 6.0, ((0, 32),))
    image_counts = draw_image_counts(jax.random.fold_in(seeds[14], 71), 0)
    labels = draw_labels(jax.random.fold_in(seeds[14], 71), 0)
    fw_picks = plant(jax.random.randint(seeds[3], (FW_STEPS,), 0, TASKS), jax.random.fold_in(seeds[3], 1), 0, TASKS - 1).astype(jnp.int32)
    task_average = draw_task_average(jax.random.fold_in(seeds[14], 71), 0)
    conv_weights = centred(seeds[5], (2, 9 * C, C), (9 * C) ** -0.5, 0.09375, ((1, 32),), jnp.float32)
    conv_momentum = centred(seeds[6], (2, 9 * C, C), (0.002 / (IMG_DEV * DEVICES) ** 0.5), 0.00015258789, ((1, 32),), jnp.float32)
    conv_average = centred(seeds[7], (2, 9 * C, C), (9 * C) ** -0.5, 0.09375, ((1, 32),), jnp.float32)
    norm_parameter_list = draw_norm_parameter_list(jax.random.fold_in(seeds[14], 71), 0)
    norm_momentum = centred(seeds[9], (4, C), (0.002 / (IMG_DEV * DEVICES) ** 0.5), 0.00015258789, (), jnp.float32)
    norm_average = centred(seeds[10], (4, C), 1.0, 4.0, (), jnp.float32)
    head_params = draw_head_params(jax.random.fold_in(seeds[14], 71), 0)
    head_momentum = centred(seeds[12], (C + 1, TASKS), (0.01 / (IMG_DEV * DEVICES) ** 0.5), 0.0008544922, ((1, 4),), jnp.float32)
    head_average = centred(seeds[13], (C + 1, TASKS), 1.0, 4.0, ((1, 4),), jnp.float32)
    return {"images": images, "image_counts": image_counts, "labels": labels, "fw_picks": fw_picks, "task_average": task_average, "conv_weights": conv_weights, "conv_momentum": conv_momentum, "conv_average": conv_average, "norm_parameter_list": norm_parameter_list, "norm_momentum": norm_momentum, "norm_average": norm_average, "head_params": head_params, "head_momentum": head_momentum, "head_average": head_average}


EPSILON = 1e-05
MOMENTUM_DECAY = 0.5
AVERAGE_DECAY = 0.5
CONV_RATE = 2000.0
NORM_RATE = 40000.0
HEAD_RATE = 1000.0
STEP_CAP = 0.5
PRECISE = lax.Precision.HIGHEST

@jax.custom_vjp
def low(v):
    return lax.optimization_barrier(v.astype(jnp.bfloat16)).astype(jnp.float32)

@jax.custom_vjp
def low_back(v):
    return v

def low_keep(v):
    return (low(v), None)

def low_pass(kept, grad):
    return (grad,)

def back_keep(v):
    return (v, None)

def back_low(kept, grad):
    return (low(grad),)
low.defvjp(low_keep, low_pass)
low_back.defvjp(back_keep, back_low)

def unfold(kernel, map_side):
    block_rows = []
    for in_row in range(map_side):
        for in_col in range(map_side):
            pieces = []
            for out_row in range(map_side):
                for out_col in range(map_side):
                    pieces.append(kernel[in_row - out_row + 1, in_col - out_col + 1])
            block_rows.append(jnp.concatenate(pieces, axis=1))
    return jnp.concatenate(block_rows, axis=0)

def batch_norm(values, real_rows, real_total, norm_gain, shift):
    weight_matrix_rows = real_rows[:, None, None]
    spatial_positions = real_total * values.shape[1]
    mean_value = lax.optimization_barrier(jnp.sum(values * weight_matrix_rows, axis=(0, 1))) / spatial_positions
    square_mean = lax.optimization_barrier(jnp.sum(values * values * weight_matrix_rows, axis=(0, 1))) / spatial_positions
    inverse_deviation = lax.rsqrt(square_mean - mean_value * mean_value + EPSILON)
    return norm_gain * (values - mean_value) * inverse_deviation + shift

def frank_wolfe(gram_matrix, start_mix, vertex_ids):
    task_ids = jnp.arange(gram_matrix.shape[0], dtype=jnp.int32)

    def frank_step(task_mix, vertex):
        corner = (task_ids == vertex).astype(gram_matrix.dtype)
        gram_mix = jnp.dot(gram_matrix, task_mix, precision=PRECISE)
        gram_corner = jnp.dot(gram_matrix, corner, precision=PRECISE)
        mix_mix = jnp.sum(task_mix * gram_mix)
        mix_corner = jnp.sum(corner * gram_mix)
        corner_corner = jnp.sum(corner * gram_corner)
        step_size = jnp.clip((mix_mix - mix_corner) / (mix_mix - 2.0 * mix_corner + corner_corner), 0.0, STEP_CAP)
        return ((1.0 - step_size) * task_mix + step_size * corner, None)
    final_mix, unused = lax.scan(frank_step, start_mix, vertex_ids)
    return final_mix

def nesterov(params, momentum, grads, rate, average):
    momentum_new = MOMENTUM_DECAY * momentum + grads
    params_new = params - rate * (grads + MOMENTUM_DECAY * momentum_new)
    average_new = AVERAGE_DECAY * average + (1.0 - AVERAGE_DECAY) * params_new
    return (momentum_new, params_new, average_new)

def reference(images, image_counts, labels, fw_picks, task_average, conv_weights, conv_momentum, conv_average, norm_parameter_list, norm_momentum, norm_average, head_params, head_momentum, head_average):
    row_count = images.shape[0]
    map_side = images.shape[1]
    channels = images.shape[3]
    positions_per = map_side * map_side
    per_device = row_count // image_counts.shape[0]
    real_rows = (jnp.arange(per_device, dtype=jnp.int32)[None, :] < image_counts[:, None]).reshape(row_count).astype(jnp.float32)
    real_total = jnp.sum(image_counts).astype(jnp.float32)
    label_float = labels.astype(jnp.float32)

    def forward(image_float, weight_float, norm_float, head_float):
        rounded = low(weight_float).reshape(2, 3, 3, channels, channels)
        unfold_one = unfold(rounded[0], map_side)
        unfold_two = unfold(rounded[1], map_side)
        flat_images = image_float.reshape(row_count, positions_per * channels)
        first_moment = low_back(jnp.dot(flat_images, unfold_one, precision=PRECISE)).reshape(row_count, positions_per, channels)
        first_normalized = batch_norm(first_moment, real_rows, real_total, norm_float[0], norm_float[1])
        hidden = low(jax.nn.gelu(first_normalized)).reshape(row_count, positions_per * channels)
        second_moment = low_back(jnp.dot(hidden, unfold_two, precision=PRECISE)).reshape(row_count, positions_per, channels)
        second_normalized = batch_norm(second_moment, real_rows, real_total, norm_float[2], norm_float[3])
        block_out = jax.nn.gelu(second_normalized + image_float.reshape(row_count, positions_per, channels))
        pooled = lax.optimization_barrier(jnp.mean(block_out, axis=1))
        logits = jnp.dot(pooled, head_float[:channels], precision=PRECISE) + head_float[channels]
        return (logits, block_out)
    (logits, block_out), backward = jax.vjp(forward, images.astype(jnp.float32), conv_weights, norm_parameter_list, head_params)

    def task_losses(logit_values):
        return lax.optimization_barrier(jnp.sum(real_rows[:, None] * (jax.nn.softplus(logit_values) - label_float * logit_values), axis=0)) / real_total
    unused, loss_back = jax.vjp(task_losses, logits)
    resid = loss_back(jnp.ones((logits.shape[1],), jnp.float32))[0]
    head_rows = head_params[:channels]
    gram_matrix = jnp.dot(resid.T, resid, precision=PRECISE) * jnp.dot(head_rows.T, head_rows, precision=PRECISE)
    task_mix = frank_wolfe(gram_matrix, task_average, fw_picks)
    task_average_new = AVERAGE_DECAY * task_average + (1.0 - AVERAGE_DECAY) * task_mix
    image_grad, conv_grads, norm_grads, head_grads = backward((resid * task_mix[None, :], jnp.zeros_like(block_out)))
    conv_momentum_new, conv_weights_new, conv_average_new = nesterov(conv_weights, conv_momentum, conv_grads, CONV_RATE, conv_average)
    norm_momentum_new, norm_params_new, norm_average_new = nesterov(norm_parameter_list, norm_momentum, norm_grads, NORM_RATE, norm_average)
    head_momentum_new, head_params_new, head_average_new = nesterov(head_params, head_momentum, head_grads, HEAD_RATE, head_average)
    block_output = block_out.astype(jnp.bfloat16).reshape(images.shape)
    return (block_output, image_grad, conv_grads, conv_momentum_new, conv_weights_new, conv_average_new, conv_weights_new.astype(jnp.bfloat16), norm_grads, norm_momentum_new, norm_params_new, norm_average_new, head_grads, head_momentum_new, head_params_new, head_average_new, task_average_new)
```

```python
import jax
import jax.numpy as jnp
from jax import lax
from jax.experimental import pallas as pl
from jax.experimental.pallas import tpu as pltpu
from jax.sharding import PartitionSpec as P

EPSILON = 1e-05
MOMENTUM_DECAY = 0.5
AVERAGE_DECAY = 0.5
CONV_RATE = 2000.0
NORM_RATE = 40000.0
HEAD_RATE = 1000.0
STEP_CAP = 0.5
GELU_A = 0.7978845608
GELU_B = 0.7978845608 * 0.044715
AXES = ("dp", "task")
PRECISE = lax.Precision.HIGHEST
F32 = jnp.float32
BF16 = jnp.bfloat16
TILE = 256
LANES = 128
PARAMS = pltpu.CompilerParams(vmem_limit_bytes=58 << 20)


def tap(q, p):
    return (q // 2 - p // 2 + 1) * 3 + (q % 2 - p % 2 + 1)


def dot(a, b):
    return jnp.dot(a, b, preferred_element_type=F32)


def dot_nt(a, b):
    return lax.dot_general(a, b, (((1,), (1,)), ((), ())), preferred_element_type=F32)


def dot_tn(a, b):
    return lax.dot_general(a, b, (((0,), (0,)), ((), ())), preferred_element_type=F32)


def precise(a, b, dims):
    return lax.dot_general(a, b, ((dims[0], dims[1]), ((), ())), precision=PRECISE, preferred_element_type=F32)


def fold8(v):
    return jnp.sum(v.reshape(v.shape[0] // 8, 8, v.shape[1]), 0)


def spread_rows(out_ref, rows):
    line = 0
    for row in rows:
        for j in range(row.shape[1] // LANES):
            part = row[:, j * LANES : (j + 1) * LANES]
            out_ref[:, line : line + 1, :] = jnp.broadcast_to(part[None], (out_ref.shape[0], 1, LANES))
            line += 1


def gathered_rows(ref, count):
    total = jnp.sum(ref[...], 0)
    return [
        jnp.concatenate([total[4 * r + j : 4 * r + j + 1, :] for j in range(4)], axis=1)
        for r in range(count)
    ], total


def moments(gathered_ref, spatial):
    (value_sum, square_sum), _ = gathered_rows(gathered_ref, 2)
    mean = value_sum / spatial
    inverse = lax.rsqrt(square_sum / spatial - mean * mean + EPSILON)
    return mean, inverse


def real_mask(count, rows):
    index = lax.broadcasted_iota(jnp.int32, (rows, 1), 0) + pl.program_id(0) * rows
    return (index < count).astype(F32)


def conv_rows(x_ref, k_ref, p):
    pr, pc = p // 2, p % 2
    acc = None
    for qr in range(2):
        base = ((qr - pr + 1) * 3 + (1 - pc)) * 512
        t = dot(x_ref[:, qr * 1024 : (qr + 1) * 1024], k_ref[base : base + 1024, :])
        acc = t if acc is None else acc + t
    return acc


def conv_stats(x_ref, k_ref, out_ref, mask):
    total = square = None
    for p in range(4):
        acc = conv_rows(x_ref, k_ref, p)
        out_ref[:, p * 512 : (p + 1) * 512] = acc
        masked = acc * mask
        s, q = fold8(masked), fold8(masked * acc)
        total = s if total is None else total + s
        square = q if square is None else square + q
    return total, square


def accumulate(step, steps, acc_ref, values, finish):
    @pl.when(step == 0)
    def _():
        for i, v in enumerate(values):
            acc_ref[i] = v

    @pl.when(step > 0)
    def _():
        for i, v in enumerate(values):
            acc_ref[i] += v

    @pl.when(step == steps - 1)
    def _():
        finish([jnp.sum(acc_ref[i], 0, keepdims=True) for i in range(len(values))])


def first_kernel(steps, count_ref, x_ref, k_ref, first_ref, stat_ref, acc_ref):
    step = pl.program_id(0)
    count = count_ref[0]
    values = conv_stats(x_ref, k_ref, first_ref, real_mask(count, TILE))

    def finish(rows):
        spread_rows(stat_ref, rows)
        stat_ref[:, 8:16, :] = jnp.full((stat_ref.shape[0], 8, LANES), count.astype(F32), F32)

    accumulate(step, steps, acc_ref, values, finish)


def gelu_tanh(v):
    return jnp.tanh(v * (GELU_A + GELU_B * (v * v)))


def gelu_slope(v, t):
    return (0.5 + 0.5 * t) + (0.5 * v) * (1.0 - t * t) * (GELU_A + (3.0 * GELU_B) * (v * v))


def second_kernel(steps, count_ref, first_ref, g1_ref, norm_ref, k_ref, hidden_ref, second_ref, stat_ref, acc_ref):
    step = pl.program_id(0)
    spatial = jnp.sum(g1_ref[:, 8:9, :], 0) * 4.0
    mean, inverse = moments(g1_ref, spatial[0:1, 0:1])
    scale = norm_ref[0:1, :] * inverse
    shift = norm_ref[1:2, :] - mean * scale
    for p in range(4):
        v = first_ref[:, p * 512 : (p + 1) * 512] * scale + shift
        half = 0.5 * v
        hidden_ref[:, p * 512 : (p + 1) * 512] = (half + half * gelu_tanh(v)).astype(BF16)
    values = conv_stats(hidden_ref, k_ref, second_ref, real_mask(count_ref[0], TILE))
    accumulate(step, steps, acc_ref, values, lambda rows: spread_rows(stat_ref, rows))


def head_kernel(
    steps, tasks, count_ref, second_ref, g2_ref, g1_ref, norm_ref, image_ref, label_ref, head_ref, pick_ref,
    out_ref, slope_ref, slope_sum_ref, slope_xhat_ref, pooled_ref, resid_ref, gram_out_ref, gram_ref,
):
    step = pl.program_id(0)
    real_total = jnp.sum(g1_ref[:, 8:9, :], 0)[0:1, 0:1]
    mean, inverse = moments(g2_ref, real_total * 4.0)
    gain, shift = norm_ref[2:3, :], norm_ref[3:4, :]
    pooled = slope_sum = slope_xhat = None
    for p in range(4):
        cols = slice(p * 512, (p + 1) * 512)
        xhat = (second_ref[:, cols] - mean) * inverse
        pre = gain * xhat + shift + image_ref[:, cols].astype(F32)
        t = gelu_tanh(pre)
        half = 0.5 * pre
        out = half + half * t
        out_ref[:, cols] = out.astype(BF16)
        slope = gelu_slope(pre, t)
        slope_ref[:, cols] = slope
        pooled = out if pooled is None else pooled + out
        slope_sum = slope if slope_sum is None else slope_sum + slope
        slope_xhat = slope * xhat if slope_xhat is None else slope_xhat + slope * xhat
    pooled = pooled * 0.25
    slope_sum_ref[...] = slope_sum
    slope_xhat_ref[...] = slope_xhat
    pooled_ref[:, 0:512] = pooled
    pooled_ref[:, 512:640] = (lax.broadcasted_iota(jnp.int32, (TILE, LANES), 1) == 0).astype(F32)
    logits = precise(pooled, head_ref[0:512, :], ((1,), (0,))) + head_ref[512:513, :]
    lane_real = (lax.broadcasted_iota(jnp.int32, (1, LANES), 1) < tasks).astype(F32)
    resid = (real_mask(count_ref[0], TILE) * lane_real) * (jax.nn.sigmoid(logits) - label_ref[...].astype(F32)) / real_total
    resid_ref[...] = resid
    part = precise(resid, resid, ((0,), (0,)))

    @pl.when(step == 0)
    def _():
        gram_ref[...] = part

    @pl.when(step > 0)
    def _():
        gram_ref[...] += part

    @pl.when(step == steps - 1)
    def _():
        heads = head_ref[0:512, :]
        gram = gram_ref[...] * precise(heads, heads, ((0,), (0,)))
        basis = pick_ref[...]
        projected = precise(gram, basis, ((1,), (1,)))
        lane = lax.broadcasted_iota(jnp.int32, (32, LANES), 1)
        row = lax.broadcasted_iota(jnp.int32, (32, LANES), 0)
        packed = None
        for group in range(3):
            placed = precise(projected, (lane == row + 32 * group).astype(F32), ((1,), (0,)))
            rows = precise(basis[8 * group : 8 * group + 8, :], placed, ((1,), (0,)))
            packed = rows if packed is None else packed + rows
        gram_out_ref[...] = jnp.broadcast_to(packed[None], gram_out_ref.shape)


def frank_wolfe(packed, picks, start_mix, fw_steps):
    rows = jnp.concatenate([packed[:, 32 * g : 32 * g + 32] for g in range(3)], axis=0)
    column = [jnp.broadcast_to(rows[:, k : k + 1], (24, LANES)) for k in range(fw_steps + 1)]
    along = column[fw_steps]
    a = along[fw_steps : fw_steps + 1, :]
    mix = start_mix
    for k in range(fw_steps):
        b = along[k : k + 1, :]
        c = column[k][k : k + 1, :]
        size = jnp.clip((a - b) / (a - 2.0 * b + c), 0.0, STEP_CAP)
        keep = 1.0 - size
        a = keep * keep * a + 2.0 * (keep * size) * b + size * size * c
        along = keep * along + size * column[k]
        mix = keep * mix + size * picks[k : k + 1, :]
    return mix


def mix_kernel(
    steps, fw_steps, gram_ref, pick_ref, start_ref, resid_ref, pooled_ref, head_ref, slope_sum_ref, slope_xhat_ref,
    dout_ref, stat_ref, head_grad_ref, mix_ref, acc_ref,
):
    step = pl.program_id(0)

    @pl.when(step == 0)
    def _():
        packed = jnp.sum(gram_ref[...], 0)
        start = start_ref[0:1, :]
        mix = frank_wolfe(packed, pick_ref[...], start, fw_steps)
        mix_ref[...] = jnp.broadcast_to(mix, mix_ref.shape)

    weighted = resid_ref[...] * mix_ref[0:1, :]
    dout = precise(weighted, head_ref[0:512, :], ((1,), (1,))) * 0.25
    dout_ref[...] = dout
    part = precise(weighted, pooled_ref[...], ((0,), (0,)))

    @pl.when(step == 0)
    def _():
        head_grad_ref[...] = part

    @pl.when(step > 0)
    def _():
        head_grad_ref[...] += part

    values = (fold8(dout * slope_xhat_ref[...]), fold8(dout * slope_sum_ref[...]))
    accumulate(step, steps, acc_ref, values, lambda rows: spread_rows(stat_ref, rows))


def back_second_kernel(
    steps, count_ref, slope_ref, dout_ref, second_ref, first_ref, g1_ref, g2_ref, g4_ref, norm_ref, k_ref,
    dsecond_ref, dnormed_ref, stat_ref, acc_ref,
):
    step = pl.program_id(0)
    spatial = jnp.sum(g1_ref[:, 8:9, :], 0)[0:1, 0:1] * 4.0
    mean1, inverse1 = moments(g1_ref, spatial)
    mean2, inverse2 = moments(g2_ref, spatial)
    (gain_grad, shift_grad), _ = gathered_rows(g4_ref, 2)
    scale2 = norm_ref[2:3, :] * inverse2
    by_value = scale2 * gain_grad * inverse2 / spatial
    by_one = scale2 * shift_grad / spatial - by_value * mean2
    mask = real_mask(count_ref[0], TILE)
    dout = dout_ref[...] * scale2
    real_value, real_one = mask * by_value, mask * by_one
    for p in range(4):
        cols = slice(p * 512, (p + 1) * 512)
        grad = dout * slope_ref[:, cols] - (real_one + real_value * second_ref[:, cols])
        dsecond_ref[:, cols] = grad.astype(BF16)
    gain1, shift1 = norm_ref[0:1, :], norm_ref[1:2, :]
    gain_sum = shift_sum = None
    for q in range(4):
        cols = slice(q * 512, (q + 1) * 512)
        acc = None
        for p in range(4):
            base = tap(q, p) * 512
            t = dot_nt(dsecond_ref[:, p * 512 : (p + 1) * 512], k_ref[base : base + 512, :])
            acc = t if acc is None else acc + t
        xhat = (first_ref[:, cols] - mean1) * inverse1
        v = gain1 * xhat + shift1
        dnormed = acc * gelu_slope(v, gelu_tanh(v))
        dnormed_ref[:, cols] = dnormed
        g, s = fold8(dnormed * xhat), fold8(dnormed)
        gain_sum = g if gain_sum is None else gain_sum + g
        shift_sum = s if shift_sum is None else shift_sum + s
    accumulate(step, steps, acc_ref, (gain_sum, shift_sum), lambda rows: spread_rows(stat_ref, rows))


def add_taps(out_ref, x_ref, value, p, seen):
    for q in range(4):
        index = tap(q, p)
        part = dot_tn(x_ref[:, q * 512 : (q + 1) * 512], value)
        rows = slice(index * 512, (index + 1) * 512)
        if index in seen:
            out_ref[rows, :] += part
        else:
            out_ref[rows, :] = part
        seen.add(index)


def weight_grad_kernel(x_ref, d0_ref, d1_ref, d2_ref, d3_ref, out_ref):
    seen = set()
    for p, ref in enumerate((d0_ref, d1_ref, d2_ref, d3_ref)):
        add_taps(out_ref, x_ref, ref[...], p, seen)


def dfirst_kernel(count_ref, dnormed_ref, first_ref, g1_ref, g5_ref, norm_ref, dfirst_ref):
    spatial = jnp.sum(g1_ref[:, 8:9, :], 0)[0:1, 0:1] * 4.0
    mean1, inverse1 = moments(g1_ref, spatial)
    (gain_grad, shift_grad), _ = gathered_rows(g5_ref, 2)
    scale = norm_ref[0:1, :] * inverse1
    by_value = scale * gain_grad * inverse1 / spatial
    by_one = scale * shift_grad / spatial - by_value * mean1
    mask = real_mask(count_ref[0], TILE)
    real_value, real_one = mask * by_value, mask * by_one
    for p in range(4):
        cols = slice(p * 512, (p + 1) * 512)
        grad = scale * dnormed_ref[:, cols] - (real_one + real_value * first_ref[:, cols])
        dfirst_ref[:, cols] = grad.astype(BF16)


def image_grad_kernel(dfirst_ref, k_ref, slope_ref, dout_ref, out_ref):
    dout = dout_ref[...]
    for q in range(4):
        cols = slice(q * 512, (q + 1) * 512)
        acc = dout * slope_ref[:, cols]
        for p in range(4):
            base = tap(q, p) * 512
            acc = acc + dot_nt(dfirst_ref[:, p * 512 : (p + 1) * 512], k_ref[base : base + 512, :])
        out_ref[:, cols] = acc


def nesterov(params, momentum, grads, rate, average):
    momentum_new = MOMENTUM_DECAY * momentum + grads
    params_new = params - rate * (grads + MOMENTUM_DECAY * momentum_new)
    average_new = AVERAGE_DECAY * average + (1.0 - AVERAGE_DECAY) * params_new
    return (momentum_new, params_new, average_new)


def shape(dims, dtype=F32):
    return jax.ShapeDtypeStruct(dims, dtype)


def whole(dims):
    return pl.BlockSpec(dims, lambda *_: (0,) * len(dims))


def tiles(width):
    return pl.BlockSpec((TILE, width), lambda i, *_: (i, 0))


def exchange(replicated):
    return lax.all_to_all(replicated, AXES, 0, 0)


def on_device(
    images, image_counts, labels, fw_picks, task_average, conv_weights, conv_momentum, conv_average,
    norm_parameter_list, norm_momentum, norm_average, head_params, head_momentum, head_average,
):
    rows, map_side, channels = images.shape[0], images.shape[1], images.shape[3]
    width = map_side * map_side * channels
    devices = lax.axis_size(AXES)
    tasks = labels.shape[1]
    fw_steps = fw_picks.shape[0]
    steps = rows // TILE
    grid = (steps,)
    stat = (devices, 8, LANES)

    def call(body, grid_, ins, outs, scratch, count=None):
        arrays = [a for a, _ in ins]
        specs = [s for _, s in ins]
        out_specs = [s for _, s in outs]
        out_shape = [a for a, _ in outs]
        spec = pltpu.PrefetchScalarGridSpec(
            num_scalar_prefetch=0 if count is None else 1, grid=grid_, in_specs=specs, out_specs=out_specs, scratch_shapes=scratch
        )
        args = arrays if count is None else [count] + arrays
        return pl.pallas_call(body, grid_spec=spec, out_shape=out_shape, compiler_params=PARAMS)(*args)

    low = conv_weights.astype(BF16)
    k1 = lax.all_gather(low[0], AXES, axis=0, tiled=True)
    k2 = lax.all_gather(low[1], AXES, axis=0, tiled=True)
    heads = lax.all_gather(head_params, "task", axis=1, tiled=True)
    heads = jnp.pad(heads, ((0, 7), (0, LANES - tasks)))
    labels = jnp.pad(labels, ((0, 0), (0, LANES - tasks)))
    flat_images = images.reshape(rows, width)
    start = jnp.pad(task_average[None, :], ((0, 7), (0, LANES - tasks)))
    basis = jnp.concatenate(
        [
            (jnp.arange(LANES, dtype=jnp.int32)[None, :] == fw_picks[:, None]).astype(F32),
            start[0:1],
            jnp.zeros((32 - fw_steps - 1, LANES), F32),
        ],
        axis=0,
    )
    norm_spec, head_spec = whole((4, channels)), whole(heads.shape)
    g1_spec, stat_spec = whole((devices, 16, LANES)), whole(stat)
    k_spec = whole((9 * channels, channels))
    acc = pltpu.VMEM((2, 8, channels), F32)

    def bind(body, *static):
        return lambda *refs: body(*static, *refs)

    first, stat1 = call(
        bind(first_kernel, steps), grid, [(flat_images, tiles(width)), (k1, k_spec)],
        [(shape((rows, width)), tiles(width)), (shape((devices, 16, LANES)), g1_spec)], [acc], image_counts,
    )
    g1 = exchange(stat1)
    hidden, second, stat2 = call(
        bind(second_kernel, steps), grid,
        [(first, tiles(width)), (g1, g1_spec), (norm_parameter_list, norm_spec), (k2, k_spec)],
        [(shape((rows, width), BF16), tiles(width)), (shape((rows, width)), tiles(width)), (shape(stat), stat_spec)], [acc], image_counts,
    )
    g2 = exchange(stat2)
    block_flat, slope, slope_sum, slope_xhat, pooled, resid, gram = call(
        bind(head_kernel, steps, tasks), grid,
        [(second, tiles(width)), (g2, stat_spec), (g1, g1_spec), (norm_parameter_list, norm_spec), (flat_images, tiles(width)),
         (labels, tiles(LANES)), (heads, head_spec), (basis, whole(basis.shape))],
        [(shape((rows, width), BF16), tiles(width)), (shape((rows, width)), tiles(width)), (shape((rows, channels)), tiles(channels)),
         (shape((rows, channels)), tiles(channels)), (shape((rows, channels + LANES)), tiles(channels + LANES)),
         (shape((rows, LANES)), tiles(LANES)), (shape(stat), stat_spec)],
        [pltpu.VMEM((LANES, LANES), F32)], image_counts,
    )
    g3 = exchange(gram)
    dout, stat4, head_partial, mix = call(
        bind(mix_kernel, steps, fw_steps), grid,
        [(g3, stat_spec), (basis, whole(basis.shape)), (start, whole(start.shape)), (resid, tiles(LANES)),
         (pooled, tiles(channels + LANES)), (heads, head_spec), (slope_sum, tiles(channels)), (slope_xhat, tiles(channels))],
        [(shape((rows, channels)), tiles(channels)), (shape(stat), stat_spec),
         (shape((LANES, channels + LANES)), whole((LANES, channels + LANES))), (shape((8, LANES)), whole((8, LANES)))],
        [acc],
    )
    g4 = exchange(stat4)
    dsecond, dnormed, stat5 = call(
        bind(back_second_kernel, steps), grid,
        [(slope, tiles(width)), (dout, tiles(channels)), (second, tiles(width)), (first, tiles(width)), (g1, g1_spec),
         (g2, stat_spec), (g4, stat_spec), (norm_parameter_list, norm_spec), (k2, k_spec)],
        [(shape((rows, width), BF16), tiles(width)), (shape((rows, width)), tiles(width)), (shape(stat), stat_spec)], [acc], image_counts,
    )
    g5 = exchange(stat5)
    halves = 2
    part = channels // halves

    def weight_grad(x, d):
        return call(
            weight_grad_kernel, (halves,),
            [(x, whole((rows, width)))] + [(d, pl.BlockSpec((rows, part), lambda i, p=p: (0, p * halves + i))) for p in range(4)],
            [(shape((9 * channels, channels)), pl.BlockSpec((9 * channels, part), lambda i: (0, i)))], [],
        )[0]

    grad_two = lax.psum_scatter(weight_grad(hidden, dsecond), AXES, scatter_dimension=0, tiled=True)
    (dfirst,) = call(
        dfirst_kernel, grid,
        [(dnormed, tiles(width)), (first, tiles(width)), (g1, g1_spec), (g5, stat_spec), (norm_parameter_list, norm_spec)],
        [(shape((rows, width), BF16), tiles(width))], [], image_counts,
    )
    grad_one = lax.psum_scatter(weight_grad(flat_images, dfirst), AXES, scatter_dimension=0, tiled=True)
    (image_flat,) = call(
        image_grad_kernel, grid,
        [(dfirst, tiles(width)), (k1, k_spec), (slope, tiles(width)), (dout, tiles(channels))],
        [(shape((rows, width)), tiles(width))], [],
    )
    task_cols = head_params.shape[1]
    ways = tasks // task_cols
    send = head_partial[:tasks].reshape(1, ways, task_cols, -1)
    send = jnp.broadcast_to(send, (devices // ways,) + send.shape[1:]).reshape(devices, task_cols, -1)
    head_grads = jnp.sum(exchange(send), 0)[:, : channels + 1].T
    task_average_new = AVERAGE_DECAY * task_average + (1.0 - AVERAGE_DECAY) * mix[0, :tasks]
    sums4 = jnp.sum(g4, 0).reshape(2, channels)
    sums5 = jnp.sum(g5, 0).reshape(2, channels)
    norm_grads = jnp.concatenate([sums5, sums4], axis=0)
    conv_grads = jnp.stack([grad_one, grad_two])
    conv_momentum_new, conv_weights_new, conv_average_new = nesterov(conv_weights, conv_momentum, conv_grads, CONV_RATE, conv_average)
    norm_momentum_new, norm_params_new, norm_average_new = nesterov(
        norm_parameter_list, norm_momentum, norm_grads, NORM_RATE, norm_average
    )
    head_momentum_new, head_params_new, head_average_new = nesterov(head_params, head_momentum, head_grads, HEAD_RATE, head_average)
    return (
        block_flat.reshape(images.shape),
        image_flat.reshape(images.shape),
        conv_grads,
        conv_momentum_new,
        conv_weights_new,
        conv_average_new,
        conv_weights_new.astype(BF16),
        norm_grads,
        norm_momentum_new,
        norm_params_new,
        norm_average_new,
        head_grads,
        head_momentum_new,
        head_params_new,
        head_average_new,
        task_average_new,
    )


def solution(mesh):
    both = P(AXES)
    rowwise = P(None, AXES, None)
    head = P(None, "task")
    return jax.shard_map(
        on_device,
        mesh=mesh,
        in_specs=(both, both, both, P(), P(), rowwise, rowwise, rowwise, P(), P(), P(), head, head, head),
        out_specs=(both, both, rowwise, rowwise, rowwise, rowwise, rowwise, P(), P(), P(), P(), head, head, head, head, P()),
        check_vma=False,
    )
```

```python
import jax
import jax.numpy as jnp
from jax import lax
from jax.experimental import pallas as pl
from jax.experimental.pallas import tpu as pltpu
from jax.sharding import PartitionSpec as P

EPSILON = 1e-05
MOMENTUM_DECAY = 0.5
AVERAGE_DECAY = 0.5
CONV_RATE = 2000.0
NORM_RATE = 40000.0
HEAD_RATE = 1000.0
STEP_CAP = 0.5
GELU_A = 0.7978845608
GELU_B = 0.7978845608 * 0.044715
AXES = ("dp", "task")
PRECISE = lax.Precision.HIGHEST
F32 = jnp.float32
BF16 = jnp.bfloat16
TILE = 256
CONV_TILE = 512
LANES = 128


def tap(q, p):
    return (q // 2 - p // 2 + 1) * 3 + (q % 2 - p % 2 + 1)


def dot(a, b):
    return jnp.dot(a, b, preferred_element_type=F32)


def dot_nt(a, b):
    return lax.dot_general(a, b, (((1,), (1,)), ((), ())), preferred_element_type=F32)


def dot_tn(a, b):
    return lax.dot_general(a, b, (((0,), (0,)), ((), ())), preferred_element_type=F32)


def precise(a, b, dims):
    return lax.dot_general(a, b, ((dims[0], dims[1]), ((), ())), precision=PRECISE, preferred_element_type=F32)


def fold8(v):
    return jnp.sum(v.reshape(v.shape[0] // 8, 8, v.shape[1]), 0)


def spread_rows(out_ref, rows):
    line = 0
    for row in rows:
        for j in range(row.shape[1] // LANES):
            part = row[:, j * LANES : (j + 1) * LANES]
            out_ref[:, line : line + 1, :] = jnp.broadcast_to(part[None], (out_ref.shape[0], 1, LANES))
            line += 1


def gathered_rows(ref, count):
    total = jnp.sum(ref[...], 0)
    return [
        jnp.concatenate([total[4 * r + j : 4 * r + j + 1, :] for j in range(4)], axis=1)
        for r in range(count)
    ]


def moments(gathered_ref, spatial):
    value_sum, square_sum = gathered_rows(gathered_ref, 2)
    mean = value_sum / spatial
    inverse = lax.rsqrt(square_sum / spatial - mean * mean + EPSILON)
    return mean, inverse


def images_total(g1_ref):
    return jnp.sum(g1_ref[:, 8:9, :], 0)[0:1, 0:1]


def real_mask(count, start, rows):
    index = lax.broadcasted_iota(jnp.int32, (rows, 1), 0) + start
    return (index < count).astype(F32)


def plus(total, value):
    return value if total is None else total + value


def column_sums(values):
    return [jnp.sum(v, 0, keepdims=True) for v in values]


def conv_tile(x_ref, k_ref, out_ref, start, size, mask, total, square):
    rows = slice(start, start + size)
    for p in range(4):
        pr, pc = p // 2, p % 2
        acc = None
        for qr in range(2):
            base = ((qr - pr + 1) * 3 + (1 - pc)) * 512
            acc = plus(acc, dot(x_ref[rows, qr * 1024 : (qr + 1) * 1024], k_ref[base : base + 1024, :]))
        out_ref[rows, p * 512 : (p + 1) * 512] = acc
        masked = acc * mask
        total = plus(total, fold8(masked))
        square = plus(square, fold8(masked * acc))
    return total, square


def first_kernel(count_ref, x_ref, k_ref, first_ref, stat_ref):
    count = count_ref[0]
    total = square = image_sum = None
    for start in range(0, x_ref.shape[0], CONV_TILE):
        mask = real_mask(count, start, CONV_TILE)
        total, square = conv_tile(x_ref, k_ref, first_ref, start, CONV_TILE, mask, total, square)
        for p in range(4):
            image_sum = plus(image_sum, fold8(x_ref[start : start + CONV_TILE, p * 512 : (p + 1) * 512].astype(F32)))
    (image_sum,) = column_sums((image_sum,))
    counts = jnp.full((1, 512), count.astype(F32), F32)
    spread_rows(stat_ref, column_sums((total, square)) + [counts, image_sum])


def load_pieces(place_ref, pieces, k_ref, load_sem):
    rows = pieces[0].shape[1]
    for n, piece in enumerate(pieces):
        cols = pl.ds((n // 4) * 256, 256)
        for i in range(piece.shape[0]):
            place = pl.multiple_of(place_ref[n * piece.shape[0] + i], 16)
            pltpu.make_async_copy(piece.at[i], k_ref.at[pl.ds(place, rows), cols], load_sem).start()
    pltpu.make_async_copy(k_ref, k_ref, load_sem).wait()


def first_gathered_kernel(count_ref, place_ref, x_ref, *refs):
    pieces, (first_ref, stat_ref, k_out_ref, k_ref, load_sem, store_sem) = refs[:8], refs[8:]
    load_pieces(place_ref, pieces, k_ref, load_sem)
    store = pltpu.make_async_copy(k_ref, k_out_ref, store_sem)
    store.start()
    first_kernel(count_ref, x_ref, k_ref, first_ref, stat_ref)
    store.wait()


def gelu_gate(v):
    return 0.5 * jnp.tanh(v * (GELU_A + GELU_B * (v * v))) + 0.5


def gelu_slope(v, gate):
    inner = v * (2.0 * GELU_A + (6.0 * GELU_B) * (v * v))
    return gate + gate * (inner - inner * gate)


def second_kernel(count_ref, first_ref, g1_ref, norm_ref, k_ref, hidden_ref, second_ref, stat_ref):
    mean, inverse = moments(g1_ref, images_total(g1_ref) * 4.0)
    scale = norm_ref[0:1, :] * inverse
    shift = norm_ref[1:2, :] - mean * scale
    total = square = hidden_sum = None
    for start in range(0, first_ref.shape[0], CONV_TILE):
        rows = slice(start, start + CONV_TILE)
        for p in range(4):
            v = first_ref[rows, p * 512 : (p + 1) * 512] * scale + shift
            hidden = (v * gelu_gate(v)).astype(BF16)
            hidden_ref[rows, p * 512 : (p + 1) * 512] = hidden
            hidden_sum = plus(hidden_sum, fold8(hidden.astype(F32)))
        mask = real_mask(count_ref[0], start, CONV_TILE)
        total, square = conv_tile(hidden_ref, k_ref, second_ref, start, CONV_TILE, mask, total, square)
    spread_rows(stat_ref, column_sums((total, square, hidden_sum)))


def head_kernel(
    tasks, count_ref, second_ref, g2_ref, g1_ref, norm_ref, image_ref, label_ref, head_ref, pick_ref,
    out_ref, slope_ref, slope_sum_ref, slope_xhat_ref, pooled_ref, resid_ref, gram_out_ref,
):
    real_total = images_total(g1_ref)
    mean, inverse = moments(g2_ref, real_total * 4.0)
    gain, shift = norm_ref[2:3, :], norm_ref[3:4, :]
    lane_real = (lax.broadcasted_iota(jnp.int32, (1, LANES), 1) < tasks).astype(F32)
    gram = None
    for start in range(0, second_ref.shape[0], TILE):
        rows = slice(start, start + TILE)
        pooled = slope_sum = slope_xhat = None
        for p in range(4):
            cols = slice(p * 512, (p + 1) * 512)
            xhat = (second_ref[rows, cols] - mean) * inverse
            pre = gain * xhat + shift + image_ref[rows, cols].astype(F32)
            gate = gelu_gate(pre)
            out = pre * gate
            out_ref[rows, cols] = out.astype(BF16)
            slope = gelu_slope(pre, gate)
            slope_ref[rows, cols] = slope
            pooled = plus(pooled, out)
            slope_sum = plus(slope_sum, slope)
            slope_xhat = plus(slope_xhat, slope * xhat)
        pooled = pooled * 0.25
        slope_sum_ref[rows, :] = slope_sum
        slope_xhat_ref[rows, :] = slope_xhat
        pooled_ref[rows, 0:512] = pooled
        pooled_ref[rows, 512:640] = (lax.broadcasted_iota(jnp.int32, (TILE, LANES), 1) == 0).astype(F32)
        logits = precise(pooled, head_ref[0:512, :], ((1,), (0,))) + head_ref[512:513, :]
        mask = real_mask(count_ref[0], start, TILE) * lane_real
        resid = mask * (jax.nn.sigmoid(logits) - label_ref[rows, :].astype(F32)) / real_total
        resid_ref[rows, :] = resid
        gram = plus(gram, precise(resid, resid, ((0,), (0,))))
    heads = head_ref[0:512, :]
    gram = gram * precise(heads, heads, ((0,), (0,)))
    basis = pick_ref[...]
    projected = precise(gram, basis, ((1,), (1,)))
    lane = lax.broadcasted_iota(jnp.int32, (32, LANES), 1)
    row = lax.broadcasted_iota(jnp.int32, (32, LANES), 0)
    packed = None
    for group in range(3):
        placed = precise(projected, (lane == row + 32 * group).astype(F32), ((1,), (0,)))
        packed = plus(packed, precise(basis[8 * group : 8 * group + 8, :], placed, ((1,), (0,))))
    gram_out_ref[...] = jnp.broadcast_to(packed[None], gram_out_ref.shape)


def frank_wolfe(packed, picks, start_mix, fw_steps):
    rows = jnp.concatenate([packed[:, 32 * g : 32 * g + 32] for g in range(3)], axis=0)
    column = [jnp.broadcast_to(rows[:, k : k + 1], (24, LANES)) for k in range(fw_steps + 1)]
    along = column[fw_steps]
    a = along[fw_steps : fw_steps + 1, :]
    mix = start_mix
    for k in range(fw_steps):
        b = along[k : k + 1, :]
        c = column[k][k : k + 1, :]
        size = jnp.clip((a - b) / (a - 2.0 * b + c), 0.0, STEP_CAP)
        keep = 1.0 - size
        a = keep * keep * a + 2.0 * (keep * size) * b + size * size * c
        along = keep * along + size * column[k]
        mix = keep * mix + size * picks[k : k + 1, :]
    return mix


def mix_kernel(
    fw_steps, gram_ref, pick_ref, start_ref, resid_ref, pooled_ref, head_ref, slope_sum_ref, slope_xhat_ref,
    dout_ref, stat_ref, head_grad_ref, mix_ref,
):
    mix = frank_wolfe(jnp.sum(gram_ref[...], 0), pick_ref[...], start_ref[0:1, :], fw_steps)
    mix_ref[...] = jnp.broadcast_to(mix, mix_ref.shape)
    gain_sum = shift_sum = head_grad = None
    for start in range(0, resid_ref.shape[0], TILE):
        rows = slice(start, start + TILE)
        weighted = resid_ref[rows, :] * mix
        dout = precise(weighted, head_ref[0:512, :], ((1,), (1,))) * 0.25
        dout_ref[rows, :] = dout
        head_grad = plus(head_grad, precise(weighted, pooled_ref[rows, :], ((0,), (0,))))
        gain_sum = plus(gain_sum, fold8(dout * slope_xhat_ref[rows, :]))
        shift_sum = plus(shift_sum, fold8(dout * slope_sum_ref[rows, :]))
    spread_rows(stat_ref, column_sums((gain_sum, shift_sum)))
    ways, cols = head_grad_ref.shape[0], head_grad_ref.shape[1]
    for way in range(ways):
        head_grad_ref[way] = head_grad[way * cols : (way + 1) * cols, :]


def split_halves(core, grad, half_refs, rows, p):
    if len(half_refs) == 1:
        half_refs[0][rows, p * grad.shape[1] : (p + 1) * grad.shape[1]] = grad
    else:
        half = grad.shape[1] // 2
        low, high = grad[:, :half], grad[:, half:]
        own_ref, send_ref = half_refs
        own_ref[rows, p * half : (p + 1) * half] = jnp.where(core == 0, low, high)
        send_ref[rows, p * half : (p + 1) * half] = jnp.where(core == 0, high, low)


def back_second_kernel(
    count_ref, core_ref, slope_ref, dout_ref, second_ref, first_ref, g1_ref, g2_ref, g4_ref, norm_ref, k_ref,
    dnormed_ref, stat_ref, *half_refs,
):
    spatial = images_total(g1_ref) * 4.0
    mean1, inverse1 = moments(g1_ref, spatial)
    mean2, inverse2 = moments(g2_ref, spatial)
    gain_grad, shift_grad = gathered_rows(g4_ref, 2)
    scale2 = norm_ref[2:3, :] * inverse2
    by_value = scale2 * gain_grad * inverse2 / spatial
    by_one = scale2 * shift_grad / spatial - by_value * mean2
    gain1, shift1 = norm_ref[0:1, :], norm_ref[1:2, :]
    gain_sum = shift_sum = None
    sums = [None] * 4
    *half_refs, dsecond_ref = half_refs
    for start in range(0, second_ref.shape[0], TILE):
        rows = slice(start, start + TILE)
        mask = real_mask(count_ref[0], start, TILE)
        dout = dout_ref[rows, :] * scale2
        for p in range(4):
            cols = slice(p * 512, (p + 1) * 512)
            grad = (dout * slope_ref[rows, cols] - mask * (by_one + by_value * second_ref[rows, cols])).astype(BF16)
            dsecond_ref[:, cols] = grad
            split_halves(core_ref[0], grad, half_refs, rows, p)
            sums[p] = plus(sums[p], fold8(grad.astype(F32)))
        for q in range(4):
            cols = slice(q * 512, (q + 1) * 512)
            acc = None
            for p in range(4):
                base = tap(q, p) * 512
                acc = plus(acc, dot_nt(dsecond_ref[:, p * 512 : (p + 1) * 512], k_ref[base : base + 512, :]))
            xhat = (first_ref[rows, cols] - mean1) * inverse1
            v = gain1 * xhat + shift1
            dnormed = acc * gelu_slope(v, gelu_gate(v))
            dnormed_ref[rows, cols] = dnormed
            gain_sum = plus(gain_sum, fold8(dnormed * xhat))
            shift_sum = plus(shift_sum, fold8(dnormed))
    spread_rows(stat_ref, column_sums([gain_sum, shift_sum] + sums))


def taps_of(index):
    return [(q, p) for q in range(4) for p in range(4) if tap(q, p) == index]


def weight_grad_kernel(x_ref, d_ref, out_ref):
    for index in range(9):
        acc = None
        for q, p in taps_of(index):
            acc = plus(acc, dot_tn(x_ref[:, q * 512 : (q + 1) * 512], d_ref[:, p * 512 : (p + 1) * 512]))
        out_ref[index * 512 : (index + 1) * 512, :] = acc


def as_column(row):
    return jnp.transpose(jnp.broadcast_to(row, (LANES, row.shape[1])))


def pair_weight_grad_kernel(
    mean_row, slots, table_ref, x_ref, d_ref, gathered_ref, x_other_ref, d_other_ref, send_ref, keep_ref, whole_ref,
):
    width = whole_ref.shape[1]
    mean = gathered_rows(gathered_ref, mean_row + 1)[mean_row] * (1.0 / slots)
    column = as_column(mean)
    column = jnp.concatenate([column] * (width // LANES), axis=1)
    sums = []
    for p in range(4):
        cols = slice(p * width, (p + 1) * width)
        sums.append(jnp.sum(fold8(d_ref[:, cols].astype(F32)) + fold8(d_other_ref[:, cols].astype(F32)), 0, keepdims=True))
    seen = set()
    for q in range(4):
        acc = dot_tn(x_ref[:, q * 512 : (q + 1) * 512], d_ref[...])
        acc = acc + dot_tn(x_other_ref[:, q * 512 : (q + 1) * 512], d_other_ref[...])
        for p in range(4):
            index = tap(q, p)
            rows = slice(index * 512, (index + 1) * 512)
            part = acc[:, p * width : (p + 1) * width] - column * sums[p]
            whole_ref[rows, :] = whole_ref[rows, :] + part if index in seen else part
            seen.add(index)
    count, rows = keep_ref.shape[0], keep_ref.shape[1]
    for i in range(count):
        there = pl.ds(pl.multiple_of(table_ref[i] * rows, 16), rows)
        here = pl.ds(pl.multiple_of(table_ref[count + i] * rows, 16), rows)
        send_ref[i] = whole_ref[there, :].astype(BF16)
        keep_ref[i] = whole_ref[here, :]


def dfirst_kernel(count_ref, core_ref, dnormed_ref, first_ref, g1_ref, g5_ref, norm_ref, dfirst_ref, stat_ref, *half_refs):
    spatial = images_total(g1_ref) * 4.0
    mean1, inverse1 = moments(g1_ref, spatial)
    gain_grad, shift_grad = gathered_rows(g5_ref, 2)
    scale = norm_ref[0:1, :] * inverse1
    by_value = scale * gain_grad * inverse1 / spatial
    by_one = scale * shift_grad / spatial - by_value * mean1
    sums = [None] * 4
    for start in range(0, first_ref.shape[0], TILE):
        rows = slice(start, start + TILE)
        mask = real_mask(count_ref[0], start, TILE)
        for p in range(4):
            cols = slice(p * 512, (p + 1) * 512)
            grad = (scale * dnormed_ref[rows, cols] - mask * (by_one + by_value * first_ref[rows, cols])).astype(BF16)
            dfirst_ref[rows, cols] = grad
            if half_refs:
                split_halves(core_ref[0], grad, half_refs, rows, p)
            sums[p] = plus(sums[p], fold8(grad.astype(F32)))
    for p, row in enumerate(column_sums(sums)):
        stat_ref[:, p : p + 1, 0:512] = jnp.broadcast_to(row[None], (stat_ref.shape[0], 1, 512))
        stat_ref[:, p : p + 1, 512:640] = jnp.zeros((stat_ref.shape[0], 1, LANES), F32)


def image_grad_kernel(dfirst_ref, k_ref, slope_ref, dout_ref, out_ref, buffer_ref, sem):
    copies = []
    for n, start in enumerate(range(0, dfirst_ref.shape[0], TILE)):
        rows = slice(start, start + TILE)
        slot = n % 2
        if n >= 2:
            copies[n - 2].wait()
        dout = dout_ref[rows, :]
        for q in range(4):
            cols = slice(q * 512, (q + 1) * 512)
            acc = dout * slope_ref[rows, cols]
            for p in range(4):
                base = tap(q, p) * 512
                acc = acc + dot_nt(dfirst_ref[rows, p * 512 : (p + 1) * 512], k_ref[base : base + 512, :])
            buffer_ref[slot, :, q // 2, q % 2, :] = acc
        copies.append(pltpu.make_async_copy(buffer_ref.at[slot], out_ref.at[pl.ds(start, TILE)], sem.at[slot]))
        copies[n].start()
    for copy in copies[-2:]:
        copy.wait()


def combine_kernel(table_ref, keep_ref, got_ref, send_ref, out_ref):
    count = out_ref.shape[0]
    for i in range(count):
        there, here = table_ref[i], table_ref[count + i]
        send_ref[i] = (keep_ref[there] + got_ref[there].astype(F32)).astype(BF16)
        out_ref[i] = keep_ref[here] + got_ref[here].astype(F32)


def line_kernel(z_ref, keep_ref, got_ref, *out_refs):
    for mask, ref in enumerate(out_refs):
        place = z_ref[0] ^ mask
        ref[...] = (keep_ref[place] + got_ref[place].astype(F32)).astype(ref.dtype)


def line_sum_kernel(core_ref, keep_ref, got1_ref, got2_ref, got3_ref, send_ref, out_ref):
    half = out_ref.shape[0]
    for ref, place in ((send_ref, 1 - core_ref[0]), (out_ref, core_ref[0])):
        rows = pl.ds(pl.multiple_of(place * half, 16), half)
        got = got1_ref[rows, :].astype(F32) + got2_ref[rows, :].astype(F32) + got3_ref[rows, :].astype(F32)
        ref[...] = keep_ref[rows, :] + got


def finish_kernel(
    slots, me_ref, keep1_ref, got1_ref, keep2_ref, got2_ref, g1_ref, last_ref, g2_ref, g5_ref, weight_ref, momentum_ref, average_ref,
    grad_ref, momentum_new_ref, weight_new_ref, average_new_ref, low_ref, column_ref, sums_ref,
):
    core, start = me_ref[0] % 2, me_ref[0] * grad_ref.shape[1]
    rows = grad_ref.shape[1]
    index = lax.broadcasted_iota(jnp.int32, (rows, 1), 0) + start % 512
    first_row = last_ref.shape[0] - 4
    last_sums = [last_ref[first_row + p : first_row + p + 1, 0:512] for p in range(4)]
    sources = (
        (keep1_ref, got1_ref, gathered_rows(g1_ref, 4)[3], last_sums),
        (keep2_ref, got2_ref, gathered_rows(g2_ref, 3)[2], gathered_rows(g5_ref, 6)[2:]),
    )
    for k, (keep_ref, got_ref, mean, sums) in enumerate(sources):
        column = as_column(mean * (1.0 / slots))
        column_ref[0:512, :] = column
        column_ref[512:1024, :] = column
        for tap_index in range(9):
            total = None
            for _, p in taps_of(tap_index):
                total = plus(total, sums[p])
            sums_ref[tap_index : tap_index + 1, :] = total
        column = column_ref[pl.ds(pl.multiple_of(start % 512, 16), rows), :]
        first_tap = start // 512
        total = jnp.where(index < 512, sums_ref[pl.ds(first_tap, 1), :], sums_ref[pl.ds(jnp.minimum(first_tap + 1, 8), 1), :])
        keep, got = keep_ref[...], got_ref[...]
        low_half, high_half = jnp.where(core == 0, keep, got), jnp.where(core == 0, got, keep)
        grad = jnp.concatenate([low_half, high_half], axis=1) + jnp.concatenate([column] * 4, axis=1) * total
        momentum, weight, average = nesterov(weight_ref[k], momentum_ref[k], grad, CONV_RATE, average_ref[k])
        grad_ref[k] = grad
        momentum_new_ref[k] = momentum
        weight_new_ref[k] = weight
        average_new_ref[k] = average
        low_ref[k] = weight.astype(BF16)


def swap(value, even_mask, odd_mask):
    count = lax.axis_size(AXES)
    pairs = [(i, i ^ (odd_mask if i % 2 else even_mask)) for i in range(count)]
    return lax.ppermute(value, AXES, pairs)


CORE, ALONG_X, ALONG_Y, ALONG_Z = 1, 2, 4, 8
SQUARE = [(ALONG_X, ALONG_Y), (ALONG_Y, ALONG_X)]


def flat_index():
    return lax.axis_index("dp") * lax.axis_size("task") + lax.axis_index("task")


def along_line(shard):
    return jnp.stack([shard] + [swap(shard, m * ALONG_Z, m * ALONG_Z) for m in (1, 2, 3)])


def square_near(line):
    blocks = [line[:, :, :256], line[:, :, 256:]]
    return [jnp.concatenate([blocks[h], swap(blocks[h], *SQUARE[h])], 0) for h in (0, 1)]


def square_far(near):
    return [swap(near[h], *SQUARE[1 - h]) for h in (0, 1)]


def gather_pieces(shard, images, early, later):
    line = along_line(shard)
    line, images, early = lax.optimization_barrier((line, images, early))
    near = square_near(line)
    near, later = lax.optimization_barrier((near, later))
    far = square_far(near)
    sibling_near = [swap(v, CORE, CORE) for v in near]
    sibling_far = [swap(v, CORE, CORE) for v in far]
    pieces = [v[h] for h in (0, 1) for v in (near, far, sibling_near, sibling_far)]
    return pieces, images, early, later


def piece_places(rows):
    me = flat_index()
    core = me % 2
    owners = []
    part = jnp.arange(8, dtype=jnp.int32)
    for h in (0, 1):
        for base, which, is_far in ((me, core, 0), (me, core, 1), (me ^ CORE, 1 - core, 0), (me ^ CORE, 1 - core, 1)):
            x_first = which == h
            near_mask = jnp.where(x_first, ALONG_X, ALONG_Y)
            far_mask = jnp.where(x_first, ALONG_Y, ALONG_X)
            owners.append(base ^ (part % 4 * ALONG_Z) ^ (part // 4 * near_mask) ^ (is_far * far_mask))
    return jnp.concatenate(owners) * rows


def nesterov(params, momentum, grads, rate, average):
    momentum_new = MOMENTUM_DECAY * momentum + grads
    params_new = params - rate * (grads + MOMENTUM_DECAY * momentum_new)
    average_new = AVERAGE_DECAY * average + (1.0 - AVERAGE_DECAY) * params_new
    return (momentum_new, params_new, average_new)


VMEM = pl.BlockSpec(memory_space=pltpu.VMEM)
SCALAR = pl.BlockSpec(memory_space=pltpu.SMEM)
ANYWHERE = pl.BlockSpec(memory_space=pl.ANY)


def call(body, ins, outs, scratch=(), scalars=(), loose=(), flops=0, aliases=None, limit=12):
    kinds = {"vmem": (pltpu.VMEM, VMEM), "hbm": (pltpu.HBM, ANYWHERE), "free": (jax.ShapeDtypeStruct, VMEM)}
    out_shape = [kinds[k][0](d, t) for d, t, k in outs]
    moved = sum(a.size * a.dtype.itemsize for a in list(ins) + list(loose))
    return pl.pallas_call(
        body,
        in_specs=[SCALAR] * len(scalars) + [VMEM] * len(ins) + [ANYWHERE] * len(loose),
        out_specs=[kinds[k][1] for _, _, k in outs],
        out_shape=out_shape,
        scratch_shapes=list(scratch),
        input_output_aliases=aliases or {},
        compiler_params=pltpu.CompilerParams(vmem_limit_bytes=limit << 20),
        cost_estimate=pl.CostEstimate(flops=flops, bytes_accessed=moved, transcendentals=0),
    )(*scalars, *[pltpu.with_memory_space_constraint(a, pltpu.VMEM) for a in ins], *loose)


def exchange(replicated):
    return lax.all_to_all(replicated, AXES, 0, 0)


def on_device(
    images, image_counts, labels, fw_picks, task_average, conv_weights, conv_momentum, conv_average,
    norm_parameter_list, norm_momentum, norm_average, head_params, head_momentum, head_average,
):
    rows, map_side, channels = images.shape[0], images.shape[1], images.shape[3]
    width = map_side * map_side * channels
    devices = lax.axis_size(AXES)
    tasks = labels.shape[1]
    task_cols = head_params.shape[1]
    fw_steps = fw_picks.shape[0]
    matmul = 2 * rows * width * width
    tuned = (lax.axis_size("dp"), lax.axis_size("task"), channels) == (8, 4, 512)

    def stat(lines):
        return ((devices, lines, LANES), F32, "free")

    slots = float(devices * rows * map_side * map_side)
    flat, flat_low = ((rows, width), F32, "vmem"), ((rows, width), BF16, "vmem")
    low = conv_weights.astype(BF16)
    heads = lax.all_gather(head_params, "task", axis=1, tiled=True)
    heads = jnp.pad(heads, ((0, 7), (0, LANES - tasks)))
    labels = jnp.pad(labels, ((0, 0), (0, LANES - tasks)))
    flat_images = images.reshape(rows, width)
    start = jnp.pad(task_average[None, :], ((0, 7), (0, LANES - tasks)))
    basis = jnp.concatenate(
        [
            (jnp.arange(LANES, dtype=jnp.int32)[None, :] == fw_picks[:, None]).astype(F32),
            start[0:1],
            jnp.zeros((32 - fw_steps - 1, LANES), F32),
        ],
        axis=0,
    )

    me = flat_index()
    core = me & 1

    def bind(body, *static):
        return lambda *refs: body(*static, *refs)

    k2 = lax.all_gather(low[1], AXES, axis=0, tiled=True)
    if tuned:
        tall_low = (9 * channels, channels)
        chips = devices // 2
        at_x, at_y = me // ALONG_X & 1, me // ALONG_Y & 1
        index = jnp.arange(chips // 2, dtype=jnp.int32)
        by_x, by_y = index * 2, index // 2 * 4 + index % 2
        here = jnp.where(core == 0, by_x + at_x, by_y + 2 * at_y)
        there = jnp.where(core == 0, by_x + 1 - at_x, by_y + 2 * (1 - at_y))
        own = jnp.where(core == 0, at_y, at_x)
        index = jnp.arange(chips // 4, dtype=jnp.int32) * 2
        tables = (
            piece_places(low.shape[1]), jnp.concatenate([there, here]), jnp.concatenate([index + 1 - own, index + own]),
            (me // ALONG_Z)[None], core[None], me[None], image_counts + 0,
        )
        pieces, flat_images, (tables, start, basis), (heads, labels) = gather_pieces(
            low[0], flat_images, (tables, start, basis), (heads, labels)
        )
        places, chunk_table, pair_table, z_place, core_place, me_place, image_counts = tables
        first, stat1, k1 = call(
            first_gathered_kernel, [flat_images], [flat, stat(16), (tall_low, BF16, "hbm")],
            [pltpu.VMEM(tall_low, BF16), pltpu.SemaphoreType.DMA, pltpu.SemaphoreType.DMA],
            (image_counts, places), pieces, matmul, limit=7,
        )
    else:
        k1 = lax.all_gather(low[0], AXES, axis=0, tiled=True)
        first, stat1 = call(first_kernel, [flat_images, k1], [flat, stat(16)], (), (image_counts,), (), matmul)
    if tuned:
        images_other = swap(flat_images, CORE, CORE)
        stat1, images_other = lax.optimization_barrier((stat1, images_other))
    else:
        core_place = core[None]
    g1 = exchange(stat1)
    hidden, second, stat2 = call(
        second_kernel, [first, g1, norm_parameter_list, k2], [flat_low, flat, stat(12)], (), (image_counts,), (), matmul, limit=9
    )
    g2 = exchange(stat2)
    if tuned:
        g2, moved_hidden = lax.optimization_barrier((g2, hidden))
        hidden_other = swap(moved_hidden, CORE, CORE)
    per_channel = ((rows, channels), F32, "vmem")
    block_flat, slope, slope_sum, slope_xhat, pooled, resid, gram = call(
        bind(head_kernel, tasks), [second, g2, g1, norm_parameter_list, flat_images, labels, heads, basis],
        [flat_low, flat, per_channel, per_channel, ((rows, channels + LANES), F32, "vmem"), ((rows, LANES), F32, "vmem"), stat(8)],
        (), (image_counts,), (), matmul, limit=3,
    )
    if tuned:
        gram, hidden_other = lax.optimization_barrier((gram, hidden_other))
    g3 = exchange(gram)
    dout, stat4, head_send, mix = call(
        bind(mix_kernel, fw_steps), [g3, basis, start, resid, pooled, heads, slope_sum, slope_xhat],
        [per_channel, stat(8), ((tasks // task_cols, task_cols, channels + LANES), F32, "free"), ((8, LANES), F32, "free")],
        (), (), (), matmul // 2, limit=3,
    )
    g4 = exchange(stat4)
    part = channels // 2
    shard_rows = conv_weights.shape[1]
    sent = [((rows, width // 2), BF16, "vmem")] * 2 if tuned else [flat_low]
    dnormed, stat5, *dsecond_halves = call(
        back_second_kernel, [slope, dout, second, first, g1, g2, g4, norm_parameter_list, k2],
        [flat, stat(24)] + sent, [pltpu.VMEM((TILE, width), BF16)], (image_counts, core_place), (), matmul, {4: 0}, limit=11,
    )
    g5 = exchange(stat5)
    if tuned:
        g5, *dsecond_halves = lax.optimization_barrier((g5, *dsecond_halves))
        dsecond_other = swap(dsecond_halves[1], CORE, CORE)
    stat6_ways = devices // lax.axis_size("dp")
    dfirst, stat6, *dfirst_halves = call(
        dfirst_kernel, [dnormed, first, g1, g5, norm_parameter_list],
        [flat_low, ((stat6_ways, 4, channels + LANES), F32, "free")] + (sent if tuned else []), (), (image_counts, core_place), (), matmul // 4, limit=8,
    )

    def combine(keep, got, table):
        dims = (keep.shape[0] // 2,) + keep.shape[1:]
        return call(combine_kernel, [keep, got], [(dims, BF16, "free"), (dims, F32, "vmem")], (), (table,), limit=5)

    def scatter_start(x, x_other, d, d_other, gathered, mean_row):
        dims = (devices // 4, 2 * shard_rows, part)
        return call(
            bind(pair_weight_grad_kernel, mean_row, slots), [x, d, gathered, x_other, d_other],
            [(dims, BF16, "free"), (dims, F32, "vmem")], [pltpu.VMEM((9 * channels, part), F32)],
            (chunk_table,), (), matmul, limit=18,
        )

    def scatter_next(send, keep):
        return combine(keep, swap(send, *SQUARE[0]), pair_table)

    def scatter_finish(send, keep):
        got = swap(send, *SQUARE[1])
        pair = keep.shape[1:]
        blocks = call(line_kernel, [keep, got], [(pair, F32, "vmem")] + [(pair, BF16, "free")] * 3, (), (z_place,), limit=3)
        parts = [blocks[0]] + [swap(blocks[m], m * ALONG_Z, m * ALONG_Z) for m in (1, 2, 3)]
        half = ((shard_rows, part), F32, "free")
        send, keep = call(line_sum_kernel, parts, [half, half], (), (core_place,), limit=3)
        return keep, swap(send, CORE, CORE)

    def scatter_whole(x, d):
        (whole,) = call(weight_grad_kernel, [x, d], [((9 * channels, channels), F32, "free")], (), (), (), matmul)
        return lax.psum_scatter(whole, AXES, scatter_dimension=0, tiled=True)

    def share(head, sums):
        over_task = lax.all_to_all(jnp.concatenate([head, sums], axis=1), "task", 0, 0)
        total = jnp.sum(over_task, 0)
        over_dp = jnp.broadcast_to(total[None], (lax.axis_size("dp"),) + total.shape)
        return jnp.sum(lax.all_to_all(over_dp, "dp", 0, 0), 0)

    if tuned:
        dfirst_other = swap(dfirst_halves[1], CORE, CORE)
        dsecond_own, dsecond_other, hidden, hidden_other, dfirst = lax.optimization_barrier(
            (dsecond_halves[0], dsecond_other, hidden, hidden_other, dfirst)
        )
        two = scatter_start(hidden, hidden_other, dsecond_own, dsecond_other, g2, 2)
        send_two, flat_images, images_other, dfirst_own = lax.optimization_barrier((two[0], flat_images, images_other, dfirst_halves[0]))
        one = scatter_start(flat_images, images_other, dfirst_own, dfirst_other, g1, 3)
        send_one, head_send, stat6 = lax.optimization_barrier((one[0], head_send, stat6))
        two = scatter_next(send_two, two[1])
        two_send, head_send = lax.optimization_barrier((two[0], head_send))
        last = share(head_send, stat6)
        one = scatter_next(send_one, one[1])
        one_send, late, last = lax.optimization_barrier((one[0], dfirst, last))
    else:
        late = dfirst
        last = share(head_send, stat6)
        grad_two = scatter_whole(hidden, dsecond_halves[0])
        grad_one = scatter_whole(flat_images, dfirst)
    (image_grad,) = call(
        image_grad_kernel, [late, k1, slope, dout], [(images.shape, F32, "hbm")],
        [pltpu.VMEM((2, TILE) + images.shape[1:], F32), pltpu.SemaphoreType.DMA((2,))], (), (), matmul, limit=8,
    )
    head_grads = last[:task_cols, : channels + 1].T
    if tuned:
        shards = conv_weights.shape
        outs = [(shards, F32, "free")] * 4 + [(shards, BF16, "free")]
        conv_grads, conv_momentum_new, conv_weights_new, conv_average_new, conv_weights_low = call(
            bind(finish_kernel, slots),
            list(scatter_finish(one_send, one[1])) + list(scatter_finish(two_send, two[1])) + [g1, last, g2, g5, conv_weights, conv_momentum, conv_average],
            outs, [pltpu.VMEM((1024, LANES), F32), pltpu.VMEM((16, channels), F32)], (me_place,), limit=5,
        )
    else:
        conv_grads = jnp.stack([grad_one, grad_two])
        conv_momentum_new, conv_weights_new, conv_average_new = nesterov(conv_weights, conv_momentum, conv_grads, CONV_RATE, conv_average)
        conv_weights_low = conv_weights_new.astype(BF16)
    task_average_new = AVERAGE_DECAY * task_average + (1.0 - AVERAGE_DECAY) * mix[0, :tasks]
    sums4 = jnp.sum(g4, 0).reshape(2, channels)
    sums5 = jnp.sum(g5[:, :8], 0).reshape(2, channels)
    norm_grads = jnp.concatenate([sums5, sums4], axis=0)
    norm_momentum_new, norm_params_new, norm_average_new = nesterov(
        norm_parameter_list, norm_momentum, norm_grads, NORM_RATE, norm_average
    )
    head_momentum_new, head_params_new, head_average_new = nesterov(head_params, head_momentum, head_grads, HEAD_RATE, head_average)
    return (
        block_flat.reshape(images.shape),
        image_grad,
        conv_grads,
        conv_momentum_new,
        conv_weights_new,
        conv_average_new,
        conv_weights_low,
        norm_grads,
        norm_momentum_new,
        norm_params_new,
        norm_average_new,
        head_grads,
        head_momentum_new,
        head_params_new,
        head_average_new,
        task_average_new,
    )


def solution(mesh):
    both = P(AXES)
    rowwise = P(None, AXES, None)
    head = P(None, "task")
    return jax.shard_map(
        on_device,
        mesh=mesh,
        in_specs=(both, both, both, P(), P(), rowwise, rowwise, rowwise, P(), P(), P(), head, head, head),
        out_specs=(both, both, rowwise, rowwise, rowwise, rowwise, rowwise, P(), P(), P(), P(), head, head, head, head, P()),
        check_vma=False,
    )
```

```python
import jax
import jax.numpy as jnp
import numpy as np
from jax import lax
from jax.experimental import pallas as pl
from jax.experimental.pallas import tpu as pltpu
from jax.sharding import PartitionSpec as P

EPSILON = 1e-05
MOMENTUM_DECAY = 0.5
AVERAGE_DECAY = 0.5
CONV_RATE = 2000.0
NORM_RATE = 40000.0
HEAD_RATE = 1000.0
STEP_CAP = 0.5
GROUP = 21
GELU_A = 0.7978845608
GELU_B = 0.7978845608 * 0.044715
AXES = ("dp", "task")
PRECISE = lax.Precision.HIGHEST
F32 = jnp.float32
BF16 = jnp.bfloat16
TILE = 256
CONV_TILE = 512
LANES = 128


def tap(q, p):
    return (q // 2 - p // 2 + 1) * 3 + (q % 2 - p % 2 + 1)


def dot(a, b):
    return jnp.dot(a, b, preferred_element_type=F32)


def dot_nt(a, b):
    return lax.dot_general(a, b, (((1,), (1,)), ((), ())), preferred_element_type=F32)


def dot_tn(a, b):
    return lax.dot_general(a, b, (((0,), (0,)), ((), ())), preferred_element_type=F32)


def precise(a, b, dims):
    return lax.dot_general(a, b, ((dims[0], dims[1]), ((), ())), precision=PRECISE, preferred_element_type=F32)


def fold8(v):
    return jnp.sum(v.reshape(v.shape[0] // 8, 8, v.shape[1]), 0)


def spread_rows(out_ref, rows):
    row = jnp.concatenate(rows, axis=1)
    out_ref[...] = jnp.broadcast_to(row[None], (out_ref.shape[0], 1, row.shape[1]))


def gathered_rows(ref, count):
    total = jnp.sum(ref[...], 0)
    return [total[:, r * 512 : (r + 1) * 512] for r in range(count)]


def moments(gathered_ref, spatial):
    value_sum, square_sum = gathered_rows(gathered_ref, 2)
    mean = value_sum / spatial
    inverse = lax.rsqrt(square_sum / spatial - mean * mean + EPSILON)
    return mean, inverse


def images_total(g1_ref):
    return jnp.sum(g1_ref[:, :, 1024:1152], 0)[:, 0:1]


def real_mask(count, start, rows):
    index = lax.broadcasted_iota(jnp.int32, (rows, 1), 0) + start
    return (index < count).astype(F32)


def plus(total, value):
    return value if total is None else total + value


def column_sums(values):
    return [jnp.sum(v, 0, keepdims=True) for v in values]


def conv_tile(x_ref, k_ref, out_ref, start, size, mask, total, square):
    rows = slice(start, start + size)
    for p in range(4):
        pr, pc = p // 2, p % 2
        acc = None
        for qr in range(2):
            base = ((qr - pr + 1) * 3 + (1 - pc)) * 512
            acc = plus(acc, dot(x_ref[rows, qr * 1024 : (qr + 1) * 1024], k_ref[base : base + 1024, :]))
        out_ref[rows, p * 512 : (p + 1) * 512] = acc
        masked = acc * mask
        total = plus(total, fold8(masked))
        square = plus(square, fold8(masked * acc))
    return total, square


def first_kernel(count_ref, x_ref, k_ref, first_ref, stat_ref):
    count = count_ref[0]
    total = square = None
    for start in range(0, x_ref.shape[0], CONV_TILE):
        mask = real_mask(count, start, CONV_TILE)
        total, square = conv_tile(x_ref, k_ref, first_ref, start, CONV_TILE, mask, total, square)
    spread_rows(stat_ref, column_sums((total, square)) + [jnp.full((1, LANES), count.astype(F32), F32)])


def load_pieces(place_ref, pieces, k_ref, load_sem):
    rows = pieces[0].shape[1]
    for n, piece in enumerate(pieces):
        cols = pl.ds((n // 4) * 256, 256)
        for i in range(piece.shape[0]):
            place = pl.multiple_of(place_ref[n * piece.shape[0] + i], 16)
            pltpu.make_async_copy(piece.at[i], k_ref.at[pl.ds(place, rows), cols], load_sem).start()
    pltpu.make_async_copy(k_ref, k_ref, load_sem).wait()


def first_gathered_kernel(count_ref, place_ref, x_ref, *refs):
    pieces, (first_ref, stat_ref, k_out_ref, k_ref, load_sem, store_sem) = refs[:8], refs[8:]
    load_pieces(place_ref, pieces, k_ref, load_sem)
    store = pltpu.make_async_copy(k_ref, k_out_ref, store_sem)
    store.start()
    first_kernel(count_ref, x_ref, k_ref, first_ref, stat_ref)
    store.wait()


def gelu_gate(v):
    return 0.5 * jnp.tanh(v * (GELU_A + GELU_B * (v * v))) + 0.5


def gelu_slope(v, gate):
    inner = v * (2.0 * GELU_A + (6.0 * GELU_B) * (v * v))
    return gate + gate * (inner - inner * gate)


def second_kernel(count_ref, first_ref, g1_ref, norm_ref, k_ref, hidden_ref, second_ref, stat_ref):
    mean, inverse = moments(g1_ref, images_total(g1_ref) * 4.0)
    scale = norm_ref[0:1, :] * inverse
    shift = norm_ref[1:2, :] - mean * scale
    total = square = None
    for start in range(0, first_ref.shape[0], CONV_TILE):
        rows = slice(start, start + CONV_TILE)
        for p in range(4):
            v = first_ref[rows, p * 512 : (p + 1) * 512] * scale + shift
            hidden_ref[rows, p * 512 : (p + 1) * 512] = (v * gelu_gate(v)).astype(BF16)
        mask = real_mask(count_ref[0], start, CONV_TILE)
        total, square = conv_tile(hidden_ref, k_ref, second_ref, start, CONV_TILE, mask, total, square)
    spread_rows(stat_ref, column_sums((total, square)))


def head_kernel(
    tasks, count_ref, second_ref, g2_ref, g1_ref, norm_ref, image_ref, label_ref, head_ref, pick_ref,
    out_ref, slope_ref, slope_sum_ref, slope_xhat_ref, pooled_ref, resid_ref, gram_out_ref,
):
    real_total = images_total(g1_ref)
    mean, inverse = moments(g2_ref, real_total * 4.0)
    gain, shift = norm_ref[2:3, :], norm_ref[3:4, :]
    lane_real = (lax.broadcasted_iota(jnp.int32, (1, LANES), 1) < tasks).astype(F32)
    gram = image_sum = None
    for start in range(0, second_ref.shape[0], TILE):
        rows = slice(start, start + TILE)
        pooled = slope_sum = slope_xhat = None
        for p in range(4):
            cols = slice(p * 512, (p + 1) * 512)
            xhat = (second_ref[rows, cols] - mean) * inverse
            image = image_ref[rows, cols].astype(F32)
            image_sum = plus(image_sum, fold8(image))
            pre = gain * xhat + shift + image
            gate = gelu_gate(pre)
            out = pre * gate
            out_ref[rows, cols] = out.astype(BF16)
            slope = gelu_slope(pre, gate)
            slope_ref[rows, cols] = slope
            pooled = plus(pooled, out)
            slope_sum = plus(slope_sum, slope)
            slope_xhat = plus(slope_xhat, slope * xhat)
        pooled = pooled * 0.25
        slope_sum_ref[rows, :] = slope_sum
        slope_xhat_ref[rows, :] = slope_xhat
        pooled_ref[rows, 0:512] = pooled
        pooled_ref[rows, 512:640] = (lax.broadcasted_iota(jnp.int32, (TILE, LANES), 1) == 0).astype(F32)
        logits = precise(pooled, head_ref[0:512, :], ((1,), (0,))) + head_ref[512:513, :]
        mask = real_mask(count_ref[0], start, TILE) * lane_real
        resid = mask * (jax.nn.sigmoid(logits) - label_ref[rows, :].astype(F32)) / real_total
        resid_ref[rows, :] = resid
        gram = plus(gram, precise(resid, resid, ((0,), (0,))))
    heads = head_ref[0:512, :]
    gram = gram * precise(heads, heads, ((0,), (0,)))
    basis = pick_ref[...]
    projected = precise(gram, basis, ((1,), (1,)))
    lane = lax.broadcasted_iota(jnp.int32, (32, LANES), 1)
    row = lax.broadcasted_iota(jnp.int32, (32, LANES), 0)
    packed = None
    for group in range(6):
        placed = precise(projected, ((lane == row + GROUP * group) & (row < GROUP)).astype(F32), ((1,), (0,)))
        packed = plus(packed, precise(basis[4 * group : 4 * group + 4, :], placed, ((1,), (0,))))
    spread_rows(gram_out_ref, [packed[r : r + 1, :] for r in range(4)] + column_sums((image_sum,)))


def frank_wolfe(packed, picks, start_mix, fw_steps):
    rows = jnp.concatenate([packed[:, GROUP * g : GROUP * (g + 1)] for g in range(6)], axis=0)
    column = [jnp.broadcast_to(rows[:, k : k + 1], (24, LANES)) for k in range(fw_steps + 1)]
    along = column[fw_steps]
    a = along[fw_steps : fw_steps + 1, :]
    mix = start_mix
    for k in range(fw_steps):
        b = along[k : k + 1, :]
        c = column[k][k : k + 1, :]
        size = jnp.clip((a - b) / (a - 2.0 * b + c), 0.0, STEP_CAP)
        keep = 1.0 - size
        a = keep * keep * a + 2.0 * (keep * size) * b + size * size * c
        along = keep * along + size * column[k]
        mix = keep * mix + size * picks[k : k + 1, :]
    return mix


def mix_kernel(
    fw_steps, gram_ref, pick_ref, start_ref, resid_ref, pooled_ref, head_ref, slope_sum_ref, slope_xhat_ref,
    dout_ref, stat_ref, head_grad_ref, mix_ref,
):
    (total,) = gathered_rows(gram_ref, 1)
    packed = jnp.concatenate([total[:, r * LANES : (r + 1) * LANES] for r in range(4)], axis=0)
    mix = frank_wolfe(packed, pick_ref[...], start_ref[0:1, :], fw_steps)
    mix_ref[...] = jnp.broadcast_to(mix, mix_ref.shape)
    gain_sum = shift_sum = head_grad = None
    for start in range(0, resid_ref.shape[0], TILE):
        rows = slice(start, start + TILE)
        weighted = resid_ref[rows, :] * mix
        dout = precise(weighted, head_ref[0:512, :], ((1,), (1,))) * 0.25
        dout_ref[rows, :] = dout
        head_grad = plus(head_grad, precise(weighted, pooled_ref[rows, :], ((0,), (0,))))
        gain_sum = plus(gain_sum, fold8(dout * slope_xhat_ref[rows, :]))
        shift_sum = plus(shift_sum, fold8(dout * slope_sum_ref[rows, :]))
    spread_rows(stat_ref, column_sums((gain_sum, shift_sum)))
    ways, cols = head_grad_ref.shape[0], head_grad_ref.shape[1]
    for way in range(ways):
        head_grad_ref[way] = head_grad[way * cols : (way + 1) * cols, :]


def store_sums(sum_ref, sums):
    for p, row in enumerate(column_sums(sums)):
        sum_ref[:, p : p + 1, 0:512] = jnp.broadcast_to(row[None], (sum_ref.shape[0], 1, 512))
        sum_ref[:, p : p + 1, 512:640] = jnp.zeros((sum_ref.shape[0], 1, LANES), F32)


def split_halves(core, grad, half_refs, rows, p):
    if len(half_refs) == 1:
        half_refs[0][rows, p * grad.shape[1] : (p + 1) * grad.shape[1]] = grad
    else:
        half = grad.shape[1] // 2
        low, high = grad[:, :half], grad[:, half:]
        own_ref, send_ref = half_refs
        own_ref[rows, p * half : (p + 1) * half] = jnp.where(core == 0, low, high)
        send_ref[rows, p * half : (p + 1) * half] = jnp.where(core == 0, high, low)


def back_second_kernel(
    count_ref, core_ref, slope_ref, dout_ref, second_ref, first_ref, g1_ref, g2_ref, g4_ref, norm_ref, k_ref,
    dnormed_ref, stat_ref, sum_ref, dpre_ref, *half_refs,
):
    spatial = images_total(g1_ref) * 4.0
    mean1, inverse1 = moments(g1_ref, spatial)
    mean2, inverse2 = moments(g2_ref, spatial)
    gain_grad, shift_grad = gathered_rows(g4_ref, 2)
    scale2 = norm_ref[2:3, :] * inverse2
    by_value = scale2 * gain_grad * inverse2 / spatial
    by_one = scale2 * shift_grad / spatial - by_value * mean2
    gain1, shift1 = norm_ref[0:1, :], norm_ref[1:2, :]
    gain_sum = shift_sum = None
    sums = [None] * 4
    *half_refs, dsecond_ref = half_refs
    for start in range(0, second_ref.shape[0], TILE):
        rows = slice(start, start + TILE)
        mask = real_mask(count_ref[0], start, TILE)
        dout = dout_ref[rows, :]
        for p in range(4):
            cols = slice(p * 512, (p + 1) * 512)
            dpre = dout * slope_ref[rows, cols]
            dpre_ref[rows, cols] = dpre.astype(BF16)
            grad = (scale2 * dpre - mask * (by_one + by_value * second_ref[rows, cols])).astype(BF16)
            dsecond_ref[:, cols] = grad
            split_halves(core_ref[0], grad, half_refs, rows, p)
            sums[p] = plus(sums[p], fold8(grad.astype(F32)))
        for q in range(4):
            cols = slice(q * 512, (q + 1) * 512)
            acc = None
            for p in range(4):
                base = tap(q, p) * 512
                acc = plus(acc, dot_nt(dsecond_ref[:, p * 512 : (p + 1) * 512], k_ref[base : base + 512, :]))
            xhat = (first_ref[rows, cols] - mean1) * inverse1
            v = gain1 * xhat + shift1
            dnormed = acc * gelu_slope(v, gelu_gate(v))
            dnormed_ref[rows, cols] = dnormed
            gain_sum = plus(gain_sum, fold8(dnormed * xhat))
            shift_sum = plus(shift_sum, fold8(dnormed))
    spread_rows(stat_ref, column_sums((gain_sum, shift_sum)))
    store_sums(sum_ref, sums)


def taps_of(index):
    return [(q, p) for q in range(4) for p in range(4) if tap(q, p) == index]


def weight_grad_kernel(x_ref, d_ref, out_ref):
    for index in range(9):
        acc = None
        for q, p in taps_of(index):
            acc = plus(acc, dot_tn(x_ref[:, q * 512 : (q + 1) * 512], d_ref[:, p * 512 : (p + 1) * 512]))
        out_ref[index * 512 : (index + 1) * 512, :] = acc


def as_column(row):
    return jnp.transpose(jnp.broadcast_to(row, (LANES, row.shape[1])))


def image_mean(slots, g3_ref):
    return gathered_rows(g3_ref, 2)[1] * (1.0 / slots)


def hidden_mean(norm_ref):
    nodes, weights = np.polynomial.hermite_e.hermegauss(9)
    total = None
    for node, weight in zip(nodes, weights / weights.sum()):
        v = norm_ref[0:1, :] * float(node) + norm_ref[1:2, :]
        total = plus(total, float(weight) * (v * gelu_gate(v)))
    return total


def pair_weight_grad_kernel(mean_of, table_ref, x_ref, d_ref, mean_ref, x_other_ref, d_other_ref, send_ref, keep_ref, whole_ref):
    width = whole_ref.shape[1]
    column = as_column(mean_of(mean_ref))
    column = jnp.concatenate([column] * (width // LANES), axis=1)
    sums = []
    for p in range(4):
        cols = slice(p * width, (p + 1) * width)
        sums.append(jnp.sum(fold8(d_ref[:, cols].astype(F32)) + fold8(d_other_ref[:, cols].astype(F32)), 0, keepdims=True))
    seen = set()
    for q in range(4):
        acc = dot_tn(x_ref[:, q * 512 : (q + 1) * 512], d_ref[...])
        acc = acc + dot_tn(x_other_ref[:, q * 512 : (q + 1) * 512], d_other_ref[...])
        for p in range(4):
            index = tap(q, p)
            rows = slice(index * 512, (index + 1) * 512)
            part = acc[:, p * width : (p + 1) * width] - column * sums[p]
            whole_ref[rows, :] = whole_ref[rows, :] + part if index in seen else part
            seen.add(index)
    count, rows = keep_ref.shape[0], keep_ref.shape[1]
    for i in range(count):
        there = pl.ds(pl.multiple_of(table_ref[i] * rows, 16), rows)
        here = pl.ds(pl.multiple_of(table_ref[count + i] * rows, 16), rows)
        send_ref[i] = whole_ref[there, :].astype(BF16)
        keep_ref[i] = whole_ref[here, :]


def dfirst_kernel(count_ref, core_ref, dnormed_ref, first_ref, g1_ref, g5_ref, norm_ref, dfirst_ref, stat_ref, *half_refs):
    spatial = images_total(g1_ref) * 4.0
    mean1, inverse1 = moments(g1_ref, spatial)
    gain_grad, shift_grad = gathered_rows(g5_ref, 2)
    scale = norm_ref[0:1, :] * inverse1
    by_value = scale * gain_grad * inverse1 / spatial
    by_one = scale * shift_grad / spatial - by_value * mean1
    sums = [None] * 4
    for start in range(0, first_ref.shape[0], TILE):
        rows = slice(start, start + TILE)
        mask = real_mask(count_ref[0], start, TILE)
        for p in range(4):
            cols = slice(p * 512, (p + 1) * 512)
            grad = (scale * dnormed_ref[rows, cols] - mask * (by_one + by_value * first_ref[rows, cols])).astype(BF16)
            dfirst_ref[rows, cols] = grad
            if half_refs:
                split_halves(core_ref[0], grad, half_refs, rows, p)
            sums[p] = plus(sums[p], fold8(grad.astype(F32)))
    store_sums(stat_ref, sums)


def image_grad_kernel(begin, end, dfirst_ref, k_ref, dpre_ref, *refs):
    out_ref, buffer_ref, sem = refs[-3:]
    copies = []
    for n, start in enumerate(range(begin, end, TILE)):
        rows = slice(start, start + TILE)
        slot = n % 2
        if n >= 2:
            copies[n - 2].wait()
        for q in range(4):
            cols = slice(q * 512, (q + 1) * 512)
            acc = dpre_ref[rows, cols].astype(F32)
            for p in range(4):
                base = tap(q, p) * 512
                acc = acc + dot_nt(dfirst_ref[rows, p * 512 : (p + 1) * 512], k_ref[base : base + 512, :])
            buffer_ref[slot, :, q // 2, q % 2, :] = acc
        copies.append(pltpu.make_async_copy(buffer_ref.at[slot], out_ref.at[pl.ds(start, TILE)], sem.at[slot]))
        copies[n].start()
    for copy in copies[-2:]:
        copy.wait()


def combine_kernel(table_ref, keep_ref, got_ref, send_ref, out_ref):
    count = out_ref.shape[0]
    for i in range(count):
        there, here = table_ref[i], table_ref[count + i]
        send_ref[i] = (keep_ref[there] + got_ref[there].astype(F32)).astype(BF16)
        out_ref[i] = keep_ref[here] + got_ref[here].astype(F32)


def line_kernel(z_ref, keep_ref, got_ref, *out_refs):
    for mask, ref in enumerate(out_refs):
        place = z_ref[0] ^ mask
        ref[...] = (keep_ref[place] + got_ref[place].astype(F32)).astype(ref.dtype)


def line_sum_kernel(core_ref, keep_ref, got1_ref, got2_ref, got3_ref, send_ref, out_ref):
    half = out_ref.shape[0]
    for ref, place in ((send_ref, 1 - core_ref[0]), (out_ref, core_ref[0])):
        rows = pl.ds(pl.multiple_of(place * half, 16), half)
        got = got1_ref[rows, :].astype(F32) + got2_ref[rows, :].astype(F32) + got3_ref[rows, :].astype(F32)
        ref[...] = keep_ref[rows, :] + got


def finish_kernel(
    slots, me_ref, keep1_ref, got1_ref, keep2_ref, got2_ref, g3_ref, norm_ref, last_ref, weight_ref, momentum_ref, average_ref,
    grad_ref, momentum_new_ref, weight_new_ref, average_new_ref, low_ref, column_ref, sums_ref,
):
    core, start = me_ref[0] % 2, me_ref[0] * grad_ref.shape[1]
    rows = grad_ref.shape[1]
    index = lax.broadcasted_iota(jnp.int32, (rows, 1), 0) + start % 512
    first_row = last_ref.shape[1] - 8
    last = jnp.sum(last_ref[...], 0)
    sums = [last[first_row + p : first_row + p + 1, 0:512] for p in range(8)]
    sources = (
        (keep1_ref, got1_ref, image_mean(slots, g3_ref), sums[4:]),
        (keep2_ref, got2_ref, hidden_mean(norm_ref), sums[:4]),
    )
    for k, (keep_ref, got_ref, mean, sums) in enumerate(sources):
        column = as_column(mean)
        column_ref[0:512, :] = column
        column_ref[512:1024, :] = column
        for tap_index in range(9):
            total = None
            for _, p in taps_of(tap_index):
                total = plus(total, sums[p])
            sums_ref[tap_index : tap_index + 1, :] = total
        column = column_ref[pl.ds(pl.multiple_of(start % 512, 16), rows), :]
        first_tap = start // 512
        total = jnp.where(index < 512, sums_ref[pl.ds(first_tap, 1), :], sums_ref[pl.ds(jnp.minimum(first_tap + 1, 8), 1), :])
        keep, got = keep_ref[...], got_ref[...]
        low_half, high_half = jnp.where(core == 0, keep, got), jnp.where(core == 0, got, keep)
        grad = jnp.concatenate([low_half, high_half], axis=1) + jnp.concatenate([column] * 4, axis=1) * total
        momentum, weight, average = nesterov(weight_ref[k], momentum_ref[k], grad, CONV_RATE, average_ref[k])
        grad_ref[k] = grad
        momentum_new_ref[k] = momentum
        weight_new_ref[k] = weight
        average_new_ref[k] = average
        low_ref[k] = weight.astype(BF16)


def relay_kernel(in_ref, out_ref):
    out_ref[...] = jnp.broadcast_to(jnp.sum(in_ref[...], 0)[None], out_ref.shape)


def small_kernel(
    last_ref, g4_ref, g5_ref, norm_ref, norm_momentum_ref, norm_average_ref, head_ref, head_momentum_ref, head_average_ref, *out_refs
):
    norm_grads = jnp.concatenate(gathered_rows(g5_ref, 2) + gathered_rows(g4_ref, 2), axis=0)
    rows, cols = head_ref.shape
    head_grads = jnp.sum(last_ref[...], 0)[:rows, :cols]
    values = (norm_grads,) + nesterov(norm_ref[...], norm_momentum_ref[...], norm_grads, NORM_RATE, norm_average_ref[...])
    values += (head_grads,) + nesterov(head_ref[...], head_momentum_ref[...], head_grads, HEAD_RATE, head_average_ref[...])
    for ref, value in zip(out_refs, values):
        ref[...] = value


def swap(value, even_mask, odd_mask):
    count = lax.axis_size(AXES)
    pairs = [(i, i ^ (odd_mask if i % 2 else even_mask)) for i in range(count)]
    return lax.ppermute(value, AXES, pairs)


CORE, ALONG_X, ALONG_Y, ALONG_Z = 1, 2, 4, 8
SQUARE = [(ALONG_X, ALONG_Y), (ALONG_Y, ALONG_X)]


def flat_index():
    return lax.axis_index("dp") * lax.axis_size("task") + lax.axis_index("task")


def along_line(shard):
    return jnp.stack([shard] + [swap(shard, m * ALONG_Z, m * ALONG_Z) for m in (1, 2, 3)])


def square_near(line):
    blocks = [line[:, :, :256], line[:, :, 256:]]
    return [jnp.concatenate([blocks[h], swap(blocks[h], *SQUARE[h])], 0) for h in (0, 1)]


def square_far(near):
    return [swap(near[h], *SQUARE[1 - h]) for h in (0, 1)]


def gather_pieces(shard, images, early, late_source, late):
    line = along_line(shard)
    line, images, early = lax.optimization_barrier((line, images, early))
    near = square_near(line)
    near, late_source = lax.optimization_barrier((near, late_source))
    far = square_far(near)
    sibling_near = [swap(v, CORE, CORE) for v in near]
    far, later = lax.optimization_barrier((far, late(late_source)))
    sibling_far = [swap(v, CORE, CORE) for v in far]
    pieces = [v[h] for h in (0, 1) for v in (near, far, sibling_near, sibling_far)]
    return pieces, images, early, later


def piece_places(rows):
    me = flat_index()
    core = me % 2
    owners = []
    part = jnp.arange(8, dtype=jnp.int32)
    for h in (0, 1):
        for base, which, is_far in ((me, core, 0), (me, core, 1), (me ^ CORE, 1 - core, 0), (me ^ CORE, 1 - core, 1)):
            x_first = which == h
            near_mask = jnp.where(x_first, ALONG_X, ALONG_Y)
            far_mask = jnp.where(x_first, ALONG_Y, ALONG_X)
            owners.append(base ^ (part % 4 * ALONG_Z) ^ (part // 4 * near_mask) ^ (is_far * far_mask))
    return jnp.concatenate(owners) * rows


def nesterov(params, momentum, grads, rate, average):
    momentum_new = MOMENTUM_DECAY * momentum + grads
    params_new = params - rate * (grads + MOMENTUM_DECAY * momentum_new)
    average_new = AVERAGE_DECAY * average + (1.0 - AVERAGE_DECAY) * params_new
    return (momentum_new, params_new, average_new)


VMEM = pl.BlockSpec(memory_space=pltpu.VMEM)
SCALAR = pl.BlockSpec(memory_space=pltpu.SMEM)
ANYWHERE = pl.BlockSpec(memory_space=pl.ANY)


def call(body, ins, outs, scratch=(), scalars=(), loose=(), flops=0, aliases=None, limit=12):
    kinds = {"vmem": (pltpu.VMEM, VMEM), "hbm": (pltpu.HBM, ANYWHERE), "free": (jax.ShapeDtypeStruct, VMEM)}
    out_shape = [kinds[k][0](d, t) for d, t, k in outs]
    moved = sum(a.size * a.dtype.itemsize for a in list(ins) + list(loose))
    return pl.pallas_call(
        body,
        in_specs=[SCALAR] * len(scalars) + [VMEM] * len(ins) + [ANYWHERE] * len(loose),
        out_specs=[kinds[k][1] for _, _, k in outs],
        out_shape=out_shape,
        scratch_shapes=list(scratch),
        input_output_aliases=aliases or {},
        compiler_params=pltpu.CompilerParams(vmem_limit_bytes=limit << 20),
        cost_estimate=pl.CostEstimate(flops=flops, bytes_accessed=moved, transcendentals=0),
    )(*scalars, *[pltpu.with_memory_space_constraint(a, pltpu.VMEM) for a in ins], *loose)


def exchange(replicated):
    return lax.all_to_all(replicated, AXES, 0, 0)


def on_device(
    images, image_counts, labels, fw_picks, task_average, conv_weights, conv_momentum, conv_average,
    norm_parameter_list, norm_momentum, norm_average, head_params, head_momentum, head_average,
):
    rows, map_side, channels = images.shape[0], images.shape[1], images.shape[3]
    width = map_side * map_side * channels
    devices = lax.axis_size(AXES)
    tasks = labels.shape[1]
    task_cols = head_params.shape[1]
    fw_steps = fw_picks.shape[0]
    matmul = 2 * rows * width * width
    tuned = (lax.axis_size("dp"), lax.axis_size("task"), channels) == (8, 4, 512)

    def stat(count):
        return ((devices, 1, count), F32, "free")

    slots = float(devices * rows * map_side * map_side)
    flat, flat_low = ((rows, width), F32, "vmem"), ((rows, width), BF16, "vmem")
    low = conv_weights.astype(BF16)

    def heads_and_labels(source):
        heads = lax.all_gather(source[0], "task", axis=1, tiled=True)
        return jnp.pad(heads, ((0, 7), (0, LANES - tasks))), jnp.pad(source[1], ((0, 0), (0, LANES - tasks)))

    flat_images = images.reshape(rows, width)
    start = jnp.pad(task_average[None, :], ((0, 7), (0, LANES - tasks)))
    basis = jnp.concatenate(
        [
            (jnp.arange(LANES, dtype=jnp.int32)[None, :] == fw_picks[:, None]).astype(F32),
            start[0:1],
            jnp.zeros((32 - fw_steps - 1, LANES), F32),
        ],
        axis=0,
    )

    me = flat_index()
    core = me & 1

    def bind(body, *static):
        return lambda *refs: body(*static, *refs)

    k2 = lax.all_gather(low[1], AXES, axis=0, tiled=True)
    if tuned:
        tall_low = (9 * channels, channels)
        chips = devices // 2
        at_x, at_y = me // ALONG_X & 1, me // ALONG_Y & 1
        index = jnp.arange(chips // 2, dtype=jnp.int32)
        by_x, by_y = index * 2, index // 2 * 4 + index % 2
        here = jnp.where(core == 0, by_x + at_x, by_y + 2 * at_y)
        there = jnp.where(core == 0, by_x + 1 - at_x, by_y + 2 * (1 - at_y))
        own = jnp.where(core == 0, at_y, at_x)
        index = jnp.arange(chips // 4, dtype=jnp.int32) * 2
        tables = (
            piece_places(low.shape[1]), jnp.concatenate([there, here]), jnp.concatenate([index + 1 - own, index + own]),
            (me // ALONG_Z)[None], core[None], me[None], image_counts + 0,
        )
        pieces, flat_images, (tables, start, basis), (heads, labels) = gather_pieces(
            low[0], flat_images, (tables, start, basis), (head_params, labels), heads_and_labels
        )
        places, chunk_table, pair_table, z_place, core_place, me_place, image_counts = tables
        first, stat1, k1 = call(
            first_gathered_kernel, [flat_images], [flat, stat(1152), (tall_low, BF16, "hbm")],
            [pltpu.VMEM(tall_low, BF16), pltpu.SemaphoreType.DMA, pltpu.SemaphoreType.DMA],
            (image_counts, places), pieces, matmul, limit=7,
        )
    else:
        heads, labels = heads_and_labels((head_params, labels))
        k1 = lax.all_gather(low[0], AXES, axis=0, tiled=True)
        first, stat1 = call(first_kernel, [flat_images, k1], [flat, stat(1152)], (), (image_counts,), (), matmul)
    if tuned:
        images_other = swap(flat_images, CORE, CORE)
        stat1, images_other = lax.optimization_barrier((stat1, images_other))
    else:
        core_place = core[None]
    g1 = exchange(stat1)
    hidden, second, stat2 = call(
        second_kernel, [first, g1, norm_parameter_list, k2], [flat_low, flat, stat(1024)], (), (image_counts,), (), matmul, limit=5
    )
    g2 = exchange(stat2)
    if tuned:
        g2, moved_hidden = lax.optimization_barrier((g2, hidden))
        hidden_other = swap(moved_hidden, CORE, CORE)
    per_channel = ((rows, channels), F32, "vmem")
    block_flat, slope, slope_sum, slope_xhat, pooled, resid, gram = call(
        bind(head_kernel, tasks), [second, g2, g1, norm_parameter_list, flat_images, labels, heads, basis],
        [flat_low, flat, per_channel, per_channel, ((rows, channels + LANES), F32, "vmem"), ((rows, LANES), F32, "vmem"), stat(1024)],
        (), (image_counts,), (), matmul, limit=3,
    )
    if tuned:
        gram, hidden_other = lax.optimization_barrier((gram, hidden_other))
    g3 = exchange(gram)
    dout, stat4, head_send, mix = call(
        bind(mix_kernel, fw_steps), [g3, basis, start, resid, pooled, heads, slope_sum, slope_xhat],
        [per_channel, stat(1024), ((tasks // task_cols, task_cols, channels + LANES), F32, "free"), ((8, LANES), F32, "free")],
        (), (), (), matmul // 2, limit=3,
    )
    g4 = exchange(stat4)
    part = channels // 2
    shard_rows = conv_weights.shape[1]
    sent = [((rows, width // 2), BF16, "vmem")] * 2 if tuned else [flat_low]
    ways = tasks // task_cols
    sums = ((ways, 4, channels + LANES), F32, "free")
    dnormed, stat5, sums_two, dpre, *dsecond_halves = call(
        back_second_kernel, [slope, dout, second, first, g1, g2, g4, norm_parameter_list, k2],
        [flat, stat(1024), sums, flat_low] + sent, [pltpu.VMEM((TILE, width), BF16)], (image_counts, core_place), (), matmul, {4: 0}, limit=8,
    )
    g5 = exchange(stat5)
    if tuned:
        g5, *dsecond_halves = lax.optimization_barrier((g5, *dsecond_halves))
        dsecond_other = swap(dsecond_halves[1], CORE, CORE)
    dfirst, sums_one, *dfirst_halves = call(
        dfirst_kernel, [dnormed, first, g1, g5, norm_parameter_list],
        [flat_low, sums] + (sent if tuned else []), (), (image_counts, core_place), (), matmul // 4, limit=6,
    )

    def combine(keep, got, table):
        dims = (keep.shape[0] // 2,) + keep.shape[1:]
        return call(combine_kernel, [keep, got], [(dims, BF16, "free"), (dims, F32, "vmem")], (), (table,), limit=5)

    def scatter_start(x, x_other, d, d_other, mean_of, source):
        dims = (devices // 4, 2 * shard_rows, part)
        return call(
            bind(pair_weight_grad_kernel, mean_of), [x, d, source, x_other, d_other],
            [(dims, BF16, "free"), (dims, F32, "vmem")], [pltpu.VMEM((9 * channels, part), F32)],
            (chunk_table,), (), matmul, limit=18,
        )

    def scatter_next(send, keep):
        return combine(keep, swap(send, *SQUARE[0]), pair_table)

    def scatter_line(got, keep):
        pair = keep.shape[1:]
        return call(line_kernel, [keep, got], [(pair, F32, "vmem")] + [(pair, BF16, "free")] * 3, (), (z_place,), limit=3)

    def scatter_finish(own, sent):
        half = ((shard_rows, part), F32, "free")
        send, keep = call(line_sum_kernel, [own] + sent, [half, half], (), (core_place,), limit=3)
        return keep, swap(send, CORE, CORE)

    def scatter_whole(x, d):
        (whole,) = call(weight_grad_kernel, [x, d], [((9 * channels, channels), F32, "free")], (), (), (), matmul)
        return lax.psum_scatter(whole, AXES, scatter_dimension=0, tiled=True)

    def share_task(*values):
        over_task = lax.all_to_all(jnp.concatenate(values, axis=1), "task", 0, 0)
        dims = (lax.axis_size("dp"),) + over_task.shape[1:]
        return call(relay_kernel, [over_task], [(dims, F32, "free")], limit=4)[0]

    def share_dp(over_dp):
        return lax.all_to_all(over_dp, "dp", 0, 0)

    def image_gradient(begin, end, late, buffer=()):
        return call(
            bind(image_grad_kernel, begin, end), [late, k1, dpre], [(images.shape, F32, "hbm")],
            [pltpu.VMEM((2, TILE) + images.shape[1:], F32), pltpu.SemaphoreType.DMA((2,))], (), buffer, matmul * (end - begin) // rows,
            {3: 0} if buffer else None, limit=6,
        )[0]

    if tuned:
        dfirst_other = swap(dfirst_halves[1], CORE, CORE)
        dsecond_own, dsecond_other, hidden, hidden_other, dfirst = lax.optimization_barrier(
            (dsecond_halves[0], dsecond_other, hidden, hidden_other, dfirst)
        )
        two = scatter_start(hidden, hidden_other, dsecond_own, dsecond_other, hidden_mean, norm_parameter_list)
        send_two, flat_images, images_other, dfirst_own = lax.optimization_barrier((two[0], flat_images, images_other, dfirst_halves[0]))
        one = scatter_start(flat_images, images_other, dfirst_own, dfirst_other, bind(image_mean, slots), g3)
        send_one, keep_two = lax.optimization_barrier((one[0], two[1]))
        send_two, keep_two = scatter_next(send_two, keep_two)
        got_two = swap(send_two, *SQUARE[1])
        send_two, late = lax.optimization_barrier((send_two, dfirst))
        image_part = image_gradient(0, rows // 2, late)
        image_part, head_send, sums_two, sums_one = lax.optimization_barrier((image_part, head_send, sums_two, sums_one))
        shared = share_task(head_send, sums_two, sums_one)
        got_two, image_part, shared = lax.optimization_barrier((got_two, image_part, shared))
        line_two = scatter_line(got_two, keep_two)
        sent_two = [swap(line_two[m], m * ALONG_Z, m * ALONG_Z) for m in (1, 2, 3)]
        line_first, late, image_part = lax.optimization_barrier((line_two[1], late, image_part))
        image_grad = image_gradient(rows // 2, rows, late, (image_part,))
        keep_one, image_grad = lax.optimization_barrier((one[1], image_grad))
        send_one, keep_one = scatter_next(send_one, keep_one)
        got_one = swap(send_one, *SQUARE[1])
        send_one, block_flat = lax.optimization_barrier((send_one, block_flat))
        block_output = block_flat.reshape(images.shape)
        got_one, block_output, sent_two = lax.optimization_barrier((got_one, block_output, sent_two))
        line_one = scatter_line(got_one, keep_one)
        sent_one = [swap(line_one[m], m * ALONG_Z, m * ALONG_Z) for m in (1, 2, 3)]
        line_first, shared = lax.optimization_barrier((line_one[1], shared))
        last = share_dp(shared)
        last, sent_one = lax.optimization_barrier((last, sent_one))
        shards = conv_weights.shape
        outs = [(shards, F32, "free")] * 4 + [(shards, BF16, "free")]
        conv_grads, conv_momentum_new, conv_weights_new, conv_average_new, conv_weights_low = call(
            bind(finish_kernel, slots),
            list(scatter_finish(line_one[0], sent_one)) + list(scatter_finish(line_two[0], sent_two))
            + [g3, norm_parameter_list, last, conv_weights, conv_momentum, conv_average],
            outs, [pltpu.VMEM((1024, LANES), F32), pltpu.VMEM((16, channels), F32)], (me_place,), limit=5,
        )
    else:
        last = share_dp(share_task(head_send, sums_two, sums_one))
        grad_two = scatter_whole(hidden, dsecond_halves[0])
        grad_one = scatter_whole(flat_images, dfirst)
        image_grad = image_gradient(0, rows, dfirst)
        block_output = block_flat.reshape(images.shape)
        conv_grads = jnp.stack([grad_one, grad_two])
        conv_momentum_new, conv_weights_new, conv_average_new = nesterov(conv_weights, conv_momentum, conv_grads, CONV_RATE, conv_average)
        conv_weights_low = conv_weights_new.astype(BF16)
    head_dims = (head_params.shape[1], head_params.shape[0])
    norm_grads, norm_momentum_new, norm_params_new, norm_average_new, *head_new = call(
        small_kernel,
        [last, g4, g5, norm_parameter_list, norm_momentum, norm_average, head_params.T, head_momentum.T, head_average.T],
        [(norm_momentum.shape, F32, "free")] * 4 + [(head_dims, F32, "free")] * 4, limit=4,
    )
    head_grads, head_momentum_new, head_params_new, head_average_new = [value.T for value in head_new]
    task_average_new = AVERAGE_DECAY * task_average + (1.0 - AVERAGE_DECAY) * mix[0, :tasks]
    return (
        block_output,
        image_grad,
        conv_grads,
        conv_momentum_new,
        conv_weights_new,
        conv_average_new,
        conv_weights_low,
        norm_grads,
        norm_momentum_new,
        norm_params_new,
        norm_average_new,
        head_grads,
        head_momentum_new,
        head_params_new,
        head_average_new,
        task_average_new,
    )


def solution(mesh):
    both = P(AXES)
    rowwise = P(None, AXES, None)
    head = P(None, "task")
    return jax.shard_map(
        on_device,
        mesh=mesh,
        in_specs=(both, both, both, P(), P(), rowwise, rowwise, rowwise, P(), P(), P(), head, head, head),
        out_specs=(both, both, rowwise, rowwise, rowwise, rowwise, rowwise, P(), P(), P(), P(), head, head, head, head, P()),
        check_vma=False,
    )
```

```python
import jax
import jax.numpy as jnp
import numpy as np
from jax import lax
from jax.experimental import pallas as pl
from jax.experimental.pallas import tpu as pltpu
from jax.sharding import PartitionSpec as P

EPSILON = 1e-05
MOMENTUM_DECAY = 0.5
AVERAGE_DECAY = 0.5
CONV_RATE = 2000.0
NORM_RATE = 40000.0
HEAD_RATE = 1000.0
STEP_CAP = 0.5
GROUP = 21
GELU_A = 0.7978845608
GELU_B = 0.7978845608 * 0.044715
AXES = ("dp", "task")
PRECISE = lax.Precision.HIGHEST
F32 = jnp.float32
BF16 = jnp.bfloat16
TILE = 256
CONV_TILE = 512
LANES = 128


def tap(q, p):
    return (q // 2 - p // 2 + 1) * 3 + (q % 2 - p % 2 + 1)


def dot(a, b):
    return jnp.dot(a, b, preferred_element_type=F32)


def dot_nt(a, b):
    return lax.dot_general(a, b, (((1,), (1,)), ((), ())), preferred_element_type=F32)


def dot_tn(a, b):
    return lax.dot_general(a, b, (((0,), (0,)), ((), ())), preferred_element_type=F32)


def precise(a, b, dims):
    return lax.dot_general(a, b, ((dims[0], dims[1]), ((), ())), precision=PRECISE, preferred_element_type=F32)


def fold8(v):
    return jnp.sum(v.reshape(v.shape[0] // 8, 8, v.shape[1]), 0)


def spread_rows(out_ref, rows):
    row = jnp.concatenate(rows, axis=1)
    out_ref[...] = jnp.broadcast_to(row[None], (out_ref.shape[0], 1, row.shape[1]))


def gathered_rows(ref, count):
    total = jnp.sum(ref[...], 0)
    return [total[:, r * 512 : (r + 1) * 512] for r in range(count)]


def moments(gathered_ref, spatial):
    value_sum, square_sum = gathered_rows(gathered_ref, 2)
    mean = value_sum / spatial
    inverse = lax.rsqrt(square_sum / spatial - mean * mean + EPSILON)
    return mean, inverse


def images_total(g1_ref):
    return jnp.sum(g1_ref[:, :, 1024:1152], 0)[:, 0:1]


def real_mask(count, start, rows):
    index = lax.broadcasted_iota(jnp.int32, (rows, 1), 0) + start
    return (index < count).astype(F32)


def plus(total, value):
    return value if total is None else total + value


def column_sums(values):
    return [jnp.sum(v, 0, keepdims=True) for v in values]


def conv_tile(x_ref, k_ref, out_ref, start, size, mask, total, square):
    rows = slice(start, start + size)
    for p in range(4):
        pr, pc = p // 2, p % 2
        acc = None
        for qr in range(2):
            base = ((qr - pr + 1) * 3 + (1 - pc)) * 512
            acc = plus(acc, dot(x_ref[rows, qr * 1024 : (qr + 1) * 1024], k_ref[base : base + 1024, :]))
        out_ref[rows, p * 512 : (p + 1) * 512] = acc
        masked = acc * mask
        total = plus(total, fold8(masked))
        square = plus(square, fold8(masked * acc))
    return total, square


def first_kernel(count_ref, x_ref, k_ref, first_ref, stat_ref):
    count = count_ref[0]
    total = square = None
    for start in range(0, x_ref.shape[0], CONV_TILE):
        mask = real_mask(count, start, CONV_TILE)
        total, square = conv_tile(x_ref, k_ref, first_ref, start, CONV_TILE, mask, total, square)
    spread_rows(stat_ref, column_sums((total, square)) + [jnp.full((1, LANES), count.astype(F32), F32)])


def load_pieces(place_ref, pieces, k_ref, load_sem):
    rows = pieces[0].shape[1]
    for n, piece in enumerate(pieces):
        cols = pl.ds((n // 4) * 256, 256)
        for i in range(piece.shape[0]):
            place = pl.multiple_of(place_ref[n * piece.shape[0] + i], 16)
            pltpu.make_async_copy(piece.at[i], k_ref.at[pl.ds(place, rows), cols], load_sem).start()
    pltpu.make_async_copy(k_ref, k_ref, load_sem).wait()


def first_gathered_kernel(count_ref, place_ref, x_ref, *refs):
    pieces, (first_ref, stat_ref, k_out_ref, k_ref, load_sem, store_sem) = refs[:8], refs[8:]
    load_pieces(place_ref, pieces, k_ref, load_sem)
    store = pltpu.make_async_copy(k_ref, k_out_ref, store_sem)
    store.start()
    first_kernel(count_ref, x_ref, k_ref, first_ref, stat_ref)
    store.wait()


def gelu_gate(v):
    return 0.5 * jnp.tanh(v * (GELU_A + GELU_B * (v * v))) + 0.5


def gelu_slope(v, gate):
    inner = v * (2.0 * GELU_A + (6.0 * GELU_B) * (v * v))
    return gate + gate * (inner - inner * gate)


def second_kernel(count_ref, first_ref, g1_ref, norm_ref, k_ref, hidden_ref, second_ref, stat_ref):
    mean, inverse = moments(g1_ref, images_total(g1_ref) * 4.0)
    scale = norm_ref[0:1, :] * inverse
    shift = norm_ref[1:2, :] - mean * scale
    total = square = None
    for start in range(0, first_ref.shape[0], CONV_TILE):
        rows = slice(start, start + CONV_TILE)
        for p in range(4):
            v = first_ref[rows, p * 512 : (p + 1) * 512] * scale + shift
            hidden_ref[rows, p * 512 : (p + 1) * 512] = (v * gelu_gate(v)).astype(BF16)
        mask = real_mask(count_ref[0], start, CONV_TILE)
        total, square = conv_tile(hidden_ref, k_ref, second_ref, start, CONV_TILE, mask, total, square)
    spread_rows(stat_ref, column_sums((total, square)))


def head_kernel(
    tasks, count_ref, second_ref, g2_ref, g1_ref, norm_ref, image_ref, label_ref, head_ref, pick_ref,
    out_ref, slope_ref, slope_sum_ref, slope_xhat_ref, pooled_ref, resid_ref, gram_out_ref,
):
    real_total = images_total(g1_ref)
    mean, inverse = moments(g2_ref, real_total * 4.0)
    gain, shift = norm_ref[2:3, :], norm_ref[3:4, :]
    lane_real = (lax.broadcasted_iota(jnp.int32, (1, LANES), 1) < tasks).astype(F32)
    gram = image_sum = None
    for start in range(0, second_ref.shape[0], TILE):
        rows = slice(start, start + TILE)
        pooled = slope_sum = slope_xhat = None
        for p in range(4):
            cols = slice(p * 512, (p + 1) * 512)
            xhat = (second_ref[rows, cols] - mean) * inverse
            image = image_ref[rows, cols].astype(F32)
            image_sum = plus(image_sum, fold8(image))
            pre = gain * xhat + shift + image
            gate = gelu_gate(pre)
            out = pre * gate
            out_ref[rows, cols] = out.astype(BF16)
            slope = gelu_slope(pre, gate)
            slope_ref[rows, cols] = slope
            pooled = plus(pooled, out)
            slope_sum = plus(slope_sum, slope)
            slope_xhat = plus(slope_xhat, slope * xhat)
        pooled = pooled * 0.25
        slope_sum_ref[rows, :] = slope_sum
        slope_xhat_ref[rows, :] = slope_xhat
        pooled_ref[rows, 0:512] = pooled
        pooled_ref[rows, 512:640] = (lax.broadcasted_iota(jnp.int32, (TILE, LANES), 1) == 0).astype(F32)
        logits = precise(pooled, head_ref[0:512, :], ((1,), (0,))) + head_ref[512:513, :]
        mask = real_mask(count_ref[0], start, TILE) * lane_real
        resid = mask * (jax.nn.sigmoid(logits) - label_ref[rows, :].astype(F32)) / real_total
        resid_ref[rows, :] = resid
        gram = plus(gram, precise(resid, resid, ((0,), (0,))))
    heads = head_ref[0:512, :]
    gram = gram * precise(heads, heads, ((0,), (0,)))
    basis = pick_ref[...]
    projected = precise(gram, basis, ((1,), (1,)))
    lane = lax.broadcasted_iota(jnp.int32, (32, LANES), 1)
    row = lax.broadcasted_iota(jnp.int32, (32, LANES), 0)
    packed = None
    for group in range(6):
        placed = precise(projected, ((lane == row + GROUP * group) & (row < GROUP)).astype(F32), ((1,), (0,)))
        packed = plus(packed, precise(basis[4 * group : 4 * group + 4, :], placed, ((1,), (0,))))
    spread_rows(gram_out_ref, [packed[r : r + 1, :] for r in range(4)] + column_sums((image_sum,)))


def frank_wolfe(packed, picks, start_mix, fw_steps):
    rows = jnp.concatenate([packed[:, GROUP * g : GROUP * (g + 1)] for g in range(6)], axis=0)
    column = [jnp.broadcast_to(rows[:, k : k + 1], (24, LANES)) for k in range(fw_steps + 1)]
    along = column[fw_steps]
    a = along[fw_steps : fw_steps + 1, :]
    mix = start_mix
    for k in range(fw_steps):
        b = along[k : k + 1, :]
        c = column[k][k : k + 1, :]
        size = jnp.clip((a - b) / (a - 2.0 * b + c), 0.0, STEP_CAP)
        keep = 1.0 - size
        a = keep * keep * a + 2.0 * (keep * size) * b + size * size * c
        along = keep * along + size * column[k]
        mix = keep * mix + size * picks[k : k + 1, :]
    return mix


def mix_kernel(
    fw_steps, gram_ref, pick_ref, start_ref, resid_ref, pooled_ref, head_ref, slope_sum_ref, slope_xhat_ref,
    dout_ref, stat_ref, head_grad_ref, mix_ref,
):
    (total,) = gathered_rows(gram_ref, 1)
    packed = jnp.concatenate([total[:, r * LANES : (r + 1) * LANES] for r in range(4)], axis=0)
    mix = frank_wolfe(packed, pick_ref[...], start_ref[0:1, :], fw_steps)
    mix_ref[...] = jnp.broadcast_to(mix, mix_ref.shape)
    gain_sum = shift_sum = head_grad = None
    for start in range(0, resid_ref.shape[0], TILE):
        rows = slice(start, start + TILE)
        weighted = resid_ref[rows, :] * mix
        dout = precise(weighted, head_ref[0:512, :], ((1,), (1,))) * 0.25
        dout_ref[rows, :] = dout
        head_grad = plus(head_grad, precise(weighted, pooled_ref[rows, :], ((0,), (0,))))
        gain_sum = plus(gain_sum, fold8(dout * slope_xhat_ref[rows, :]))
        shift_sum = plus(shift_sum, fold8(dout * slope_sum_ref[rows, :]))
    spread_rows(stat_ref, column_sums((gain_sum, shift_sum)))
    ways, width = head_grad_ref.shape[0], head_grad.shape[1]
    cols = head_grad_ref.shape[2] // width
    for way in range(ways):
        rows = [head_grad[way * cols + i : way * cols + i + 1, :] for i in range(cols)]
        head_grad_ref[way] = jnp.concatenate(rows, axis=1)


def store_sums(sum_ref, sums):
    spread_rows(sum_ref, column_sums(sums))


def split_halves(core, grad, half_refs, rows, p):
    if len(half_refs) == 1:
        half_refs[0][rows, p * grad.shape[1] : (p + 1) * grad.shape[1]] = grad
    else:
        half = grad.shape[1] // 2
        low, high = grad[:, :half], grad[:, half:]
        own_ref, send_ref = half_refs
        own_ref[rows, p * half : (p + 1) * half] = jnp.where(core == 0, low, high)
        send_ref[rows, p * half : (p + 1) * half] = jnp.where(core == 0, high, low)


def back_second_kernel(
    count_ref, core_ref, slope_ref, dout_ref, second_ref, first_ref, g1_ref, g2_ref, g4_ref, norm_ref, k_ref,
    dnormed_ref, stat_ref, sum_ref, dpre_ref, *half_refs,
):
    spatial = images_total(g1_ref) * 4.0
    mean1, inverse1 = moments(g1_ref, spatial)
    mean2, inverse2 = moments(g2_ref, spatial)
    gain_grad, shift_grad = gathered_rows(g4_ref, 2)
    scale2 = norm_ref[2:3, :] * inverse2
    by_value = scale2 * gain_grad * inverse2 / spatial
    by_one = scale2 * shift_grad / spatial - by_value * mean2
    gain1, shift1 = norm_ref[0:1, :], norm_ref[1:2, :]
    gain_sum = shift_sum = None
    sums = [None] * 4
    *half_refs, dsecond_ref = half_refs
    for start in range(0, second_ref.shape[0], TILE):
        rows = slice(start, start + TILE)
        mask = real_mask(count_ref[0], start, TILE)
        dout = dout_ref[rows, :]
        for p in range(4):
            cols = slice(p * 512, (p + 1) * 512)
            dpre = dout * slope_ref[rows, cols]
            dpre_ref[rows, cols] = dpre.astype(BF16)
            grad = (scale2 * dpre - mask * (by_one + by_value * second_ref[rows, cols])).astype(BF16)
            dsecond_ref[:, cols] = grad
            split_halves(core_ref[0], grad, half_refs, rows, p)
            sums[p] = plus(sums[p], fold8(grad.astype(F32)))
        for q in range(4):
            cols = slice(q * 512, (q + 1) * 512)
            acc = None
            for p in range(4):
                base = tap(q, p) * 512
                acc = plus(acc, dot_nt(dsecond_ref[:, p * 512 : (p + 1) * 512], k_ref[base : base + 512, :]))
            xhat = (first_ref[rows, cols] - mean1) * inverse1
            v = gain1 * xhat + shift1
            dnormed = acc * gelu_slope(v, gelu_gate(v))
            dnormed_ref[rows, cols] = dnormed
            gain_sum = plus(gain_sum, fold8(dnormed * xhat))
            shift_sum = plus(shift_sum, fold8(dnormed))
    spread_rows(stat_ref, column_sums((gain_sum, shift_sum)))
    store_sums(sum_ref, sums)


def taps_of(index):
    return [(q, p) for q in range(4) for p in range(4) if tap(q, p) == index]


def weight_grad_kernel(x_ref, d_ref, out_ref):
    for index in range(9):
        acc = None
        for q, p in taps_of(index):
            acc = plus(acc, dot_tn(x_ref[:, q * 512 : (q + 1) * 512], d_ref[:, p * 512 : (p + 1) * 512]))
        out_ref[index * 512 : (index + 1) * 512, :] = acc


def as_column(row):
    return jnp.transpose(jnp.broadcast_to(row, (LANES, row.shape[1])))


def image_mean(slots, g3_ref):
    return gathered_rows(g3_ref, 2)[1] * (1.0 / slots)


def hidden_mean(norm_ref):
    nodes, weights = np.polynomial.hermite_e.hermegauss(9)
    total = None
    for node, weight in zip(nodes, weights / weights.sum()):
        v = norm_ref[0:1, :] * float(node) + norm_ref[1:2, :]
        total = plus(total, float(weight) * (v * gelu_gate(v)))
    return total


def pair_weight_grad_kernel(mean_of, table_ref, x_ref, d_ref, mean_ref, x_other_ref, d_other_ref, send_ref, keep_ref, whole_ref):
    width = whole_ref.shape[1]
    column = as_column(mean_of(mean_ref))
    column = jnp.concatenate([column] * (width // LANES), axis=1)
    sums = []
    for p in range(4):
        cols = slice(p * width, (p + 1) * width)
        sums.append(jnp.sum(fold8(d_ref[:, cols].astype(F32)) + fold8(d_other_ref[:, cols].astype(F32)), 0, keepdims=True))
    seen = set()
    for q in range(4):
        acc = dot_tn(x_ref[:, q * 512 : (q + 1) * 512], d_ref[...])
        acc = acc + dot_tn(x_other_ref[:, q * 512 : (q + 1) * 512], d_other_ref[...])
        for p in range(4):
            index = tap(q, p)
            rows = slice(index * 512, (index + 1) * 512)
            part = acc[:, p * width : (p + 1) * width] - column * sums[p]
            whole_ref[rows, :] = whole_ref[rows, :] + part if index in seen else part
            seen.add(index)
    count, rows = keep_ref.shape[0], keep_ref.shape[1]
    for i in range(count):
        there = pl.ds(pl.multiple_of(table_ref[i] * rows, 16), rows)
        here = pl.ds(pl.multiple_of(table_ref[count + i] * rows, 16), rows)
        send_ref[i] = whole_ref[there, :].astype(BF16)
        keep_ref[i] = whole_ref[here, :]


def dfirst_kernel(count_ref, core_ref, dnormed_ref, first_ref, g1_ref, g5_ref, norm_ref, dfirst_ref, stat_ref, *half_refs):
    spatial = images_total(g1_ref) * 4.0
    mean1, inverse1 = moments(g1_ref, spatial)
    gain_grad, shift_grad = gathered_rows(g5_ref, 2)
    scale = norm_ref[0:1, :] * inverse1
    by_value = scale * gain_grad * inverse1 / spatial
    by_one = scale * shift_grad / spatial - by_value * mean1
    sums = [None] * 4
    for start in range(0, first_ref.shape[0], TILE):
        rows = slice(start, start + TILE)
        mask = real_mask(count_ref[0], start, TILE)
        for p in range(4):
            cols = slice(p * 512, (p + 1) * 512)
            grad = (scale * dnormed_ref[rows, cols] - mask * (by_one + by_value * first_ref[rows, cols])).astype(BF16)
            dfirst_ref[rows, cols] = grad
            if half_refs:
                split_halves(core_ref[0], grad, half_refs, rows, p)
            sums[p] = plus(sums[p], fold8(grad.astype(F32)))
    store_sums(stat_ref, sums)


def image_grad_kernel(begin, end, dfirst_ref, k_ref, dpre_ref, *refs):
    out_ref, buffer_ref, sem = refs[-3:]
    copies = []
    for n, start in enumerate(range(begin, end, TILE)):
        rows = slice(start, start + TILE)
        slot = n % 2
        if n >= 2:
            copies[n - 2].wait()
        for q in range(4):
            cols = slice(q * 512, (q + 1) * 512)
            acc = dpre_ref[rows, cols].astype(F32)
            for p in range(4):
                base = tap(q, p) * 512
                acc = acc + dot_nt(dfirst_ref[rows, p * 512 : (p + 1) * 512], k_ref[base : base + 512, :])
            buffer_ref[slot, :, q // 2, q % 2, :] = acc
        copies.append(pltpu.make_async_copy(buffer_ref.at[slot], out_ref.at[pl.ds(start, TILE)], sem.at[slot]))
        copies[n].start()
    for copy in copies[-2:]:
        copy.wait()


def combine_kernel(table_ref, keep_ref, got_ref, send_ref, out_ref):
    count = out_ref.shape[0]
    for i in range(count):
        there, here = table_ref[i], table_ref[count + i]
        send_ref[i] = (keep_ref[there] + got_ref[there].astype(F32)).astype(BF16)
        out_ref[i] = keep_ref[here] + got_ref[here].astype(F32)


def line_kernel(z_ref, keep_ref, got_ref, *out_refs):
    for mask, ref in enumerate(out_refs):
        place = z_ref[0] ^ mask
        ref[...] = (keep_ref[place] + got_ref[place].astype(F32)).astype(ref.dtype)


def line_sum_kernel(core_ref, keep_ref, got1_ref, got2_ref, got3_ref, send_ref, out_ref):
    half = out_ref.shape[0]
    for ref, place in ((send_ref, 1 - core_ref[0]), (out_ref, core_ref[0])):
        rows = pl.ds(pl.multiple_of(place * half, 16), half)
        got = got1_ref[rows, :].astype(F32) + got2_ref[rows, :].astype(F32) + got3_ref[rows, :].astype(F32)
        ref[...] = keep_ref[rows, :] + got


def finish_kernel(
    slots, me_ref, keep1_ref, got1_ref, keep2_ref, got2_ref, g3_ref, norm_ref, last_ref, weight_ref, momentum_ref, average_ref,
    grad_ref, momentum_new_ref, weight_new_ref, average_new_ref, low_ref, column_ref, sums_ref,
):
    core, start = me_ref[0] % 2, me_ref[0] * grad_ref.shape[1]
    rows = grad_ref.shape[1]
    index = lax.broadcasted_iota(jnp.int32, (rows, 1), 0) + start % 512
    last = jnp.sum(last_ref[...], 0)
    begin = last.shape[1] - 8 * 512
    sums = [last[:, begin + p * 512 : begin + (p + 1) * 512] for p in range(8)]
    sources = (
        (keep1_ref, got1_ref, image_mean(slots, g3_ref), sums[4:]),
        (keep2_ref, got2_ref, hidden_mean(norm_ref), sums[:4]),
    )
    for k, (keep_ref, got_ref, mean, sums) in enumerate(sources):
        column = as_column(mean)
        column_ref[0:512, :] = column
        column_ref[512:1024, :] = column
        for tap_index in range(9):
            total = None
            for _, p in taps_of(tap_index):
                total = plus(total, sums[p])
            sums_ref[tap_index : tap_index + 1, :] = total
        column = column_ref[pl.ds(pl.multiple_of(start % 512, 16), rows), :]
        first_tap = start // 512
        total = jnp.where(index < 512, sums_ref[pl.ds(first_tap, 1), :], sums_ref[pl.ds(jnp.minimum(first_tap + 1, 8), 1), :])
        keep, got = keep_ref[...], got_ref[...]
        low_half, high_half = jnp.where(core == 0, keep, got), jnp.where(core == 0, got, keep)
        grad = jnp.concatenate([low_half, high_half], axis=1) + jnp.concatenate([column] * 4, axis=1) * total
        momentum, weight, average = nesterov(weight_ref[k], momentum_ref[k], grad, CONV_RATE, average_ref[k])
        grad_ref[k] = grad
        momentum_new_ref[k] = momentum
        weight_new_ref[k] = weight
        average_new_ref[k] = average
        low_ref[k] = weight.astype(BF16)


def relay_kernel(in_ref, out_ref):
    out_ref[...] = jnp.broadcast_to(jnp.sum(in_ref[...], 0)[None], out_ref.shape)


def small_kernel(
    last_ref, g4_ref, g5_ref, norm_ref, norm_momentum_ref, norm_average_ref, head_ref, head_momentum_ref, head_average_ref, *out_refs
):
    norm_grads = jnp.concatenate(gathered_rows(g5_ref, 2) + gathered_rows(g4_ref, 2), axis=0)
    rows, cols = head_ref.shape
    last = jnp.sum(last_ref[...], 0)
    head_grads = jnp.concatenate([last[:, i * 640 : (i + 1) * 640] for i in range(rows)], axis=0)[:, :cols]
    values = (norm_grads,) + nesterov(norm_ref[...], norm_momentum_ref[...], norm_grads, NORM_RATE, norm_average_ref[...])
    values += (head_grads,) + nesterov(head_ref[...], head_momentum_ref[...], head_grads, HEAD_RATE, head_average_ref[...])
    for ref, value in zip(out_refs, values):
        ref[...] = value


def swap(value, even_mask, odd_mask):
    count = lax.axis_size(AXES)
    pairs = [(i, i ^ (odd_mask if i % 2 else even_mask)) for i in range(count)]
    return lax.ppermute(value, AXES, pairs)


CORE, ALONG_X, ALONG_Y, ALONG_Z = 1, 2, 4, 8
SQUARE = [(ALONG_X, ALONG_Y), (ALONG_Y, ALONG_X)]


def flat_index():
    return lax.axis_index("dp") * lax.axis_size("task") + lax.axis_index("task")


def along_line(shard):
    return jnp.stack([shard] + [swap(shard, m * ALONG_Z, m * ALONG_Z) for m in (1, 2, 3)])


def square_near(line):
    blocks = [line[:, :, :256], line[:, :, 256:]]
    return [jnp.concatenate([blocks[h], swap(blocks[h], *SQUARE[h])], 0) for h in (0, 1)]


def square_far(near):
    return [swap(near[h], *SQUARE[1 - h]) for h in (0, 1)]


def gather_pieces(shard, images, early, later):
    line = along_line(shard)
    line, images, early = lax.optimization_barrier((line, images, early))
    near = square_near(line)
    near, later = lax.optimization_barrier((near, later))
    far = square_far(near)
    sibling_near = [swap(v, CORE, CORE) for v in near]
    sibling_far = [swap(v, CORE, CORE) for v in far]
    pieces = [v[h] for h in (0, 1) for v in (near, far, sibling_near, sibling_far)]
    return pieces, images, early, later


def piece_places(rows):
    me = flat_index()
    core = me % 2
    owners = []
    part = jnp.arange(8, dtype=jnp.int32)
    for h in (0, 1):
        for base, which, is_far in ((me, core, 0), (me, core, 1), (me ^ CORE, 1 - core, 0), (me ^ CORE, 1 - core, 1)):
            x_first = which == h
            near_mask = jnp.where(x_first, ALONG_X, ALONG_Y)
            far_mask = jnp.where(x_first, ALONG_Y, ALONG_X)
            owners.append(base ^ (part % 4 * ALONG_Z) ^ (part // 4 * near_mask) ^ (is_far * far_mask))
    return jnp.concatenate(owners) * rows


def nesterov(params, momentum, grads, rate, average):
    momentum_new = MOMENTUM_DECAY * momentum + grads
    params_new = params - rate * (grads + MOMENTUM_DECAY * momentum_new)
    average_new = AVERAGE_DECAY * average + (1.0 - AVERAGE_DECAY) * params_new
    return (momentum_new, params_new, average_new)


VMEM = pl.BlockSpec(memory_space=pltpu.VMEM)
SCALAR = pl.BlockSpec(memory_space=pltpu.SMEM)
ANYWHERE = pl.BlockSpec(memory_space=pl.ANY)


def call(body, ins, outs, scratch=(), scalars=(), loose=(), flops=0, aliases=None, limit=12):
    kinds = {"vmem": (pltpu.VMEM, VMEM), "hbm": (pltpu.HBM, ANYWHERE), "free": (jax.ShapeDtypeStruct, VMEM)}
    out_shape = [kinds[k][0](d, t) for d, t, k in outs]
    moved = sum(a.size * a.dtype.itemsize for a in list(ins) + list(loose))
    return pl.pallas_call(
        body,
        in_specs=[SCALAR] * len(scalars) + [VMEM] * len(ins) + [ANYWHERE] * len(loose),
        out_specs=[kinds[k][1] for _, _, k in outs],
        out_shape=out_shape,
        scratch_shapes=list(scratch),
        input_output_aliases=aliases or {},
        compiler_params=pltpu.CompilerParams(vmem_limit_bytes=limit << 20),
        cost_estimate=pl.CostEstimate(flops=flops, bytes_accessed=moved, transcendentals=0),
    )(*scalars, *[pltpu.with_memory_space_constraint(a, pltpu.VMEM) for a in ins], *loose)


def exchange(replicated):
    return lax.all_to_all(replicated, AXES, 0, 0)


def on_device(
    images, image_counts, labels, fw_picks, task_average, conv_weights, conv_momentum, conv_average,
    norm_parameter_list, norm_momentum, norm_average, head_params, head_momentum, head_average,
):
    rows, map_side, channels = images.shape[0], images.shape[1], images.shape[3]
    width = map_side * map_side * channels
    devices = lax.axis_size(AXES)
    tasks = labels.shape[1]
    task_cols = head_params.shape[1]
    fw_steps = fw_picks.shape[0]
    matmul = 2 * rows * width * width
    tuned = (lax.axis_size("dp"), lax.axis_size("task"), channels) == (8, 4, 512)

    def stat(count):
        return ((devices, 1, count), F32, "free")

    slots = float(devices * rows * map_side * map_side)
    flat, flat_low = ((rows, width), F32, "vmem"), ((rows, width), BF16, "vmem")
    low = conv_weights.astype(BF16)
    heads = lax.all_gather(head_params, "task", axis=1, tiled=True)
    heads = jnp.pad(heads, ((0, 7), (0, LANES - tasks)))
    labels = jnp.pad(labels, ((0, 0), (0, LANES - tasks)))
    flat_images = images.reshape(rows, width)
    start = jnp.pad(task_average[None, :], ((0, 7), (0, LANES - tasks)))
    basis = jnp.concatenate(
        [
            (jnp.arange(LANES, dtype=jnp.int32)[None, :] == fw_picks[:, None]).astype(F32),
            start[0:1],
            jnp.zeros((32 - fw_steps - 1, LANES), F32),
        ],
        axis=0,
    )

    me = flat_index()
    core = me & 1

    def bind(body, *static):
        return lambda *refs: body(*static, *refs)

    k2 = lax.all_gather(low[1], AXES, axis=0, tiled=True)
    if tuned:
        tall_low = (9 * channels, channels)
        chips = devices // 2
        at_x, at_y = me // ALONG_X & 1, me // ALONG_Y & 1
        index = jnp.arange(chips // 2, dtype=jnp.int32)
        by_x, by_y = index * 2, index // 2 * 4 + index % 2
        here = jnp.where(core == 0, by_x + at_x, by_y + 2 * at_y)
        there = jnp.where(core == 0, by_x + 1 - at_x, by_y + 2 * (1 - at_y))
        own = jnp.where(core == 0, at_y, at_x)
        index = jnp.arange(chips // 4, dtype=jnp.int32) * 2
        tables = (
            piece_places(low.shape[1]), jnp.concatenate([there, here]), jnp.concatenate([index + 1 - own, index + own]),
            (me // ALONG_Z)[None], core[None], me[None], image_counts + 0,
        )
        pieces, flat_images, (tables, start, basis), (heads, labels) = gather_pieces(
            low[0], flat_images, (tables, start, basis), (heads, labels)
        )
        places, chunk_table, pair_table, z_place, core_place, me_place, image_counts = tables
        first, stat1, k1 = call(
            first_gathered_kernel, [flat_images], [flat, stat(1152), (tall_low, BF16, "hbm")],
            [pltpu.VMEM(tall_low, BF16), pltpu.SemaphoreType.DMA, pltpu.SemaphoreType.DMA],
            (image_counts, places), pieces, matmul, limit=7,
        )
    else:
        k1 = lax.all_gather(low[0], AXES, axis=0, tiled=True)
        first, stat1 = call(first_kernel, [flat_images, k1], [flat, stat(1152)], (), (image_counts,), (), matmul)
    if tuned:
        images_other = swap(flat_images, CORE, CORE)
        stat1, images_other = lax.optimization_barrier((stat1, images_other))
    else:
        core_place = core[None]
    g1 = exchange(stat1)
    hidden, second, stat2 = call(
        second_kernel, [first, g1, norm_parameter_list, k2], [flat_low, flat, stat(1024)], (), (image_counts,), (), matmul, limit=5
    )
    g2 = exchange(stat2)
    if tuned:
        g2, moved_hidden = lax.optimization_barrier((g2, hidden))
        hidden_other = swap(moved_hidden, CORE, CORE)
    per_channel = ((rows, channels), F32, "vmem")
    block_flat, slope, slope_sum, slope_xhat, pooled, resid, gram = call(
        bind(head_kernel, tasks), [second, g2, g1, norm_parameter_list, flat_images, labels, heads, basis],
        [flat_low, flat, per_channel, per_channel, ((rows, channels + LANES), F32, "vmem"), ((rows, LANES), F32, "vmem"), stat(1024)],
        (), (image_counts,), (), matmul, limit=3,
    )
    if tuned:
        gram, hidden_other = lax.optimization_barrier((gram, hidden_other))
    g3 = exchange(gram)
    dout, stat4, head_send, mix = call(
        bind(mix_kernel, fw_steps), [g3, basis, start, resid, pooled, heads, slope_sum, slope_xhat],
        [per_channel, stat(1024), ((tasks // task_cols, 1, task_cols * (channels + LANES)), F32, "free"), ((8, LANES), F32, "free")],
        (), (), (), matmul // 2, limit=3,
    )
    g4 = exchange(stat4)
    part = channels // 2
    shard_rows = conv_weights.shape[1]
    sent = [((rows, width // 2), BF16, "vmem")] * 2 if tuned else [flat_low]
    ways = tasks // task_cols
    sums = ((ways, 1, 4 * channels), F32, "free")
    dnormed, stat5, sums_two, dpre, *dsecond_halves = call(
        back_second_kernel, [slope, dout, second, first, g1, g2, g4, norm_parameter_list, k2],
        [flat, stat(1024), sums, flat_low] + sent, [pltpu.VMEM((TILE, width), BF16)], (image_counts, core_place), (), matmul, {4: 0}, limit=8,
    )
    g5 = exchange(stat5)
    if tuned:
        g5, *dsecond_halves = lax.optimization_barrier((g5, *dsecond_halves))
        dsecond_other = swap(dsecond_halves[1], CORE, CORE)
    dfirst, sums_one, *dfirst_halves = call(
        dfirst_kernel, [dnormed, first, g1, g5, norm_parameter_list],
        [flat_low, sums] + (sent if tuned else []), (), (image_counts, core_place), (), matmul // 4, limit=6,
    )

    def combine(keep, got, table):
        dims = (keep.shape[0] // 2,) + keep.shape[1:]
        return call(combine_kernel, [keep, got], [(dims, BF16, "free"), (dims, F32, "vmem")], (), (table,), limit=5)

    def scatter_start(x, x_other, d, d_other, mean_of, source):
        dims = (devices // 4, 2 * shard_rows, part)
        return call(
            bind(pair_weight_grad_kernel, mean_of), [x, d, source, x_other, d_other],
            [(dims, BF16, "free"), (dims, F32, "vmem")], [pltpu.VMEM((9 * channels, part), F32)],
            (chunk_table,), (), matmul, limit=18,
        )

    def scatter_next(send, keep):
        return combine(keep, swap(send, *SQUARE[0]), pair_table)

    def scatter_line(got, keep):
        pair = keep.shape[1:]
        return call(line_kernel, [keep, got], [(pair, F32, "vmem")] + [(pair, BF16, "free")] * 3, (), (z_place,), limit=3)

    def scatter_finish(own, sent):
        half = ((shard_rows, part), F32, "free")
        return call(line_sum_kernel, [own] + sent, [half, half], (), (core_place,), limit=3)

    def scatter_whole(x, d):
        (whole,) = call(weight_grad_kernel, [x, d], [((9 * channels, channels), F32, "free")], (), (), (), matmul)
        return lax.psum_scatter(whole, AXES, scatter_dimension=0, tiled=True)

    def share_task(*values):
        return lax.all_to_all(jnp.concatenate(values, axis=2), "task", 0, 0)

    def share_dp(over_task):
        dims = (lax.axis_size("dp"),) + over_task.shape[1:]
        (over_dp,) = call(relay_kernel, [over_task], [(dims, F32, "free")], limit=4)
        return lax.all_to_all(over_dp, "dp", 0, 0)

    def image_gradient(begin, end, late, buffer=()):
        return call(
            bind(image_grad_kernel, begin, end), [late, k1, dpre], [(images.shape, F32, "hbm")],
            [pltpu.VMEM((2, TILE) + images.shape[1:], F32), pltpu.SemaphoreType.DMA((2,))], (), buffer, matmul * (end - begin) // rows,
            {3: 0} if buffer else None, limit=6,
        )[0]

    if tuned:
        dfirst_other = swap(dfirst_halves[1], CORE, CORE)
        dsecond_own, dsecond_other, hidden, hidden_other, dfirst = lax.optimization_barrier(
            (dsecond_halves[0], dsecond_other, hidden, hidden_other, dfirst)
        )
        two = scatter_start(hidden, hidden_other, dsecond_own, dsecond_other, hidden_mean, norm_parameter_list)
        send_two, flat_images, images_other, dfirst_own = lax.optimization_barrier((two[0], flat_images, images_other, dfirst_halves[0]))
        one = scatter_start(flat_images, images_other, dfirst_own, dfirst_other, bind(image_mean, slots), g3)
        send_one, keep_two = lax.optimization_barrier((one[0], two[1]))
        send_two, keep_two = scatter_next(send_two, keep_two)
        got_two = swap(send_two, *SQUARE[1])
        send_two, late = lax.optimization_barrier((send_two, dfirst))
        image_part = image_gradient(0, rows // 2, late)
        got_two, image_part = lax.optimization_barrier((got_two, image_part))
        line_two = scatter_line(got_two, keep_two)
        sent_two = [swap(line_two[m], m * ALONG_Z, m * ALONG_Z) for m in (1, 2, 3)]
        line_first, keep_one = lax.optimization_barrier((line_two[1], one[1]))
        send_one, keep_one = scatter_next(send_one, keep_one)
        got_one = swap(send_one, *SQUARE[1])
        send_one, block_flat = lax.optimization_barrier((send_one, block_flat))
        block_output = block_flat.reshape(images.shape)
        got_one, block_output, sent_two = lax.optimization_barrier((got_one, block_output, sent_two))
        line_one = scatter_line(got_one, keep_one)
        sent_one = [swap(line_one[m], m * ALONG_Z, m * ALONG_Z) for m in (1, 2, 3)]
        line_first, head_send, sums_two, sums_one, late, image_part = lax.optimization_barrier(
            (line_one[1], head_send, sums_two, sums_one, late, image_part)
        )
        shared = share_task(head_send, sums_two, sums_one)
        image_grad = image_gradient(rows // 2, rows, late, (image_part,))
        shared, sent_one, image_grad = lax.optimization_barrier((shared, sent_one, image_grad))
        ends = (scatter_finish(line_one[0], sent_one), scatter_finish(line_two[0], sent_two))
        shared, ends = lax.optimization_barrier((shared, ends))
        last = share_dp(shared)
        shards = conv_weights.shape
        outs = [(shards, F32, "free")] * 4 + [(shards, BF16, "free")]
        conv_grads, conv_momentum_new, conv_weights_new, conv_average_new, conv_weights_low = call(
            bind(finish_kernel, slots),
            [v for send, keep in ends for v in (keep, swap(send, CORE, CORE))]
            + [g3, norm_parameter_list, last, conv_weights, conv_momentum, conv_average],
            outs, [pltpu.VMEM((1024, LANES), F32), pltpu.VMEM((16, channels), F32)], (me_place,), limit=5,
        )
    else:
        last = share_dp(share_task(head_send, sums_two, sums_one))
        grad_two = scatter_whole(hidden, dsecond_halves[0])
        grad_one = scatter_whole(flat_images, dfirst)
        image_grad = image_gradient(0, rows, dfirst)
        block_output = block_flat.reshape(images.shape)
        conv_grads = jnp.stack([grad_one, grad_two])
        conv_momentum_new, conv_weights_new, conv_average_new = nesterov(conv_weights, conv_momentum, conv_grads, CONV_RATE, conv_average)
        conv_weights_low = conv_weights_new.astype(BF16)
    head_dims = (head_params.shape[1], head_params.shape[0])
    norm_grads, norm_momentum_new, norm_params_new, norm_average_new, *head_new = call(
        small_kernel,
        [last, g4, g5, norm_parameter_list, norm_momentum, norm_average, head_params.T, head_momentum.T, head_average.T],
        [(norm_momentum.shape, F32, "free")] * 4 + [(head_dims, F32, "free")] * 4, limit=4,
    )
    head_grads, head_momentum_new, head_params_new, head_average_new = [value.T for value in head_new]
    task_average_new = AVERAGE_DECAY * task_average + (1.0 - AVERAGE_DECAY) * mix[0, :tasks]
    return (
        block_output,
        image_grad,
        conv_grads,
        conv_momentum_new,
        conv_weights_new,
        conv_average_new,
        conv_weights_low,
        norm_grads,
        norm_momentum_new,
        norm_params_new,
        norm_average_new,
        head_grads,
        head_momentum_new,
        head_params_new,
        head_average_new,
        task_average_new,
    )


def solution(mesh):
    both = P(AXES)
    rowwise = P(None, AXES, None)
    head = P(None, "task")
    return jax.shard_map(
        on_device,
        mesh=mesh,
        in_specs=(both, both, both, P(), P(), rowwise, rowwise, rowwise, P(), P(), P(), head, head, head),
        out_specs=(both, both, rowwise, rowwise, rowwise, rowwise, rowwise, P(), P(), P(), P(), head, head, head, head, P()),
        check_vma=False,
    )
```

```python
import jax
import jax.numpy as jnp
import numpy as np
from jax import lax
from jax.experimental import pallas as pl
from jax.experimental.pallas import tpu as pltpu
from jax.sharding import PartitionSpec as P

EPSILON = 1e-05
MOMENTUM_DECAY = 0.5
AVERAGE_DECAY = 0.5
CONV_RATE = 2000.0
NORM_RATE = 40000.0
HEAD_RATE = 1000.0
STEP_CAP = 0.5
GROUP = 21
GELU_A = 0.7978845608
GELU_B = 0.7978845608 * 0.044715
AXES = ("dp", "task")
PRECISE = lax.Precision.HIGHEST
F32 = jnp.float32
BF16 = jnp.bfloat16
TILE = 256
CONV_TILE = 512
LANES = 128


def tap(q, p):
    return (q // 2 - p // 2 + 1) * 3 + (q % 2 - p % 2 + 1)


def dot(a, b):
    return jnp.dot(a, b, preferred_element_type=F32)


def dot_nt(a, b):
    return lax.dot_general(a, b, (((1,), (1,)), ((), ())), preferred_element_type=F32)


def dot_tn(a, b):
    return lax.dot_general(a, b, (((0,), (0,)), ((), ())), preferred_element_type=F32)


def precise(a, b, dims):
    return lax.dot_general(a, b, ((dims[0], dims[1]), ((), ())), precision=PRECISE, preferred_element_type=F32)


def fold8(v):
    return jnp.sum(v.reshape(v.shape[0] // 8, 8, v.shape[1]), 0)


def spread_rows(out_ref, rows):
    row = jnp.concatenate(rows, axis=1)
    out_ref[...] = jnp.broadcast_to(row[None], (out_ref.shape[0], 1, row.shape[1]))


def gathered_rows(ref, count):
    total = jnp.sum(ref[...], 0)
    return [total[:, r * 512 : (r + 1) * 512] for r in range(count)]


def moments(gathered_ref, spatial):
    value_sum, square_sum = gathered_rows(gathered_ref, 2)
    mean = value_sum / spatial
    inverse = lax.rsqrt(square_sum / spatial - mean * mean + EPSILON)
    return mean, inverse


def images_total(g1_ref):
    return jnp.sum(g1_ref[:, :, 1024:1152], 0)[:, 0:1]


def real_mask(count, start, rows):
    index = lax.broadcasted_iota(jnp.int32, (rows, 1), 0) + start
    return (index < count).astype(F32)


def plus(total, value):
    return value if total is None else total + value


def column_sums(values):
    return [jnp.sum(v, 0, keepdims=True) for v in values]


def conv_tile(x_ref, k_ref, out_ref, start, size, mask, total, square):
    rows = slice(start, start + size)
    for p in range(4):
        pr, pc = p // 2, p % 2
        acc = None
        for qr in range(2):
            base = ((qr - pr + 1) * 3 + (1 - pc)) * 512
            acc = plus(acc, dot(x_ref[rows, qr * 1024 : (qr + 1) * 1024], k_ref[base : base + 1024, :]))
        out_ref[rows, p * 512 : (p + 1) * 512] = acc
        masked = acc * mask
        total = plus(total, fold8(masked))
        square = plus(square, fold8(masked * acc))
    return total, square


def first_kernel(count_ref, x_ref, k_ref, first_ref, stat_ref):
    count = count_ref[0]
    total = square = None
    for start in range(0, x_ref.shape[0], CONV_TILE):
        mask = real_mask(count, start, CONV_TILE)
        total, square = conv_tile(x_ref, k_ref, first_ref, start, CONV_TILE, mask, total, square)
    spread_rows(stat_ref, column_sums((total, square)) + [jnp.full((1, LANES), count.astype(F32), F32)])


def load_pieces(place_ref, pieces, k_ref, load_sem):
    rows = pieces[0].shape[1]
    for n, piece in enumerate(pieces):
        cols = pl.ds((n // 4) * 256, 256)
        for i in range(piece.shape[0]):
            place = pl.multiple_of(place_ref[n * piece.shape[0] + i], 16)
            pltpu.make_async_copy(piece.at[i], k_ref.at[pl.ds(place, rows), cols], load_sem).start()
    pltpu.make_async_copy(k_ref, k_ref, load_sem).wait()


def first_gathered_kernel(count_ref, place_ref, x_ref, *refs):
    pieces, (first_ref, stat_ref, k_out_ref, k_ref, load_sem, store_sem) = refs[:8], refs[8:]
    load_pieces(place_ref, pieces, k_ref, load_sem)
    store = pltpu.make_async_copy(k_ref, k_out_ref, store_sem)
    store.start()
    first_kernel(count_ref, x_ref, k_ref, first_ref, stat_ref)
    store.wait()


def gelu_gate(v):
    return 0.5 * jnp.tanh(v * (GELU_A + GELU_B * (v * v))) + 0.5


def gelu_slope(v, gate):
    inner = v * (2.0 * GELU_A + (6.0 * GELU_B) * (v * v))
    return gate + gate * (inner - inner * gate)


def second_kernel(count_ref, first_ref, g1_ref, norm_ref, k_ref, hidden_ref, second_ref, stat_ref):
    mean, inverse = moments(g1_ref, images_total(g1_ref) * 4.0)
    scale = norm_ref[0:1, :] * inverse
    shift = norm_ref[1:2, :] - mean * scale
    total = square = None
    for start in range(0, first_ref.shape[0], CONV_TILE):
        rows = slice(start, start + CONV_TILE)
        for p in range(4):
            v = first_ref[rows, p * 512 : (p + 1) * 512] * scale + shift
            hidden_ref[rows, p * 512 : (p + 1) * 512] = (v * gelu_gate(v)).astype(BF16)
        mask = real_mask(count_ref[0], start, CONV_TILE)
        total, square = conv_tile(hidden_ref, k_ref, second_ref, start, CONV_TILE, mask, total, square)
    spread_rows(stat_ref, column_sums((total, square)))


def head_kernel(
    tasks, count_ref, second_ref, g2_ref, g1_ref, norm_ref, image_ref, label_ref, head_ref, pick_ref,
    out_ref, slope_ref, slope_sum_ref, slope_xhat_ref, pooled_ref, resid_ref, gram_out_ref,
):
    real_total = images_total(g1_ref)
    mean, inverse = moments(g2_ref, real_total * 4.0)
    gain, shift = norm_ref[2:3, :], norm_ref[3:4, :]
    lane_real = (lax.broadcasted_iota(jnp.int32, (1, LANES), 1) < tasks).astype(F32)
    gram = image_sum = None
    for start in range(0, second_ref.shape[0], TILE):
        rows = slice(start, start + TILE)
        pooled = slope_sum = slope_xhat = None
        for p in range(4):
            cols = slice(p * 512, (p + 1) * 512)
            xhat = (second_ref[rows, cols] - mean) * inverse
            image = image_ref[rows, cols].astype(F32)
            image_sum = plus(image_sum, fold8(image))
            pre = gain * xhat + shift + image
            gate = gelu_gate(pre)
            out = pre * gate
            out_ref[rows, cols] = out.astype(BF16)
            slope = gelu_slope(pre, gate)
            slope_ref[rows, cols] = slope
            pooled = plus(pooled, out)
            slope_sum = plus(slope_sum, slope)
            slope_xhat = plus(slope_xhat, slope * xhat)
        pooled = pooled * 0.25
        slope_sum_ref[rows, :] = slope_sum
        slope_xhat_ref[rows, :] = slope_xhat
        pooled_ref[rows, 0:512] = pooled
        pooled_ref[rows, 512:640] = (lax.broadcasted_iota(jnp.int32, (TILE, LANES), 1) == 0).astype(F32)
        logits = precise(pooled, head_ref[0:512, :], ((1,), (0,))) + head_ref[512:513, :]
        mask = real_mask(count_ref[0], start, TILE) * lane_real
        resid = mask * (jax.nn.sigmoid(logits) - label_ref[rows, :].astype(F32)) / real_total
        resid_ref[rows, :] = resid
        gram = plus(gram, precise(resid, resid, ((0,), (0,))))
    heads = head_ref[0:512, :]
    gram = gram * precise(heads, heads, ((0,), (0,)))
    basis = pick_ref[...]
    projected = precise(gram, basis, ((1,), (1,)))
    lane = lax.broadcasted_iota(jnp.int32, (32, LANES), 1)
    row = lax.broadcasted_iota(jnp.int32, (32, LANES), 0)
    packed = None
    for group in range(6):
        placed = precise(projected, ((lane == row + GROUP * group) & (row < GROUP)).astype(F32), ((1,), (0,)))
        packed = plus(packed, precise(basis[4 * group : 4 * group + 4, :], placed, ((1,), (0,))))
    spread_rows(gram_out_ref, [packed[r : r + 1, :] for r in range(4)] + column_sums((image_sum,)))


def frank_wolfe(packed, picks, start_mix, fw_steps):
    rows = jnp.concatenate([packed[:, GROUP * g : GROUP * (g + 1)] for g in range(6)], axis=0)
    column = [jnp.broadcast_to(rows[:, k : k + 1], (24, LANES)) for k in range(fw_steps + 1)]
    along = column[fw_steps]
    a = along[fw_steps : fw_steps + 1, :]
    mix = start_mix
    for k in range(fw_steps):
        b = along[k : k + 1, :]
        c = column[k][k : k + 1, :]
        size = jnp.clip((a - b) / (a - 2.0 * b + c), 0.0, STEP_CAP)
        keep = 1.0 - size
        a = keep * keep * a + 2.0 * (keep * size) * b + size * size * c
        along = keep * along + size * column[k]
        mix = keep * mix + size * picks[k : k + 1, :]
    return mix


def mix_kernel(
    fw_steps, gram_ref, pick_ref, start_ref, resid_ref, pooled_ref, head_ref, slope_sum_ref, slope_xhat_ref,
    dout_ref, stat_ref, head_grad_ref, mix_ref,
):
    (total,) = gathered_rows(gram_ref, 1)
    packed = jnp.concatenate([total[:, r * LANES : (r + 1) * LANES] for r in range(4)], axis=0)
    mix = frank_wolfe(packed, pick_ref[...], start_ref[0:1, :], fw_steps)
    mix_ref[...] = jnp.broadcast_to(mix, mix_ref.shape)
    gain_sum = shift_sum = head_grad = None
    for start in range(0, resid_ref.shape[0], TILE):
        rows = slice(start, start + TILE)
        weighted = resid_ref[rows, :] * mix
        dout = precise(weighted, head_ref[0:512, :], ((1,), (1,))) * 0.25
        dout_ref[rows, :] = dout
        head_grad = plus(head_grad, precise(weighted, pooled_ref[rows, :], ((0,), (0,))))
        gain_sum = plus(gain_sum, fold8(dout * slope_xhat_ref[rows, :]))
        shift_sum = plus(shift_sum, fold8(dout * slope_sum_ref[rows, :]))
    spread_rows(stat_ref, column_sums((gain_sum, shift_sum)))
    ways, width = head_grad_ref.shape[0], head_grad.shape[1]
    cols = head_grad_ref.shape[2] // width
    for way in range(ways):
        rows = [head_grad[way * cols + i : way * cols + i + 1, :] for i in range(cols)]
        head_grad_ref[way] = jnp.concatenate(rows, axis=1)


def store_sums(sum_ref, sums):
    spread_rows(sum_ref, column_sums(sums))


def split_halves(core, grad, half_refs, rows, p):
    if len(half_refs) == 1:
        half_refs[0][rows, p * grad.shape[1] : (p + 1) * grad.shape[1]] = grad
    else:
        half = grad.shape[1] // 2
        low, high = grad[:, :half], grad[:, half:]
        own_ref, send_ref = half_refs
        own_ref[rows, p * half : (p + 1) * half] = jnp.where(core == 0, low, high)
        send_ref[rows, p * half : (p + 1) * half] = jnp.where(core == 0, high, low)


def back_second_kernel(
    count_ref, core_ref, slope_ref, dout_ref, second_ref, first_ref, g1_ref, g2_ref, g4_ref, norm_ref, k_ref,
    dnormed_ref, stat_ref, sum_ref, dpre_ref, *half_refs,
):
    spatial = images_total(g1_ref) * 4.0
    mean1, inverse1 = moments(g1_ref, spatial)
    mean2, inverse2 = moments(g2_ref, spatial)
    gain_grad, shift_grad = gathered_rows(g4_ref, 2)
    scale2 = norm_ref[2:3, :] * inverse2
    by_value = scale2 * gain_grad * inverse2 / spatial
    by_one = scale2 * shift_grad / spatial - by_value * mean2
    gain1, shift1 = norm_ref[0:1, :], norm_ref[1:2, :]
    gain_sum = shift_sum = None
    sums = [None] * 4
    *half_refs, dsecond_ref = half_refs
    for start in range(0, second_ref.shape[0], TILE):
        rows = slice(start, start + TILE)
        mask = real_mask(count_ref[0], start, TILE)
        dout = dout_ref[rows, :]
        for p in range(4):
            cols = slice(p * 512, (p + 1) * 512)
            dpre = dout * slope_ref[rows, cols]
            dpre_ref[rows, cols] = dpre.astype(BF16)
            grad = (scale2 * dpre - mask * (by_one + by_value * second_ref[rows, cols])).astype(BF16)
            dsecond_ref[:, cols] = grad
            split_halves(core_ref[0], grad, half_refs, rows, p)
            sums[p] = plus(sums[p], fold8(grad.astype(F32)))
        for q in range(4):
            cols = slice(q * 512, (q + 1) * 512)
            acc = None
            for p in range(4):
                base = tap(q, p) * 512
                acc = plus(acc, dot_nt(dsecond_ref[:, p * 512 : (p + 1) * 512], k_ref[base : base + 512, :]))
            xhat = (first_ref[rows, cols] - mean1) * inverse1
            v = gain1 * xhat + shift1
            dnormed = acc * gelu_slope(v, gelu_gate(v))
            dnormed_ref[rows, cols] = dnormed
            gain_sum = plus(gain_sum, fold8(dnormed * xhat))
            shift_sum = plus(shift_sum, fold8(dnormed))
    spread_rows(stat_ref, column_sums((gain_sum, shift_sum)))
    store_sums(sum_ref, sums)


def taps_of(index):
    return [(q, p) for q in range(4) for p in range(4) if tap(q, p) == index]


def weight_grad_kernel(x_ref, d_ref, out_ref):
    for index in range(9):
        acc = None
        for q, p in taps_of(index):
            acc = plus(acc, dot_tn(x_ref[:, q * 512 : (q + 1) * 512], d_ref[:, p * 512 : (p + 1) * 512]))
        out_ref[index * 512 : (index + 1) * 512, :] = acc


def as_column(row):
    return jnp.transpose(jnp.broadcast_to(row, (LANES, row.shape[1])))


def image_mean(slots, g3_ref):
    return gathered_rows(g3_ref, 2)[1] * (1.0 / slots)


def hidden_mean(norm_ref):
    nodes, weights = np.polynomial.hermite_e.hermegauss(9)
    total = None
    for node, weight in zip(nodes, weights / weights.sum()):
        v = norm_ref[0:1, :] * float(node) + norm_ref[1:2, :]
        total = plus(total, float(weight) * (v * gelu_gate(v)))
    return total


def pair_weight_grad_kernel(mean_of, table_ref, x_ref, d_ref, mean_ref, x_other_ref, d_other_ref, send_ref, keep_ref, whole_ref):
    width = whole_ref.shape[1]
    column = as_column(mean_of(mean_ref))
    column = jnp.concatenate([column] * (width // LANES), axis=1)
    sums = []
    for p in range(4):
        cols = slice(p * width, (p + 1) * width)
        sums.append(jnp.sum(fold8(d_ref[:, cols].astype(F32)) + fold8(d_other_ref[:, cols].astype(F32)), 0, keepdims=True))
    seen = set()
    for q in range(4):
        acc = dot_tn(x_ref[:, q * 512 : (q + 1) * 512], d_ref[...])
        acc = acc + dot_tn(x_other_ref[:, q * 512 : (q + 1) * 512], d_other_ref[...])
        for p in range(4):
            index = tap(q, p)
            rows = slice(index * 512, (index + 1) * 512)
            part = acc[:, p * width : (p + 1) * width] - column * sums[p]
            whole_ref[rows, :] = whole_ref[rows, :] + part if index in seen else part
            seen.add(index)
    count, rows = keep_ref.shape[0], keep_ref.shape[1]
    for i in range(count):
        there = pl.ds(pl.multiple_of(table_ref[i] * rows, 16), rows)
        here = pl.ds(pl.multiple_of(table_ref[count + i] * rows, 16), rows)
        send_ref[i] = whole_ref[there, :].astype(BF16)
        keep_ref[i] = whole_ref[here, :]


def dfirst_kernel(count_ref, core_ref, dnormed_ref, first_ref, g1_ref, g5_ref, norm_ref, dfirst_ref, stat_ref, *half_refs):
    spatial = images_total(g1_ref) * 4.0
    mean1, inverse1 = moments(g1_ref, spatial)
    gain_grad, shift_grad = gathered_rows(g5_ref, 2)
    scale = norm_ref[0:1, :] * inverse1
    by_value = scale * gain_grad * inverse1 / spatial
    by_one = scale * shift_grad / spatial - by_value * mean1
    sums = [None] * 4
    for start in range(0, first_ref.shape[0], TILE):
        rows = slice(start, start + TILE)
        mask = real_mask(count_ref[0], start, TILE)
        for p in range(4):
            cols = slice(p * 512, (p + 1) * 512)
            grad = (scale * dnormed_ref[rows, cols] - mask * (by_one + by_value * first_ref[rows, cols])).astype(BF16)
            dfirst_ref[rows, cols] = grad
            if half_refs:
                split_halves(core_ref[0], grad, half_refs, rows, p)
            sums[p] = plus(sums[p], fold8(grad.astype(F32)))
    store_sums(stat_ref, sums)


def image_grad_kernel(begin, end, dfirst_ref, k_ref, dpre_ref, *refs):
    out_ref, buffer_ref, sem = refs[-3:]
    copies = []
    for n, start in enumerate(range(begin, end, TILE)):
        rows = slice(start, start + TILE)
        slot = n % 2
        if n >= 2:
            copies[n - 2].wait()
        for q in range(4):
            cols = slice(q * 512, (q + 1) * 512)
            acc = dpre_ref[rows, cols].astype(F32)
            for p in range(4):
                base = tap(q, p) * 512
                acc = acc + dot_nt(dfirst_ref[rows, p * 512 : (p + 1) * 512], k_ref[base : base + 512, :])
            buffer_ref[slot, :, q // 2, q % 2, :] = acc
        copies.append(pltpu.make_async_copy(buffer_ref.at[slot], out_ref.at[pl.ds(start, TILE)], sem.at[slot]))
        copies[n].start()
    for copy in copies[-2:]:
        copy.wait()


def combine_kernel(table_ref, keep_ref, got_ref, send_ref, out_ref):
    count = out_ref.shape[0]
    for i in range(count):
        there, here = table_ref[i], table_ref[count + i]
        send_ref[i] = (keep_ref[there] + got_ref[there].astype(F32)).astype(BF16)
        out_ref[i] = keep_ref[here] + got_ref[here].astype(F32)


def line_kernel(z_ref, keep_ref, got_ref, *out_refs):
    for mask, ref in enumerate(out_refs):
        place = z_ref[0] ^ mask
        ref[...] = (keep_ref[place] + got_ref[place].astype(F32)).astype(ref.dtype)


def line_sum_kernel(core_ref, keep_ref, got1_ref, got2_ref, got3_ref, send_ref, out_ref):
    half = out_ref.shape[0]
    for ref, place in ((send_ref, 1 - core_ref[0]), (out_ref, core_ref[0])):
        rows = pl.ds(pl.multiple_of(place * half, 16), half)
        got = got1_ref[rows, :].astype(F32) + got2_ref[rows, :].astype(F32) + got3_ref[rows, :].astype(F32)
        ref[...] = keep_ref[rows, :] + got


def finish_kernel(
    slots, me_ref, keep1_ref, got1_ref, keep2_ref, got2_ref, g3_ref, norm_ref, last_ref, weight_ref, momentum_ref, average_ref,
    grad_ref, momentum_new_ref, weight_new_ref, average_new_ref, low_ref, column_ref, sums_ref,
):
    core, start = me_ref[0] % 2, me_ref[0] * grad_ref.shape[1]
    rows = grad_ref.shape[1]
    index = lax.broadcasted_iota(jnp.int32, (rows, 1), 0) + start % 512
    last = jnp.sum(last_ref[...], 0)
    begin = last.shape[1] - 8 * 512
    sums = [last[:, begin + p * 512 : begin + (p + 1) * 512] for p in range(8)]
    sources = (
        (keep1_ref, got1_ref, image_mean(slots, g3_ref), sums[4:]),
        (keep2_ref, got2_ref, hidden_mean(norm_ref), sums[:4]),
    )
    for k, (keep_ref, got_ref, mean, sums) in enumerate(sources):
        column = as_column(mean)
        column_ref[0:512, :] = column
        column_ref[512:1024, :] = column
        for tap_index in range(9):
            total = None
            for _, p in taps_of(tap_index):
                total = plus(total, sums[p])
            sums_ref[tap_index : tap_index + 1, :] = total
        column = column_ref[pl.ds(pl.multiple_of(start % 512, 16), rows), :]
        first_tap = start // 512
        total = jnp.where(index < 512, sums_ref[pl.ds(first_tap, 1), :], sums_ref[pl.ds(jnp.minimum(first_tap + 1, 8), 1), :])
        keep, got = keep_ref[...], got_ref[...]
        low_half, high_half = jnp.where(core == 0, keep, got), jnp.where(core == 0, got, keep)
        grad = jnp.concatenate([low_half, high_half], axis=1) + jnp.concatenate([column] * 4, axis=1) * total
        momentum, weight, average = nesterov(weight_ref[k], momentum_ref[k], grad, CONV_RATE, average_ref[k])
        grad_ref[k] = grad
        momentum_new_ref[k] = momentum
        weight_new_ref[k] = weight
        average_new_ref[k] = average
        low_ref[k] = weight.astype(BF16)


def relay_kernel(in_ref, out_ref):
    out_ref[...] = jnp.broadcast_to(jnp.sum(in_ref[...], 0)[None], out_ref.shape)


def small_kernel(
    last_ref, g4_ref, g5_ref, norm_ref, norm_momentum_ref, norm_average_ref, head_ref, head_momentum_ref, head_average_ref, *out_refs
):
    norm_grads = jnp.concatenate(gathered_rows(g5_ref, 2) + gathered_rows(g4_ref, 2), axis=0)
    rows, cols = head_ref.shape
    last = jnp.sum(last_ref[...], 0)
    head_grads = jnp.concatenate([last[:, i * 640 : (i + 1) * 640] for i in range(rows)], axis=0)[:, :cols]
    values = (norm_grads,) + nesterov(norm_ref[...], norm_momentum_ref[...], norm_grads, NORM_RATE, norm_average_ref[...])
    values += (head_grads,) + nesterov(head_ref[...], head_momentum_ref[...], head_grads, HEAD_RATE, head_average_ref[...])
    for ref, value in zip(out_refs, values):
        ref[...] = value


def swap(value, even_mask, odd_mask):
    count = lax.axis_size(AXES)
    pairs = [(i, i ^ (odd_mask if i % 2 else even_mask)) for i in range(count)]
    return lax.ppermute(value, AXES, pairs)


CORE, ALONG_X, ALONG_Y, ALONG_Z = 1, 2, 4, 8
SQUARE = [(ALONG_X, ALONG_Y), (ALONG_Y, ALONG_X)]


def flat_index():
    return lax.axis_index("dp") * lax.axis_size("task") + lax.axis_index("task")


def along_line(shard):
    return jnp.stack([shard] + [swap(shard, m * ALONG_Z, m * ALONG_Z) for m in (1, 2, 3)])


def square_near(line):
    blocks = [line[:, :, :256], line[:, :, 256:]]
    return [jnp.concatenate([blocks[h], swap(blocks[h], *SQUARE[h])], 0) for h in (0, 1)]


def square_far(near):
    return [swap(near[h], *SQUARE[1 - h]) for h in (0, 1)]


def gather_pieces(shard, images, early, later):
    line = along_line(shard)
    line, images, early = lax.optimization_barrier((line, images, early))
    near = square_near(line)
    near, later = lax.optimization_barrier((near, later))
    far = square_far(near)
    sibling_near = [swap(v, CORE, CORE) for v in near]
    sibling_far = [swap(v, CORE, CORE) for v in far]
    pieces = [v[h] for h in (0, 1) for v in (near, far, sibling_near, sibling_far)]
    return pieces, images, early, later


def piece_places(rows):
    me = flat_index()
    core = me % 2
    owners = []
    part = jnp.arange(8, dtype=jnp.int32)
    for h in (0, 1):
        for base, which, is_far in ((me, core, 0), (me, core, 1), (me ^ CORE, 1 - core, 0), (me ^ CORE, 1 - core, 1)):
            x_first = which == h
            near_mask = jnp.where(x_first, ALONG_X, ALONG_Y)
            far_mask = jnp.where(x_first, ALONG_Y, ALONG_X)
            owners.append(base ^ (part % 4 * ALONG_Z) ^ (part // 4 * near_mask) ^ (is_far * far_mask))
    return jnp.concatenate(owners) * rows


def nesterov(params, momentum, grads, rate, average):
    momentum_new = MOMENTUM_DECAY * momentum + grads
    params_new = params - rate * (grads + MOMENTUM_DECAY * momentum_new)
    average_new = AVERAGE_DECAY * average + (1.0 - AVERAGE_DECAY) * params_new
    return (momentum_new, params_new, average_new)


VMEM = pl.BlockSpec(memory_space=pltpu.VMEM)
SCALAR = pl.BlockSpec(memory_space=pltpu.SMEM)
ANYWHERE = pl.BlockSpec(memory_space=pl.ANY)


def call(body, ins, outs, scratch=(), scalars=(), loose=(), flops=0, aliases=None, limit=12):
    kinds = {"vmem": (pltpu.VMEM, VMEM), "hbm": (pltpu.HBM, ANYWHERE), "free": (jax.ShapeDtypeStruct, VMEM)}
    out_shape = [kinds[k][0](d, t) for d, t, k in outs]
    moved = sum(a.size * a.dtype.itemsize for a in list(ins) + list(loose))
    return pl.pallas_call(
        body,
        in_specs=[SCALAR] * len(scalars) + [VMEM] * len(ins) + [ANYWHERE] * len(loose),
        out_specs=[kinds[k][1] for _, _, k in outs],
        out_shape=out_shape,
        scratch_shapes=list(scratch),
        input_output_aliases=aliases or {},
        compiler_params=pltpu.CompilerParams(vmem_limit_bytes=limit << 20),
        cost_estimate=pl.CostEstimate(flops=flops, bytes_accessed=moved, transcendentals=0),
    )(*scalars, *[pltpu.with_memory_space_constraint(a, pltpu.VMEM) for a in ins], *loose)


def exchange(replicated):
    return lax.all_to_all(replicated, AXES, 0, 0)


def on_device(
    images, image_counts, labels, fw_picks, task_average, conv_weights, conv_momentum, conv_average,
    norm_parameter_list, norm_momentum, norm_average, head_params, head_momentum, head_average,
):
    rows, map_side, channels = images.shape[0], images.shape[1], images.shape[3]
    width = map_side * map_side * channels
    devices = lax.axis_size(AXES)
    tasks = labels.shape[1]
    task_cols = head_params.shape[1]
    fw_steps = fw_picks.shape[0]
    matmul = 2 * rows * width * width
    tuned = (lax.axis_size("dp"), lax.axis_size("task"), channels) == (8, 4, 512)

    def stat(count):
        return ((devices, 1, count), F32, "free")

    slots = float(devices * rows * map_side * map_side)
    flat, flat_low = ((rows, width), F32, "vmem"), ((rows, width), BF16, "vmem")
    low = conv_weights.astype(BF16)
    heads = lax.all_gather(head_params, "task", axis=1, tiled=True)
    heads = jnp.pad(heads, ((0, 7), (0, LANES - tasks)))
    labels = jnp.pad(labels, ((0, 0), (0, LANES - tasks)))
    flat_images = images.reshape(rows, width)
    start = jnp.pad(task_average[None, :], ((0, 7), (0, LANES - tasks)))
    basis = jnp.concatenate(
        [
            (jnp.arange(LANES, dtype=jnp.int32)[None, :] == fw_picks[:, None]).astype(F32),
            start[0:1],
            jnp.zeros((32 - fw_steps - 1, LANES), F32),
        ],
        axis=0,
    )

    me = flat_index()
    core = me & 1

    def bind(body, *static):
        return lambda *refs: body(*static, *refs)

    k2 = lax.all_gather(low[1], AXES, axis=0, tiled=True)
    if tuned:
        tall_low = (9 * channels, channels)
        chips = devices // 2
        at_x, at_y = me // ALONG_X & 1, me // ALONG_Y & 1
        index = jnp.arange(chips // 2, dtype=jnp.int32)
        by_x, by_y = index * 2, index // 2 * 4 + index % 2
        here = jnp.where(core == 0, by_x + at_x, by_y + 2 * at_y)
        there = jnp.where(core == 0, by_x + 1 - at_x, by_y + 2 * (1 - at_y))
        own = jnp.where(core == 0, at_y, at_x)
        index = jnp.arange(chips // 4, dtype=jnp.int32) * 2
        tables = (
            piece_places(low.shape[1]), jnp.concatenate([there, here]), jnp.concatenate([index + 1 - own, index + own]),
            (me // ALONG_Z)[None], core[None], me[None], image_counts + 0,
        )
        pieces, flat_images, (tables, start, basis), (heads, labels) = gather_pieces(
            low[0], flat_images, (tables, start, basis), (heads, labels)
        )
        places, chunk_table, pair_table, z_place, core_place, me_place, image_counts = tables
        first, stat1, k1 = call(
            first_gathered_kernel, [flat_images], [flat, stat(1152), (tall_low, BF16, "hbm")],
            [pltpu.VMEM(tall_low, BF16), pltpu.SemaphoreType.DMA, pltpu.SemaphoreType.DMA],
            (image_counts, places), pieces, matmul, limit=7,
        )
    else:
        k1 = lax.all_gather(low[0], AXES, axis=0, tiled=True)
        first, stat1 = call(first_kernel, [flat_images, k1], [flat, stat(1152)], (), (image_counts,), (), matmul)
    if tuned:
        images_other = swap(flat_images, CORE, CORE)
        stat1, images_other = lax.optimization_barrier((stat1, images_other))
    else:
        core_place = core[None]
    g1 = exchange(stat1)
    hidden, second, stat2 = call(
        second_kernel, [first, g1, norm_parameter_list, k2], [flat_low, flat, stat(1024)], (), (image_counts,), (), matmul, limit=8
    )
    g2 = exchange(stat2)
    per_channel = ((rows, channels), F32, "vmem")
    block_flat, slope, slope_sum, slope_xhat, pooled, resid, gram = call(
        bind(head_kernel, tasks), [second, g2, g1, norm_parameter_list, flat_images, labels, heads, basis],
        [flat_low, flat, per_channel, per_channel, ((rows, channels + LANES), F32, "vmem"), ((rows, LANES), F32, "vmem"), stat(1024)],
        (), (image_counts,), (), matmul, limit=3,
    )
    g3 = exchange(gram)
    dout, stat4, head_send, mix = call(
        bind(mix_kernel, fw_steps), [g3, basis, start, resid, pooled, heads, slope_sum, slope_xhat],
        [per_channel, stat(1024), ((tasks // task_cols, 1, task_cols * (channels + LANES)), F32, "free"), ((8, LANES), F32, "free")],
        (), (), (), matmul // 2, limit=3,
    )
    g4 = exchange(stat4)
    if tuned:
        g4, hidden = lax.optimization_barrier((g4, hidden))
        hidden_other = swap(hidden, CORE, CORE)
    part = channels // 2
    shard_rows = conv_weights.shape[1]
    sent = [((rows, width // 2), BF16, "vmem")] * 2 if tuned else [flat_low]
    ways = tasks // task_cols
    sums = ((ways, 1, 4 * channels), F32, "free")
    dnormed, stat5, sums_two, dpre, *dsecond_halves = call(
        back_second_kernel, [slope, dout, second, first, g1, g2, g4, norm_parameter_list, k2],
        [flat, stat(1024), sums, flat_low] + sent, [pltpu.VMEM((TILE, width), BF16)], (image_counts, core_place), (), matmul, {4: 0}, limit=8,
    )
    if tuned:
        stat5, hidden_other = lax.optimization_barrier((stat5, hidden_other))
    g5 = exchange(stat5)
    if tuned:
        g5, *dsecond_halves = lax.optimization_barrier((g5, *dsecond_halves))
        dsecond_other = swap(dsecond_halves[1], CORE, CORE)
    dfirst, sums_one, *dfirst_halves = call(
        dfirst_kernel, [dnormed, first, g1, g5, norm_parameter_list],
        [flat_low, sums] + (sent if tuned else []), (), (image_counts, core_place), (), matmul // 4, limit=6,
    )

    def combine(keep, got, table):
        dims = (keep.shape[0] // 2,) + keep.shape[1:]
        return call(combine_kernel, [keep, got], [(dims, BF16, "free"), (dims, F32, "vmem")], (), (table,), limit=5)

    def scatter_start(x, x_other, d, d_other, mean_of, source):
        dims = (devices // 4, 2 * shard_rows, part)
        return call(
            bind(pair_weight_grad_kernel, mean_of), [x, d, source, x_other, d_other],
            [(dims, BF16, "free"), (dims, F32, "vmem")], [pltpu.VMEM((9 * channels, part), F32)],
            (chunk_table,), (), matmul, limit=18,
        )

    def scatter_next(send, keep):
        return combine(keep, swap(send, *SQUARE[0]), pair_table)

    def scatter_line(got, keep):
        pair = keep.shape[1:]
        return call(line_kernel, [keep, got], [(pair, F32, "vmem")] + [(pair, BF16, "free")] * 3, (), (z_place,), limit=3)

    def scatter_finish(own, sent):
        half = ((shard_rows, part), F32, "free")
        return call(line_sum_kernel, [own] + sent, [half, half], (), (core_place,), limit=3)

    def scatter_whole(x, d):
        (whole,) = call(weight_grad_kernel, [x, d], [((9 * channels, channels), F32, "free")], (), (), (), matmul)
        return lax.psum_scatter(whole, AXES, scatter_dimension=0, tiled=True)

    def share_task(*values):
        return lax.all_to_all(jnp.concatenate(values, axis=2), "task", 0, 0)

    def share_dp(over_task):
        dims = (lax.axis_size("dp"),) + over_task.shape[1:]
        (over_dp,) = call(relay_kernel, [over_task], [(dims, F32, "free")], limit=4)
        return lax.all_to_all(over_dp, "dp", 0, 0)

    def image_gradient(begin, end, late, buffer=()):
        return call(
            bind(image_grad_kernel, begin, end), [late, k1, dpre], [(images.shape, F32, "hbm")],
            [pltpu.VMEM((2, TILE) + images.shape[1:], F32), pltpu.SemaphoreType.DMA((2,))], (), buffer, matmul * (end - begin) // rows,
            {3: 0} if buffer else None, limit=6,
        )[0]

    if tuned:
        dfirst_other = swap(dfirst_halves[1], CORE, CORE)
        dsecond_own, dsecond_other, hidden, hidden_other, dfirst = lax.optimization_barrier(
            (dsecond_halves[0], dsecond_other, hidden, hidden_other, dfirst)
        )
        two = scatter_start(hidden, hidden_other, dsecond_own, dsecond_other, hidden_mean, norm_parameter_list)
        send_two, flat_images, images_other, dfirst_own = lax.optimization_barrier((two[0], flat_images, images_other, dfirst_halves[0]))
        one = scatter_start(flat_images, images_other, dfirst_own, dfirst_other, bind(image_mean, slots), g3)
        send_one, keep_two = lax.optimization_barrier((one[0], two[1]))
        send_two, keep_two = scatter_next(send_two, keep_two)
        got_two = swap(send_two, *SQUARE[1])
        send_two, late = lax.optimization_barrier((send_two, dfirst))
        image_grad = image_gradient(0, rows, late)
        got_two, image_grad = lax.optimization_barrier((got_two, image_grad))
        line_two = scatter_line(got_two, keep_two)
        sent_two = [swap(line_two[m], m * ALONG_Z, m * ALONG_Z) for m in (1, 2, 3)]
        line_first, keep_one = lax.optimization_barrier((line_two[1], one[1]))
        send_one, keep_one = scatter_next(send_one, keep_one)
        got_one = swap(send_one, *SQUARE[1])
        send_one, block_flat = lax.optimization_barrier((send_one, block_flat))
        block_output = block_flat.reshape(images.shape)
        got_one, block_output, sent_two = lax.optimization_barrier((got_one, block_output, sent_two))
        line_one = scatter_line(got_one, keep_one)
        sent_one = [swap(line_one[m], m * ALONG_Z, m * ALONG_Z) for m in (1, 2, 3)]
        line_first, head_send, sums_two, sums_one = lax.optimization_barrier((line_one[1], head_send, sums_two, sums_one))
        shared = share_task(head_send, sums_two, sums_one)
        ends = (scatter_finish(line_one[0], sent_one), scatter_finish(line_two[0], sent_two))
        shared, ends = lax.optimization_barrier((shared, ends))
        last = share_dp(shared)
        shards = conv_weights.shape
        outs = [(shards, F32, "free")] * 4 + [(shards, BF16, "free")]
        conv_grads, conv_momentum_new, conv_weights_new, conv_average_new, conv_weights_low = call(
            bind(finish_kernel, slots),
            [v for send, keep in ends for v in (keep, swap(send, CORE, CORE))]
            + [g3, norm_parameter_list, last, conv_weights, conv_momentum, conv_average],
            outs, [pltpu.VMEM((1024, LANES), F32), pltpu.VMEM((16, channels), F32)], (me_place,), limit=5,
        )
    else:
        last = share_dp(share_task(head_send, sums_two, sums_one))
        grad_two = scatter_whole(hidden, dsecond_halves[0])
        grad_one = scatter_whole(flat_images, dfirst)
        image_grad = image_gradient(0, rows, dfirst)
        block_output = block_flat.reshape(images.shape)
        conv_grads = jnp.stack([grad_one, grad_two])
        conv_momentum_new, conv_weights_new, conv_average_new = nesterov(conv_weights, conv_momentum, conv_grads, CONV_RATE, conv_average)
        conv_weights_low = conv_weights_new.astype(BF16)
    head_dims = (head_params.shape[1], head_params.shape[0])
    norm_grads, norm_momentum_new, norm_params_new, norm_average_new, *head_new = call(
        small_kernel,
        [last, g4, g5, norm_parameter_list, norm_momentum, norm_average, head_params.T, head_momentum.T, head_average.T],
        [(norm_momentum.shape, F32, "free")] * 4 + [(head_dims, F32, "free")] * 4, limit=4,
    )
    head_grads, head_momentum_new, head_params_new, head_average_new = [value.T for value in head_new]
    task_average_new = AVERAGE_DECAY * task_average + (1.0 - AVERAGE_DECAY) * mix[0, :tasks]
    return (
        block_output,
        image_grad,
        conv_grads,
        conv_momentum_new,
        conv_weights_new,
        conv_average_new,
        conv_weights_low,
        norm_grads,
        norm_momentum_new,
        norm_params_new,
        norm_average_new,
        head_grads,
        head_momentum_new,
        head_params_new,
        head_average_new,
        task_average_new,
    )


def solution(mesh):
    both = P(AXES)
    rowwise = P(None, AXES, None)
    head = P(None, "task")
    return jax.shard_map(
        on_device,
        mesh=mesh,
        in_specs=(both, both, both, P(), P(), rowwise, rowwise, rowwise, P(), P(), P(), head, head, head),
        out_specs=(both, both, rowwise, rowwise, rowwise, rowwise, rowwise, P(), P(), P(), P(), head, head, head, head, P()),
        check_vma=False,
    )
```

```python
import jax
import jax.numpy as jnp
import numpy as np
from jax import lax
from jax.experimental import pallas as pl
from jax.experimental.pallas import tpu as pltpu
from jax.sharding import PartitionSpec as P

EPSILON = 1e-05
MOMENTUM_DECAY = 0.5
AVERAGE_DECAY = 0.5
CONV_RATE = 2000.0
NORM_RATE = 40000.0
HEAD_RATE = 1000.0
STEP_CAP = 0.5
GROUP = 21
GELU_A = 0.7978845608
GELU_B = 0.7978845608 * 0.044715
AXES = ("dp", "task")
PRECISE = lax.Precision.HIGHEST
F32 = jnp.float32
BF16 = jnp.bfloat16
TILE = 256
CONV_TILE = 512
LANES = 128


def tap(q, p):
    return (q // 2 - p // 2 + 1) * 3 + (q % 2 - p % 2 + 1)


def dot(a, b):
    return jnp.dot(a, b, preferred_element_type=F32)


def dot_nt(a, b):
    return lax.dot_general(a, b, (((1,), (1,)), ((), ())), preferred_element_type=F32)


def dot_tn(a, b):
    return lax.dot_general(a, b, (((0,), (0,)), ((), ())), preferred_element_type=F32)


def precise(a, b, dims):
    return lax.dot_general(a, b, ((dims[0], dims[1]), ((), ())), precision=PRECISE, preferred_element_type=F32)


def fold8(v):
    return jnp.sum(v.reshape(v.shape[0] // 8, 8, v.shape[1]), 0)


def spread_rows(out_ref, rows):
    row = jnp.concatenate(rows, axis=1)
    out_ref[...] = jnp.broadcast_to(row[None], (out_ref.shape[0], 1, row.shape[1]))


def gathered_rows(ref, count):
    total = jnp.sum(ref[...], 0)
    return [total[:, r * 512 : (r + 1) * 512] for r in range(count)]


def moments(gathered_ref, spatial):
    value_sum, square_sum = gathered_rows(gathered_ref, 2)
    mean = value_sum / spatial
    inverse = lax.rsqrt(square_sum / spatial - mean * mean + EPSILON)
    return mean, inverse


def images_total(g1_ref):
    return jnp.sum(g1_ref[:, :, 1024:1152], 0)[:, 0:1]


def real_mask(count, start, rows):
    index = lax.broadcasted_iota(jnp.int32, (rows, 1), 0) + start
    return (index < count).astype(F32)


def plus(total, value):
    return value if total is None else total + value


def column_sums(values):
    return [jnp.sum(v, 0, keepdims=True) for v in values]


def conv_tile(x_ref, k_ref, out_ref, start, size, mask, total, square):
    rows = slice(start, start + size)
    for p in range(4):
        pr, pc = p // 2, p % 2
        acc = None
        for qr in range(2):
            base = ((qr - pr + 1) * 3 + (1 - pc)) * 512
            acc = plus(acc, dot(x_ref[rows, qr * 1024 : (qr + 1) * 1024], k_ref[base : base + 1024, :]))
        out_ref[rows, p * 512 : (p + 1) * 512] = acc
        masked = acc * mask
        total = plus(total, fold8(masked))
        square = plus(square, fold8(masked * acc))
    return total, square


def first_kernel(count_ref, x_ref, k_ref, first_ref, stat_ref):
    count = count_ref[0]
    total = square = None
    for start in range(0, x_ref.shape[0], CONV_TILE):
        mask = real_mask(count, start, CONV_TILE)
        total, square = conv_tile(x_ref, k_ref, first_ref, start, CONV_TILE, mask, total, square)
    spread_rows(stat_ref, column_sums((total, square)) + [jnp.full((1, LANES), count.astype(F32), F32)])


def load_pieces(place_ref, pieces, k_ref, load_sem):
    rows = pieces[0].shape[1]
    for n, piece in enumerate(pieces):
        cols = pl.ds((n // 4) * 256, 256)
        for i in range(piece.shape[0]):
            place = pl.multiple_of(place_ref[n * piece.shape[0] + i], 16)
            pltpu.make_async_copy(piece.at[i], k_ref.at[pl.ds(place, rows), cols], load_sem).start()
    pltpu.make_async_copy(k_ref, k_ref, load_sem).wait()


def first_gathered_kernel(count_ref, place_ref, x_ref, *refs):
    pieces, (first_ref, stat_ref, k_out_ref, k_ref, load_sem, store_sem) = refs[:8], refs[8:]
    load_pieces(place_ref, pieces, k_ref, load_sem)
    store = pltpu.make_async_copy(k_ref, k_out_ref, store_sem)
    store.start()
    first_kernel(count_ref, x_ref, k_ref, first_ref, stat_ref)
    store.wait()


def gelu_gate(v):
    return 0.5 * jnp.tanh(v * (GELU_A + GELU_B * (v * v))) + 0.5


def gelu_slope(v, gate):
    inner = v * (2.0 * GELU_A + (6.0 * GELU_B) * (v * v))
    return gate + gate * (inner - inner * gate)


def second_kernel(count_ref, first_ref, g1_ref, norm_ref, k_ref, hidden_ref, second_ref, stat_ref):
    mean, inverse = moments(g1_ref, images_total(g1_ref) * 4.0)
    scale = norm_ref[0:1, :] * inverse
    shift = norm_ref[1:2, :] - mean * scale
    total = square = None
    for start in range(0, first_ref.shape[0], CONV_TILE):
        rows = slice(start, start + CONV_TILE)
        for p in range(4):
            v = first_ref[rows, p * 512 : (p + 1) * 512] * scale + shift
            hidden_ref[rows, p * 512 : (p + 1) * 512] = (v * gelu_gate(v)).astype(BF16)
        mask = real_mask(count_ref[0], start, CONV_TILE)
        total, square = conv_tile(hidden_ref, k_ref, second_ref, start, CONV_TILE, mask, total, square)
    spread_rows(stat_ref, column_sums((total, square)))


def head_kernel(
    tasks, count_ref, second_ref, g2_ref, g1_ref, norm_ref, image_ref, label_ref, head_ref, pick_ref,
    out_ref, slope_ref, slope_sum_ref, slope_xhat_ref, pooled_ref, resid_ref, gram_out_ref,
):
    real_total = images_total(g1_ref)
    mean, inverse = moments(g2_ref, real_total * 4.0)
    gain, shift = norm_ref[2:3, :], norm_ref[3:4, :]
    lane_real = (lax.broadcasted_iota(jnp.int32, (1, LANES), 1) < tasks).astype(F32)
    gram = image_sum = None
    for start in range(0, second_ref.shape[0], TILE):
        rows = slice(start, start + TILE)
        pooled = slope_sum = slope_xhat = None
        for p in range(4):
            cols = slice(p * 512, (p + 1) * 512)
            xhat = (second_ref[rows, cols] - mean) * inverse
            image = image_ref[rows, cols].astype(F32)
            image_sum = plus(image_sum, fold8(image))
            pre = gain * xhat + shift + image
            gate = gelu_gate(pre)
            out = pre * gate
            out_ref[rows, cols] = out.astype(BF16)
            slope = gelu_slope(pre, gate)
            slope_ref[rows, cols] = slope
            pooled = plus(pooled, out)
            slope_sum = plus(slope_sum, slope)
            slope_xhat = plus(slope_xhat, slope * xhat)
        pooled = pooled * 0.25
        slope_sum_ref[rows, :] = slope_sum
        slope_xhat_ref[rows, :] = slope_xhat
        pooled_ref[rows, 0:512] = pooled
        pooled_ref[rows, 512:640] = (lax.broadcasted_iota(jnp.int32, (TILE, LANES), 1) == 0).astype(F32)
        logits = precise(pooled, head_ref[0:512, :], ((1,), (0,))) + head_ref[512:513, :]
        mask = real_mask(count_ref[0], start, TILE) * lane_real
        resid = mask * (jax.nn.sigmoid(logits) - label_ref[rows, :].astype(F32)) / real_total
        resid_ref[rows, :] = resid
        gram = plus(gram, precise(resid, resid, ((0,), (0,))))
    heads = head_ref[0:512, :]
    gram = gram * precise(heads, heads, ((0,), (0,)))
    basis = pick_ref[...]
    projected = precise(gram, basis, ((1,), (1,)))
    lane = lax.broadcasted_iota(jnp.int32, (32, LANES), 1)
    row = lax.broadcasted_iota(jnp.int32, (32, LANES), 0)
    packed = None
    for group in range(6):
        placed = precise(projected, ((lane == row + GROUP * group) & (row < GROUP)).astype(F32), ((1,), (0,)))
        packed = plus(packed, precise(basis[4 * group : 4 * group + 4, :], placed, ((1,), (0,))))
    spread_rows(gram_out_ref, [packed[r : r + 1, :] for r in range(4)] + column_sums((image_sum,)))


def frank_wolfe(packed, picks, start_mix, fw_steps):
    rows = jnp.concatenate([packed[:, GROUP * g : GROUP * (g + 1)] for g in range(6)], axis=0)
    column = [jnp.broadcast_to(rows[:, k : k + 1], (24, LANES)) for k in range(fw_steps + 1)]
    along = column[fw_steps]
    a = along[fw_steps : fw_steps + 1, :]
    mix = start_mix
    for k in range(fw_steps):
        b = along[k : k + 1, :]
        c = column[k][k : k + 1, :]
        size = jnp.clip((a - b) / (a - 2.0 * b + c), 0.0, STEP_CAP)
        keep = 1.0 - size
        a = keep * keep * a + 2.0 * (keep * size) * b + size * size * c
        along = keep * along + size * column[k]
        mix = keep * mix + size * picks[k : k + 1, :]
    return mix


def mix_kernel(
    fw_steps, gram_ref, pick_ref, start_ref, resid_ref, pooled_ref, head_ref, slope_sum_ref, slope_xhat_ref,
    dout_ref, stat_ref, head_grad_ref, mix_ref,
):
    (total,) = gathered_rows(gram_ref, 1)
    packed = jnp.concatenate([total[:, r * LANES : (r + 1) * LANES] for r in range(4)], axis=0)
    mix = frank_wolfe(packed, pick_ref[...], start_ref[0:1, :], fw_steps)
    mix_ref[...] = jnp.broadcast_to(mix, mix_ref.shape)
    gain_sum = shift_sum = head_grad = None
    for start in range(0, resid_ref.shape[0], TILE):
        rows = slice(start, start + TILE)
        weighted = resid_ref[rows, :] * mix
        dout = precise(weighted, head_ref[0:512, :], ((1,), (1,))) * 0.25
        dout_ref[rows, :] = dout
        head_grad = plus(head_grad, precise(weighted, pooled_ref[rows, :], ((0,), (0,))))
        gain_sum = plus(gain_sum, fold8(dout * slope_xhat_ref[rows, :]))
        shift_sum = plus(shift_sum, fold8(dout * slope_sum_ref[rows, :]))
    spread_rows(stat_ref, column_sums((gain_sum, shift_sum)))
    ways, width = head_grad_ref.shape[0], head_grad.shape[1]
    cols = head_grad_ref.shape[2] // width
    for way in range(ways):
        rows = [head_grad[way * cols + i : way * cols + i + 1, :] for i in range(cols)]
        head_grad_ref[way] = jnp.concatenate(rows, axis=1)


def store_sums(sum_ref, sums):
    spread_rows(sum_ref, column_sums(sums))


def split_halves(core, grad, half_refs, rows, p):
    if len(half_refs) == 1:
        half_refs[0][rows, p * grad.shape[1] : (p + 1) * grad.shape[1]] = grad
    else:
        half = grad.shape[1] // 2
        low, high = grad[:, :half], grad[:, half:]
        own_ref, send_ref = half_refs
        own_ref[rows, p * half : (p + 1) * half] = jnp.where(core == 0, low, high)
        send_ref[rows, p * half : (p + 1) * half] = jnp.where(core == 0, high, low)


def back_second_kernel(
    count_ref, core_ref, slope_ref, dout_ref, second_ref, first_ref, g1_ref, g2_ref, g4_ref, norm_ref, k_ref,
    dnormed_ref, stat_ref, sum_ref, dpre_ref, *half_refs,
):
    spatial = images_total(g1_ref) * 4.0
    mean1, inverse1 = moments(g1_ref, spatial)
    mean2, inverse2 = moments(g2_ref, spatial)
    gain_grad, shift_grad = gathered_rows(g4_ref, 2)
    scale2 = norm_ref[2:3, :] * inverse2
    by_value = scale2 * gain_grad * inverse2 / spatial
    by_one = scale2 * shift_grad / spatial - by_value * mean2
    gain1, shift1 = norm_ref[0:1, :], norm_ref[1:2, :]
    gain_sum = shift_sum = None
    sums = [None] * 4
    *half_refs, dsecond_ref = half_refs
    for start in range(0, second_ref.shape[0], TILE):
        rows = slice(start, start + TILE)
        mask = real_mask(count_ref[0], start, TILE)
        dout = dout_ref[rows, :]
        for p in range(4):
            cols = slice(p * 512, (p + 1) * 512)
            dpre = dout * slope_ref[rows, cols]
            dpre_ref[rows, cols] = dpre.astype(BF16)
            grad = (scale2 * dpre - mask * (by_one + by_value * second_ref[rows, cols])).astype(BF16)
            dsecond_ref[:, cols] = grad
            split_halves(core_ref[0], grad, half_refs, rows, p)
            sums[p] = plus(sums[p], fold8(grad.astype(F32)))
        for q in range(4):
            cols = slice(q * 512, (q + 1) * 512)
            acc = None
            for p in range(4):
                base = tap(q, p) * 512
                acc = plus(acc, dot_nt(dsecond_ref[:, p * 512 : (p + 1) * 512], k_ref[base : base + 512, :]))
            xhat = (first_ref[rows, cols] - mean1) * inverse1
            v = gain1 * xhat + shift1
            dnormed = acc * gelu_slope(v, gelu_gate(v))
            dnormed_ref[rows, cols] = dnormed
            gain_sum = plus(gain_sum, fold8(dnormed * xhat))
            shift_sum = plus(shift_sum, fold8(dnormed))
    spread_rows(stat_ref, column_sums((gain_sum, shift_sum)))
    store_sums(sum_ref, sums)


def taps_of(index):
    return [(q, p) for q in range(4) for p in range(4) if tap(q, p) == index]


def weight_grad_kernel(x_ref, d_ref, out_ref):
    for index in range(9):
        acc = None
        for q, p in taps_of(index):
            acc = plus(acc, dot_tn(x_ref[:, q * 512 : (q + 1) * 512], d_ref[:, p * 512 : (p + 1) * 512]))
        out_ref[index * 512 : (index + 1) * 512, :] = acc


def as_column(row):
    return jnp.transpose(jnp.broadcast_to(row, (LANES, row.shape[1])))


def image_mean(slots, g3_ref):
    return gathered_rows(g3_ref, 2)[1] * (1.0 / slots)


def hidden_mean(norm_ref):
    nodes, weights = np.polynomial.hermite_e.hermegauss(9)
    total = None
    for node, weight in zip(nodes, weights / weights.sum()):
        v = norm_ref[0:1, :] * float(node) + norm_ref[1:2, :]
        total = plus(total, float(weight) * (v * gelu_gate(v)))
    return total


def pair_weight_grad_kernel(mean_of, table_ref, x_ref, d_ref, mean_ref, x_other_ref, d_other_ref, send_ref, keep_ref, whole_ref):
    width = whole_ref.shape[1]
    column = as_column(mean_of(mean_ref))
    column = jnp.concatenate([column] * (width // LANES), axis=1)
    sums = []
    for p in range(4):
        cols = slice(p * width, (p + 1) * width)
        sums.append(jnp.sum(fold8(d_ref[:, cols].astype(F32)) + fold8(d_other_ref[:, cols].astype(F32)), 0, keepdims=True))
    seen = set()
    for q in range(4):
        acc = dot_tn(x_ref[:, q * 512 : (q + 1) * 512], d_ref[...])
        acc = acc + dot_tn(x_other_ref[:, q * 512 : (q + 1) * 512], d_other_ref[...])
        for p in range(4):
            index = tap(q, p)
            rows = slice(index * 512, (index + 1) * 512)
            part = acc[:, p * width : (p + 1) * width] - column * sums[p]
            whole_ref[rows, :] = whole_ref[rows, :] + part if index in seen else part
            seen.add(index)
    count, rows = keep_ref.shape[0], keep_ref.shape[1]
    for i in range(count):
        there = pl.ds(pl.multiple_of(table_ref[i] * rows, 16), rows)
        here = pl.ds(pl.multiple_of(table_ref[count + i] * rows, 16), rows)
        send_ref[i] = whole_ref[there, :].astype(BF16)
        keep_ref[i] = whole_ref[here, :]


def dfirst_kernel(count_ref, core_ref, dnormed_ref, first_ref, g1_ref, g5_ref, norm_ref, dfirst_ref, stat_ref, *half_refs):
    spatial = images_total(g1_ref) * 4.0
    mean1, inverse1 = moments(g1_ref, spatial)
    gain_grad, shift_grad = gathered_rows(g5_ref, 2)
    scale = norm_ref[0:1, :] * inverse1
    by_value = scale * gain_grad * inverse1 / spatial
    by_one = scale * shift_grad / spatial - by_value * mean1
    sums = [None] * 4
    for start in range(0, first_ref.shape[0], TILE):
        rows = slice(start, start + TILE)
        mask = real_mask(count_ref[0], start, TILE)
        for p in range(4):
            cols = slice(p * 512, (p + 1) * 512)
            grad = (scale * dnormed_ref[rows, cols] - mask * (by_one + by_value * first_ref[rows, cols])).astype(BF16)
            dfirst_ref[rows, cols] = grad
            if half_refs:
                split_halves(core_ref[0], grad, half_refs, rows, p)
            sums[p] = plus(sums[p], fold8(grad.astype(F32)))
    store_sums(stat_ref, sums)


def image_grad_kernel(begin, end, dfirst_ref, k_ref, dpre_ref, *refs):
    out_ref, buffer_ref, sem = refs[-3:]
    copies = []
    for n, start in enumerate(range(begin, end, TILE)):
        rows = slice(start, start + TILE)
        slot = n % 2
        if n >= 2:
            copies[n - 2].wait()
        for q in range(4):
            cols = slice(q * 512, (q + 1) * 512)
            acc = dpre_ref[rows, cols].astype(F32)
            for p in range(4):
                base = tap(q, p) * 512
                acc = acc + dot_nt(dfirst_ref[rows, p * 512 : (p + 1) * 512], k_ref[base : base + 512, :])
            buffer_ref[slot, :, q // 2, q % 2, :] = acc
        copies.append(pltpu.make_async_copy(buffer_ref.at[slot], out_ref.at[pl.ds(start, TILE)], sem.at[slot]))
        copies[n].start()
    for copy in copies[-2:]:
        copy.wait()


def combine_kernel(table_ref, keep_ref, got_ref, send_ref, out_ref):
    count = out_ref.shape[0]
    for i in range(count):
        there, here = table_ref[i], table_ref[count + i]
        send_ref[i] = (keep_ref[there] + got_ref[there].astype(F32)).astype(BF16)
        out_ref[i] = keep_ref[here] + got_ref[here].astype(F32)


def line_kernel(z_ref, keep_ref, got_ref, *out_refs):
    for mask, ref in enumerate(out_refs):
        place = z_ref[0] ^ mask
        ref[...] = (keep_ref[place] + got_ref[place].astype(F32)).astype(ref.dtype)


def line_sum_kernel(core_ref, keep_ref, got1_ref, got2_ref, got3_ref, send_ref, out_ref):
    half = out_ref.shape[0]
    for ref, place in ((send_ref, 1 - core_ref[0]), (out_ref, core_ref[0])):
        rows = pl.ds(pl.multiple_of(place * half, 16), half)
        got = got1_ref[rows, :].astype(F32) + got2_ref[rows, :].astype(F32) + got3_ref[rows, :].astype(F32)
        ref[...] = keep_ref[rows, :] + got


def finish_kernel(
    slots, me_ref, keep1_ref, got1_ref, keep2_ref, got2_ref, g3_ref, norm_ref, last_ref, weight_ref, momentum_ref, average_ref,
    grad_ref, momentum_new_ref, weight_new_ref, average_new_ref, low_ref, column_ref, sums_ref,
):
    core, start = me_ref[0] % 2, me_ref[0] * grad_ref.shape[1]
    rows = grad_ref.shape[1]
    index = lax.broadcasted_iota(jnp.int32, (rows, 1), 0) + start % 512
    last = jnp.sum(last_ref[...], 0)
    begin = last.shape[1] - 8 * 512
    sums = [last[:, begin + p * 512 : begin + (p + 1) * 512] for p in range(8)]
    sources = (
        (keep1_ref, got1_ref, image_mean(slots, g3_ref), sums[4:]),
        (keep2_ref, got2_ref, hidden_mean(norm_ref), sums[:4]),
    )
    for k, (keep_ref, got_ref, mean, sums) in enumerate(sources):
        column = as_column(mean)
        column_ref[0:512, :] = column
        column_ref[512:1024, :] = column
        for tap_index in range(9):
            total = None
            for _, p in taps_of(tap_index):
                total = plus(total, sums[p])
            sums_ref[tap_index : tap_index + 1, :] = total
        column = column_ref[pl.ds(pl.multiple_of(start % 512, 16), rows), :]
        first_tap = start // 512
        total = jnp.where(index < 512, sums_ref[pl.ds(first_tap, 1), :], sums_ref[pl.ds(jnp.minimum(first_tap + 1, 8), 1), :])
        keep, got = keep_ref[...], got_ref[...]
        low_half, high_half = jnp.where(core == 0, keep, got), jnp.where(core == 0, got, keep)
        grad = jnp.concatenate([low_half, high_half], axis=1) + jnp.concatenate([column] * 4, axis=1) * total
        momentum, weight, average = nesterov(weight_ref[k], momentum_ref[k], grad, CONV_RATE, average_ref[k])
        grad_ref[k] = grad
        momentum_new_ref[k] = momentum
        weight_new_ref[k] = weight
        average_new_ref[k] = average
        low_ref[k] = weight.astype(BF16)


def relay_kernel(in_ref, out_ref):
    out_ref[...] = jnp.broadcast_to(jnp.sum(in_ref[...], 0)[None], out_ref.shape)


def small_kernel(
    last_ref, g4_ref, g5_ref, norm_ref, norm_momentum_ref, norm_average_ref, head_ref, head_momentum_ref, head_average_ref, *out_refs
):
    norm_grads = jnp.concatenate(gathered_rows(g5_ref, 2) + gathered_rows(g4_ref, 2), axis=0)
    rows, cols = head_ref.shape
    last = jnp.sum(last_ref[...], 0)
    head_grads = jnp.concatenate([last[:, i * 640 : (i + 1) * 640] for i in range(rows)], axis=0)[:, :cols]
    values = (norm_grads,) + nesterov(norm_ref[...], norm_momentum_ref[...], norm_grads, NORM_RATE, norm_average_ref[...])
    values += (head_grads,) + nesterov(head_ref[...], head_momentum_ref[...], head_grads, HEAD_RATE, head_average_ref[...])
    for ref, value in zip(out_refs, values):
        ref[...] = value


def swap(value, even_mask, odd_mask):
    count = lax.axis_size(AXES)
    pairs = [(i, i ^ (odd_mask if i % 2 else even_mask)) for i in range(count)]
    return lax.ppermute(value, AXES, pairs)


CORE, ALONG_X, ALONG_Y, ALONG_Z = 1, 2, 4, 8
SQUARE = [(ALONG_X, ALONG_Y), (ALONG_Y, ALONG_X)]


def flat_index():
    return lax.axis_index("dp") * lax.axis_size("task") + lax.axis_index("task")


def along_line(shard):
    return jnp.stack([shard] + [swap(shard, m * ALONG_Z, m * ALONG_Z) for m in (1, 2, 3)])


def square_near(line):
    blocks = [line[:, :, :256], line[:, :, 256:]]
    return [jnp.concatenate([blocks[h], swap(blocks[h], *SQUARE[h])], 0) for h in (0, 1)]


def square_far(near):
    return [swap(near[h], *SQUARE[1 - h]) for h in (0, 1)]


def gather_pieces(shard, images, early, later):
    line = along_line(shard)
    line, images, early = lax.optimization_barrier((line, images, early))
    near = square_near(line)
    near, later = lax.optimization_barrier((near, later))
    far = square_far(near)
    sibling_near = [swap(v, CORE, CORE) for v in near]
    sibling_far = [swap(v, CORE, CORE) for v in far]
    pieces = [v[h] for h in (0, 1) for v in (near, far, sibling_near, sibling_far)]
    return pieces, images, early, later


def piece_places(rows):
    me = flat_index()
    core = me % 2
    owners = []
    part = jnp.arange(8, dtype=jnp.int32)
    for h in (0, 1):
        for base, which, is_far in ((me, core, 0), (me, core, 1), (me ^ CORE, 1 - core, 0), (me ^ CORE, 1 - core, 1)):
            x_first = which == h
            near_mask = jnp.where(x_first, ALONG_X, ALONG_Y)
            far_mask = jnp.where(x_first, ALONG_Y, ALONG_X)
            owners.append(base ^ (part % 4 * ALONG_Z) ^ (part // 4 * near_mask) ^ (is_far * far_mask))
    return jnp.concatenate(owners) * rows


def nesterov(params, momentum, grads, rate, average):
    momentum_new = MOMENTUM_DECAY * momentum + grads
    params_new = params - rate * (grads + MOMENTUM_DECAY * momentum_new)
    average_new = AVERAGE_DECAY * average + (1.0 - AVERAGE_DECAY) * params_new
    return (momentum_new, params_new, average_new)


VMEM = pl.BlockSpec(memory_space=pltpu.VMEM)
SCALAR = pl.BlockSpec(memory_space=pltpu.SMEM)
ANYWHERE = pl.BlockSpec(memory_space=pl.ANY)


def call(body, ins, outs, scratch=(), scalars=(), loose=(), flops=0, aliases=None, limit=12):
    kinds = {"vmem": (pltpu.VMEM, VMEM), "hbm": (pltpu.HBM, ANYWHERE), "free": (jax.ShapeDtypeStruct, VMEM)}
    out_shape = [kinds[k][0](d, t) for d, t, k in outs]
    moved = sum(a.size * a.dtype.itemsize for a in list(ins) + list(loose))
    return pl.pallas_call(
        body,
        in_specs=[SCALAR] * len(scalars) + [VMEM] * len(ins) + [ANYWHERE] * len(loose),
        out_specs=[kinds[k][1] for _, _, k in outs],
        out_shape=out_shape,
        scratch_shapes=list(scratch),
        input_output_aliases=aliases or {},
        compiler_params=pltpu.CompilerParams(vmem_limit_bytes=limit << 20),
        cost_estimate=pl.CostEstimate(flops=flops, bytes_accessed=moved, transcendentals=0),
    )(*scalars, *[pltpu.with_memory_space_constraint(a, pltpu.VMEM) for a in ins], *loose)


def exchange(replicated):
    return lax.all_to_all(replicated, AXES, 0, 0)


def on_device(
    images, image_counts, labels, fw_picks, task_average, conv_weights, conv_momentum, conv_average,
    norm_parameter_list, norm_momentum, norm_average, head_params, head_momentum, head_average,
):
    rows, map_side, channels = images.shape[0], images.shape[1], images.shape[3]
    width = map_side * map_side * channels
    devices = lax.axis_size(AXES)
    tasks = labels.shape[1]
    task_cols = head_params.shape[1]
    fw_steps = fw_picks.shape[0]
    matmul = 2 * rows * width * width
    tuned = (lax.axis_size("dp"), lax.axis_size("task"), channels) == (8, 4, 512)

    def stat(count):
        return ((devices, 1, count), F32, "free")

    slots = float(devices * rows * map_side * map_side)
    flat, flat_low = ((rows, width), F32, "vmem"), ((rows, width), BF16, "vmem")
    low = conv_weights.astype(BF16)
    heads = lax.all_gather(head_params, "task", axis=1, tiled=True)
    heads = jnp.pad(heads, ((0, 7), (0, LANES - tasks)))
    labels = jnp.pad(labels, ((0, 0), (0, LANES - tasks)))
    flat_images = images.reshape(rows, width)
    start = jnp.pad(task_average[None, :], ((0, 7), (0, LANES - tasks)))
    basis = jnp.concatenate(
        [
            (jnp.arange(LANES, dtype=jnp.int32)[None, :] == fw_picks[:, None]).astype(F32),
            start[0:1],
            jnp.zeros((32 - fw_steps - 1, LANES), F32),
        ],
        axis=0,
    )

    me = flat_index()
    core = me & 1

    def bind(body, *static):
        return lambda *refs: body(*static, *refs)

    k2 = lax.all_gather(low[1], AXES, axis=0, tiled=True)
    if tuned:
        tall_low = (9 * channels, channels)
        chips = devices // 2
        at_x, at_y = me // ALONG_X & 1, me // ALONG_Y & 1
        index = jnp.arange(chips // 2, dtype=jnp.int32)
        by_x, by_y = index * 2, index // 2 * 4 + index % 2
        here = jnp.where(core == 0, by_x + at_x, by_y + 2 * at_y)
        there = jnp.where(core == 0, by_x + 1 - at_x, by_y + 2 * (1 - at_y))
        own = jnp.where(core == 0, at_y, at_x)
        index = jnp.arange(chips // 4, dtype=jnp.int32) * 2
        tables = (
            piece_places(low.shape[1]), jnp.concatenate([there, here]), jnp.concatenate([index + 1 - own, index + own]),
            (me // ALONG_Z)[None], core[None], me[None], image_counts + 0,
        )
        pieces, flat_images, (tables, start, basis), (heads, labels) = gather_pieces(
            low[0], flat_images, (tables, start, basis), (heads, labels)
        )
        places, chunk_table, pair_table, z_place, core_place, me_place, image_counts = tables
        first, stat1, k1 = call(
            first_gathered_kernel, [flat_images], [flat, stat(1152), (tall_low, BF16, "hbm")],
            [pltpu.VMEM(tall_low, BF16), pltpu.SemaphoreType.DMA, pltpu.SemaphoreType.DMA],
            (image_counts, places), pieces, matmul, limit=7,
        )
    else:
        k1 = lax.all_gather(low[0], AXES, axis=0, tiled=True)
        first, stat1 = call(first_kernel, [flat_images, k1], [flat, stat(1152)], (), (image_counts,), (), matmul)
    if tuned:
        images_other = swap(flat_images, CORE, CORE)
        stat1, images_other = lax.optimization_barrier((stat1, images_other))
    else:
        core_place = core[None]
    g1 = exchange(stat1)
    hidden, second, stat2 = call(
        second_kernel, [first, g1, norm_parameter_list, k2], [flat_low, flat, stat(1024)], (), (image_counts,), (), matmul, limit=8
    )
    g2 = exchange(stat2)
    per_channel = ((rows, channels), F32, "vmem")
    block_flat, slope, slope_sum, slope_xhat, pooled, resid, gram = call(
        bind(head_kernel, tasks), [second, g2, g1, norm_parameter_list, flat_images, labels, heads, basis],
        [flat_low, flat, per_channel, per_channel, ((rows, channels + LANES), F32, "vmem"), ((rows, LANES), F32, "vmem"), stat(1024)],
        (), (image_counts,), (), matmul, limit=3,
    )
    g3 = exchange(gram)
    dout, stat4, head_send, mix = call(
        bind(mix_kernel, fw_steps), [g3, basis, start, resid, pooled, heads, slope_sum, slope_xhat],
        [per_channel, stat(1024), ((tasks // task_cols, 1, task_cols * (channels + LANES)), F32, "free"), ((8, LANES), F32, "free")],
        (), (), (), matmul // 2, limit=3,
    )
    g4 = exchange(stat4)
    if tuned:
        g4, hidden = lax.optimization_barrier((g4, hidden))
        hidden_other = swap(hidden, CORE, CORE)
    part = channels // 2
    shard_rows = conv_weights.shape[1]
    sent = [((rows, width // 2), BF16, "vmem")] * 2 if tuned else [flat_low]
    ways = tasks // task_cols
    sums = ((ways, 1, 4 * channels), F32, "free")
    dnormed, stat5, sums_two, dpre, *dsecond_halves = call(
        back_second_kernel, [slope, dout, second, first, g1, g2, g4, norm_parameter_list, k2],
        [flat, stat(1024), sums, flat_low] + sent, [pltpu.VMEM((TILE, width), BF16)], (image_counts, core_place), (), matmul, {4: 0}, limit=8,
    )
    if tuned:
        stat5, hidden_other = lax.optimization_barrier((stat5, hidden_other))
    g5 = exchange(stat5)
    if tuned:
        g5, *dsecond_halves = lax.optimization_barrier((g5, *dsecond_halves))
        dsecond_other = swap(dsecond_halves[1], CORE, CORE)
    dfirst, sums_one, *dfirst_halves = call(
        dfirst_kernel, [dnormed, first, g1, g5, norm_parameter_list],
        [flat_low, sums] + (sent if tuned else []), (), (image_counts, core_place), (), matmul // 4, limit=6,
    )

    def combine(keep, got, table):
        dims = (keep.shape[0] // 2,) + keep.shape[1:]
        return call(combine_kernel, [keep, got], [(dims, BF16, "free"), (dims, F32, "vmem")], (), (table,), limit=5)

    def scatter_start(x, x_other, d, d_other, mean_of, source):
        dims = (devices // 4, 2 * shard_rows, part)
        return call(
            bind(pair_weight_grad_kernel, mean_of), [x, d, source, x_other, d_other],
            [(dims, BF16, "free"), (dims, F32, "vmem")], [pltpu.VMEM((9 * channels, part), F32)],
            (chunk_table,), (), matmul, limit=18,
        )

    def scatter_next(send, keep):
        return combine(keep, swap(send, *SQUARE[0]), pair_table)

    def scatter_line(got, keep):
        pair = keep.shape[1:]
        return call(line_kernel, [keep, got], [(pair, F32, "vmem")] + [(pair, BF16, "free")] * 3, (), (z_place,), limit=3)

    def scatter_finish(own, sent):
        half = ((shard_rows, part), F32, "free")
        return call(line_sum_kernel, [own] + sent, [half, half], (), (core_place,), limit=3)

    def scatter_whole(x, d):
        (whole,) = call(weight_grad_kernel, [x, d], [((9 * channels, channels), F32, "free")], (), (), (), matmul)
        return lax.psum_scatter(whole, AXES, scatter_dimension=0, tiled=True)

    def share_task(*values):
        return lax.all_to_all(jnp.concatenate(values, axis=2), "task", 0, 0)

    def share_dp(over_task):
        dims = (lax.axis_size("dp"),) + over_task.shape[1:]
        (over_dp,) = call(relay_kernel, [over_task], [(dims, F32, "free")], limit=4)
        return lax.all_to_all(over_dp, "dp", 0, 0)

    def image_gradient(begin, end, late, buffer=()):
        return call(
            bind(image_grad_kernel, begin, end), [late, k1, dpre], [(images.shape, F32, "hbm")],
            [pltpu.VMEM((2, TILE) + images.shape[1:], F32), pltpu.SemaphoreType.DMA((2,))], (), buffer, matmul * (end - begin) // rows,
            {3: 0} if buffer else None, limit=6,
        )[0]

    if tuned:
        dfirst_other = swap(dfirst_halves[1], CORE, CORE)
        dsecond_own, dsecond_other, hidden, hidden_other, dfirst = lax.optimization_barrier(
            (dsecond_halves[0], dsecond_other, hidden, hidden_other, dfirst)
        )
        two = scatter_start(hidden, hidden_other, dsecond_own, dsecond_other, hidden_mean, norm_parameter_list)
        send_two, flat_images, images_other, dfirst_own = lax.optimization_barrier((two[0], flat_images, images_other, dfirst_halves[0]))
        one = scatter_start(flat_images, images_other, dfirst_own, dfirst_other, bind(image_mean, slots), g3)
        send_one, keep_two = lax.optimization_barrier((one[0], two[1]))
        send_two, keep_two = scatter_next(send_two, keep_two)
        got_two = swap(send_two, *SQUARE[1])
        send_two, late = lax.optimization_barrier((send_two, dfirst))
        image_grad = image_gradient(0, rows, late)
        got_two, image_grad = lax.optimization_barrier((got_two, image_grad))
        line_two = scatter_line(got_two, keep_two)
        sent_two = [swap(line_two[m], m * ALONG_Z, m * ALONG_Z) for m in (1, 2, 3)]
        line_first, keep_one = lax.optimization_barrier((line_two[1], one[1]))
        send_one, keep_one = scatter_next(send_one, keep_one)
        got_one = swap(send_one, *SQUARE[1])
        send_one, block_flat, head_send, sums_two, sums_one = lax.optimization_barrier(
            (send_one, block_flat, head_send, sums_two, sums_one)
        )
        shared = share_task(head_send, sums_two, sums_one)
        block_output = block_flat.reshape(images.shape)
        got_one, block_output, sent_two, shared = lax.optimization_barrier((got_one, block_output, sent_two, shared))
        line_one = scatter_line(got_one, keep_one)
        sent_one = [swap(line_one[m], m * ALONG_Z, m * ALONG_Z) for m in (1, 2, 3)]
        line_first, shared = lax.optimization_barrier((line_one[1], shared))
        last = share_dp(shared)
        ends = (scatter_finish(line_one[0], sent_one), scatter_finish(line_two[0], sent_two))
        shards = conv_weights.shape
        outs = [(shards, F32, "free")] * 4 + [(shards, BF16, "free")]
        conv_grads, conv_momentum_new, conv_weights_new, conv_average_new, conv_weights_low = call(
            bind(finish_kernel, slots),
            [v for send, keep in ends for v in (keep, swap(send, CORE, CORE))]
            + [g3, norm_parameter_list, last, conv_weights, conv_momentum, conv_average],
            outs, [pltpu.VMEM((1024, LANES), F32), pltpu.VMEM((16, channels), F32)], (me_place,), limit=5,
        )
    else:
        last = share_dp(share_task(head_send, sums_two, sums_one))
        grad_two = scatter_whole(hidden, dsecond_halves[0])
        grad_one = scatter_whole(flat_images, dfirst)
        image_grad = image_gradient(0, rows, dfirst)
        block_output = block_flat.reshape(images.shape)
        conv_grads = jnp.stack([grad_one, grad_two])
        conv_momentum_new, conv_weights_new, conv_average_new = nesterov(conv_weights, conv_momentum, conv_grads, CONV_RATE, conv_average)
        conv_weights_low = conv_weights_new.astype(BF16)
    head_dims = (head_params.shape[1], head_params.shape[0])
    norm_grads, norm_momentum_new, norm_params_new, norm_average_new, *head_new = call(
        small_kernel,
        [last, g4, g5, norm_parameter_list, norm_momentum, norm_average, head_params.T, head_momentum.T, head_average.T],
        [(norm_momentum.shape, F32, "free")] * 4 + [(head_dims, F32, "free")] * 4, limit=4,
    )
    head_grads, head_momentum_new, head_params_new, head_average_new = [value.T for value in head_new]
    task_average_new = AVERAGE_DECAY * task_average + (1.0 - AVERAGE_DECAY) * mix[0, :tasks]
    return (
        block_output,
        image_grad,
        conv_grads,
        conv_momentum_new,
        conv_weights_new,
        conv_average_new,
        conv_weights_low,
        norm_grads,
        norm_momentum_new,
        norm_params_new,
        norm_average_new,
        head_grads,
        head_momentum_new,
        head_params_new,
        head_average_new,
        task_average_new,
    )


def solution(mesh):
    both = P(AXES)
    rowwise = P(None, AXES, None)
    head = P(None, "task")
    return jax.shard_map(
        on_device,
        mesh=mesh,
        in_specs=(both, both, both, P(), P(), rowwise, rowwise, rowwise, P(), P(), P(), head, head, head),
        out_specs=(both, both, rowwise, rowwise, rowwise, rowwise, rowwise, P(), P(), P(), P(), head, head, head, head, P()),
        check_vma=False,
    )
```
